32 devices in a mesh: gx: 8 (over z, x), gy: 4 (over y, core).
Axes of the slice: x: 2, y: 2, z: 4, core: 2. Of those that a mesh axis runs over, the one named last changes fastest.
Arguments:
- patches: bfloat16 [13824, 768], P(('gx', 'gy')), may hold values from -6 to 6
- clip_of_row: int32 [13824], P('gx'), may hold values from 0 to 15, as said below
- position_of_row: int32 [13824], P(('gx', 'gy')), may hold values from 0 to 1213, as said below
- pos_embed: bfloat16 [1214, 768], P(None, ('gx', 'gy')), may hold values from -3 to 3
- norm1_gain: bfloat16 [2, 768], P(None, ('gx', 'gy')), may hold values from 0.5 to 1.5
- norm1_bias: bfloat16 [2, 768], P(None, ('gx', 'gy')), may hold values from -1.5 to 1.5
- query_bias: bfloat16 [2, 768], P(None, ('gx', 'gy')), may hold values from -1.5 to 1.5
- value_bias: bfloat16 [2, 768], P(None, ('gx', 'gy')), may hold values from -1.5 to 1.5
- out_bias: bfloat16 [2, 768], P(None, ('gx', 'gy')), may hold values from -1.5 to 1.5
- norm2_gain: bfloat16 [2, 768], P(None, ('gx', 'gy')), may hold values from 0.5 to 1.5
- norm2_bias: bfloat16 [2, 768], P(None, ('gx', 'gy')), may hold values from -1.5 to 1.5
- up_bias: bfloat16 [2, 3072], P(None, ('gx', 'gy')), may hold values from -1.5 to 1.5
- down_bias: bfloat16 [2, 768], P(None, ('gx', 'gy')), may hold values from -1.5 to 1.5
- qkv_weight: bfloat16 [2, 768, 2304], P(None, ('gx', 'gy')), may hold values from -0.21875 to 0.21875
- out_weight: bfloat16 [2, 768, 768], P(None, ('gx', 'gy')), may hold values from -4 to 4
- up_weight: bfloat16 [2, 768, 3072], P(None, 'gx', 'gy'), may hold values from -0.21875 to 0.21875
- down_weight: bfloat16 [2, 3072, 768], P(None, 'gy', 'gx'), may hold values from -0.109375 to 0.109375
- cotangent: bfloat16 [13824, 768], P(('gx', 'gy')), may hold values from -6 to 6
Outputs:
- activations: float32 [13824, 768], P(('gx', 'gy'))
- input_grad: float32 [13824, 768], P(('gx', 'gy'))
- pos_embed_grad: float32 [1214, 768], P(None, ('gx', 'gy'))
- norm1_gain_grad: float32 [2, 768], P(None, ('gx', 'gy'))
- norm1_bias_grad: float32 [2, 768], P(None, ('gx', 'gy'))
- query_bias_grad: float32 [2, 768], P(None, ('gx', 'gy'))
- value_bias_grad: float32 [2, 768], P(None, ('gx', 'gy'))
- out_bias_grad: float32 [2, 768], P(None, ('gx', 'gy'))
- norm2_gain_grad: float32 [2, 768], P(None, ('gx', 'gy'))
- norm2_bias_grad: float32 [2, 768], P(None, ('gx', 'gy'))
- up_bias_grad: float32 [2, 3072], P(None, ('gx', 'gy'))
- down_bias_grad: float32 [2, 768], P(None, ('gx', 'gy'))
- qkv_weight_grad: float32 [2, 768, 2304], P(None, ('gx', 'gy'))
- out_weight_grad: float32 [2, 768, 768], P(None, ('gx', 'gy'))
- up_weight_grad: float32 [2, 768, 3072], P(None, 'gx', 'gy')
- down_weight_grad: float32 [2, 3072, 768], P(None, 'gy', 'gx')
The draws below stay inside these ranges and needn't reach their ends.
Inputs may be any that keep to these rules, and one draw needn't show every extreme that they name: `clip_of_row`: rows of one clip lie within one aligned block of 1728 rows; each block holds 1 clips of 1214 rows and 1 clips of 514 rows, and each clip number names one clip. Each of the block's 432-row pieces holds the length of every clip of the block divided by 4, rounded down or up, of its rows. `position_of_row`: A clip of 1214 rows uses each position 0 to 1213 once. A clip of 514 rows uses 0 and 1 for its two class tokens and, by a one-dimensional nearest-index map over the flattened table (not a two-dimensional interpolation of the frequency and time grid), 2 + ((k - 2) * 1212) // 512 for its other tokens k = 2 to 513.
All inputs are finite; a program needn't handle non-finite values.
Results may differ from the reference program's by a relative error of at most 0.014.
Values may be sent and summed in bfloat16 or wider, within the bound.
A program may use at most 192 MiB of HBM per device.

```python
from functools import partial
import jax
import jax.numpy as jnp
from jax import lax

D = 768
HEADS = 12
HEAD_DIM = 64
FF = 3072
LAYERS = 2
LONG = 1214
SHORT = 514
PAIRS = 1
POS = 1214
GROUP_ROWS = 1728
TOK_DEV = 432
TOKENS = 13824


def clip_layout(key):
    group_count = TOKENS // GROUP_ROWS
    members = GROUP_ROWS // TOK_DEV
    clip_count = 2 * PAIRS
    row_index = jnp.arange(GROUP_ROWS, dtype=jnp.int32)
    token_index = row_index % TOK_DEV * members + row_index // TOK_DEV

    def one_group(group_key, group_number):
        clip_order = jax.random.permutation(group_key, clip_count).astype(jnp.int32)
        lengths = jnp.where(clip_order < PAIRS, LONG, SHORT).astype(jnp.int32)
        starts = jnp.cumsum(lengths) - lengths
        slot_index = jnp.sum((token_index[:, None] >= starts[None, :]).astype(jnp.int32), axis=1) - 1
        within = token_index - starts[slot_index]
        chosen = clip_order[slot_index]
        spread = 2 + (within - 2) * (LONG - 2) // (SHORT - 2)
        position = jnp.where(chosen < PAIRS, within, jnp.where(within < 2, within, spread))
        return (group_number * clip_count + chosen, position)
    group_keys = jax.random.split(key, group_count)
    clip_rows, position_rows = jax.vmap(one_group)(group_keys, jnp.arange(group_count, dtype=jnp.int32))
    return (clip_rows.reshape(TOKENS).astype(jnp.int32), position_rows.reshape(TOKENS).astype(jnp.int32))


def draw_clip_of_row(key, part):
    return clip_layout(key)[0]


def draw_position_of_row(key, part):
    return clip_layout(key)[1]


def spiked(drawn, rng, source, target, shards_of, factor):
    owner, partner = [(jnp.arange(drawn.shape[dim]) // (drawn.shape[dim] // shards_of)).reshape([-1 if axis == dim else 1 for axis in range(drawn.ndim)]) for dim in (source, target)]
    chosen = jax.random.permutation(rng, shards_of)[partner]
    strong = (owner == chosen) | (owner == (partner + shards_of // 2) % shards_of)
    return jnp.where(strong, factor * drawn, drawn)


def level_of(rng, shape, pieces, least, high):
    level = 1.0
    for dim, shards_of in pieces:
        draws = jax.random.uniform(jax.random.fold_in(jax.random.fold_in(rng, 6), dim), (shards_of,), jnp.float32, least / len(pieces), high / len(pieces))
        level = level * jnp.repeat(jnp.exp(draws), shape[dim] // shards_of).reshape((-1,) + (1,) * (len(shape) - 1 - dim))
    return level


def normal_values(own_key, extent, scale, reach, cuts=(), held_as=jnp.bfloat16):
    drawn = jax.random.normal(own_key, extent, jnp.float32) * scale
    if len(cuts) > 0:
        drawn = level_of(own_key, extent, cuts, -0.22, 0.18) * drawn
    return jnp.clip(drawn, min=-reach, max=reach).astype(held_as)


def heavy_noise(own_key, dims, width, bound, cuts, heavy, held_as=jnp.bfloat16):
    entries = width * jax.random.normal(own_key, dims, jnp.float32)
    if cuts:
        entries = entries * level_of(own_key, dims, cuts, -0.22, 0.18)
    return jnp.clip(spiked(entries, jax.random.fold_in(own_key, 3), *heavy), -bound, bound).astype(held_as)


def setup_inputs(seed: int = 0) -> dict:
    key_list = jax.random.split(jax.random.key(seed), 19)
    return {
        "patches": normal_values(key_list[0], (TOKENS, D), 1.0, 6.0, ((0, 32),)),
        "clip_of_row": draw_clip_of_row(jax.random.fold_in(key_list[18], 71), 0),
        "position_of_row": draw_position_of_row(jax.random.fold_in(key_list[18], 71), 0),
        "pos_embed": normal_values(key_list[3], (POS, D), 0.5, 3.0, ((1, 32),)),
        "norm1_gain": jnp.clip(1.0 + 0.1 * jax.random.normal(key_list[4], (LAYERS, D), jnp.float32), 0.5, 1.5).astype(jnp.bfloat16),
        "norm1_bias": normal_values(key_list[5], (LAYERS, D), 0.3, 1.5, ((1, 32),)),
        "query_bias": normal_values(key_list[6], (LAYERS, D), 0.3, 1.5, ((1, 32),)),
        "value_bias": normal_values(key_list[7], (LAYERS, D), 0.3, 1.5, ((1, 32),)),
        "out_bias": normal_values(key_list[8], (LAYERS, D), 0.3, 1.5, ((1, 32),)),
        "norm2_gain": jnp.clip(1.0 + 0.1 * jax.random.normal(key_list[9], (LAYERS, D), jnp.float32), 0.5, 1.5).astype(jnp.bfloat16),
        "norm2_bias": normal_values(key_list[10], (LAYERS, D), 0.3, 1.5, ((1, 32),)),
        "up_bias": normal_values(key_list[11], (LAYERS, FF), 0.3, 1.5, ((1, 32),)),
        "down_bias": normal_values(key_list[12], (LAYERS, D), 0.3, 1.5, ((1, 32),)),
        "qkv_weight": normal_values(key_list[13], (LAYERS, D, 3 * D), D ** -0.5, 0.21875, ((1, 32),)),
        "out_weight": normal_values(key_list[14], (LAYERS, D, D), (max(1, 6 * D * PAIRS // GROUP_ROWS)) ** -0.5, 4.0, ((1, 32),)),
        "up_weight": normal_values(key_list[15], (LAYERS, D, FF), D ** -0.5, 0.21875, ((1, 8), (2, 4))),
        "down_weight": normal_values(key_list[16], (LAYERS, FF, D), FF ** -0.5, 0.109375, ((1, 4), (2, 8))),
        "cotangent": heavy_noise(key_list[17], (TOKENS, D), 1.0, 6.0, ((0, 32),), (0, 1, 32, 2.75)),
    }


EPSILON = 1e-06
HIGHEST = lax.Precision.HIGHEST

@jax.custom_vjp
def low(v):
    return lax.optimization_barrier(v.astype(jnp.bfloat16)).astype(jnp.float32)

@jax.custom_vjp
def low_back(v):
    return v

def low_keep(v):
    return (low(v), None)

def low_pass(kept, grad):
    return (grad,)

def back_keep(v):
    return (v, None)

def back_low(kept, grad):
    return (low(grad),)
low.defvjp(low_keep, low_pass)
low_back.defvjp(back_keep, back_low)

def layer_norm(values, norm_gain, norm_shift):
    row_mean = lax.optimization_barrier(jnp.mean(values, axis=-1, keepdims=True))
    centred = values - row_mean
    row_var = lax.optimization_barrier(jnp.mean(centred * centred, axis=-1, keepdims=True))
    return centred * lax.rsqrt(row_var + EPSILON) * norm_gain + norm_shift

def dense(left, right):
    return jnp.dot(left, right, precision=HIGHEST, preferred_element_type=jnp.float32)

def by_head(matrix):
    return jnp.transpose(matrix.reshape(matrix.shape[0], HEADS, HEAD_DIM), (1, 0, 2))

def group_attention(parts):
    queries, key_rows, value_rows, clip_ids = parts
    same_clip = clip_ids[:, None] == clip_ids[None, :]

    def one_head(head_parts):
        head_query, head_keys, head_values = head_parts
        scores = low_back(HEAD_DIM ** (-0.5) * dense(head_query, head_keys.T))
        scores = jnp.where(same_clip, scores, -1e+30)
        row_max = lax.optimization_barrier(jnp.max(scores, axis=-1, keepdims=True))
        shifted = jnp.exp(scores - row_max)
        probabilities = low(shifted / lax.optimization_barrier(jnp.sum(shifted, axis=-1, keepdims=True)))
        return dense(probabilities, head_values)
    mixed = lax.map(jax.checkpoint(one_head), (by_head(queries), by_head(key_rows), by_head(value_rows)))
    return jnp.transpose(mixed, (1, 0, 2)).reshape(queries.shape[0], HEADS * HEAD_DIM)

def attention(queries, key_rows, value_rows, clip_of_row):
    group_count = queries.shape[0] // GROUP_ROWS

    def grouped(matrix):
        return matrix.reshape(group_count, GROUP_ROWS, matrix.shape[1])
    mixed = lax.map(jax.checkpoint(group_attention), (grouped(queries), grouped(key_rows), grouped(value_rows), clip_of_row.reshape(group_count, GROUP_ROWS)))
    return mixed.reshape(queries.shape[0], queries.shape[1])

def forward(position_of_row, clip_of_row, floats):
    patches, pos_embed, norm1_gain, norm1_bias, query_bias, value_bias, out_bias, norm2_gain, norm2_bias, up_bias, down_bias, qkv_weight, out_weight, up_weight, down_weight = floats

    def one_layer(state, weights):
        gain_one, shift_one, bias_query, bias_value, bias_out, gain_two, shift_two, bias_up, bias_down, weight_qkv, weight_out, weight_up, weight_down = weights
        features = state.shape[1]
        act_one = low(layer_norm(state, gain_one, shift_one))
        projected = dense(act_one, weight_qkv)
        queries = low(low_back(projected[:, :features] + bias_query))
        key_rows = low(low_back(projected[:, features:2 * features]))
        value_rows = low(low_back(projected[:, 2 * features:] + bias_value))
        mixed = low(low_back(attention(queries, key_rows, value_rows, clip_of_row)))
        middle = state + low_back(dense(mixed, weight_out) + bias_out)
        act_two = low(layer_norm(middle, gain_two, shift_two))
        pre_act = low_back(dense(act_two, weight_up) + bias_up)
        hidden = low(jax.nn.gelu(pre_act, approximate=False))
        return middle + low_back(dense(hidden, weight_down) + bias_down)
    state = patches + pos_embed[position_of_row]
    for layer_index in range(LAYERS):
        weights = tuple((matrix[layer_index] for matrix in (norm1_gain, norm1_bias, query_bias, value_bias, out_bias, norm2_gain, norm2_bias, up_bias, down_bias, qkv_weight, out_weight, up_weight, down_weight)))
        state = jax.checkpoint(one_layer)(state, weights)
    return state

def reference(patches, clip_of_row, position_of_row, pos_embed, norm1_gain, norm1_bias, query_bias, value_bias, out_bias, norm2_gain, norm2_bias, up_bias, down_bias, qkv_weight, out_weight, up_weight, down_weight, cotangent):
    floats = tuple((matrix.astype(jnp.float32) for matrix in (patches, pos_embed, norm1_gain, norm1_bias, query_bias, value_bias, out_bias, norm2_gain, norm2_bias, up_bias, down_bias, qkv_weight, out_weight, up_weight, down_weight)))
    activations, pull_back = jax.vjp(partial(forward, position_of_row, clip_of_row), floats)
    grads = pull_back(cotangent.astype(jnp.float32))[0]
    return (activations, grads[0], grads[1], grads[2], grads[3], grads[4], grads[5], grads[6], grads[7], grads[8], grads[9], grads[10], grads[11], grads[12], grads[13], grads[14])
```

```python
import functools
import math

import jax
import jax.numpy as jnp
from jax import lax
from jax.experimental import pallas as pl
from jax.experimental.pallas import tpu as pltpu
from jax.sharding import PartitionSpec as P

HEAD_DIM = 64


EPSILON = 1e-06
SQRT_HALF = 1.0 / math.sqrt(2.0)
NORMAL_PEAK = 1.0 / math.sqrt(2.0 * math.pi)
MASKED = -1e30


def layer_norm(values, norm_gain, norm_shift):
    row_mean = jnp.mean(values, axis=-1, keepdims=True)
    centred = values - row_mean
    row_var = jnp.mean(centred * centred, axis=-1, keepdims=True)
    return centred * lax.rsqrt(row_var + EPSILON) * norm_gain + norm_shift


def gelu_slope(pre_act):
    return (
        0.5 * (1.0 + lax.erf(pre_act * SQRT_HALF))
        + pre_act * jnp.exp(-0.5 * pre_act * pre_act) * NORMAL_PEAK
    )


def column_pair(matrix, pair_index, pair_width):
    block = lax.dynamic_slice_in_dim(matrix, pair_index * pair_width, pair_width, 1)
    return block.reshape(matrix.shape[0], 2, pair_width // 2)


def join_pairs(stacked):
    return jnp.transpose(stacked, (1, 0, 2)).reshape(
        stacked.shape[1], stacked.shape[0] * stacked.shape[2]
    )


def pair_scores(head_query, head_keys, same_clip):
    scores = jnp.einsum(
        "qhd,khd->hqk", head_query, head_keys, preferred_element_type=jnp.float32
    ) * HEAD_DIM ** (-0.5)
    return jnp.where(same_clip[None], scores, MASKED)


def pair_parts(head_query, head_keys, head_values, head_grad, same_clip, pair_total):
    scores = pair_scores(head_query, head_keys, same_clip)
    weights = jnp.exp(scores - pair_total)
    weight_grad = jnp.einsum(
        "qhd,khd->hqk", head_grad, head_values, preferred_element_type=jnp.float32
    )
    return (weights, weight_grad)


def attend(queries, key_rows, value_rows, same_clip):
    pair_width = 2 * HEAD_DIM
    pair_count = queries.shape[1] // pair_width

    def one_pair(pair_index):
        head_query = column_pair(queries, pair_index, pair_width)
        head_keys = column_pair(key_rows, pair_index, pair_width)
        head_values = column_pair(value_rows, pair_index, pair_width)
        scores = pair_scores(head_query, head_keys, same_clip)
        row_max = jnp.max(scores, axis=-1, keepdims=True)
        log_total = row_max + jnp.log(jnp.sum(jnp.exp(scores - row_max), axis=-1, keepdims=True))
        weights = jnp.exp(scores - log_total).astype(jnp.bfloat16)
        mixed = jnp.einsum("hqk,khd->qhd", weights, head_values, preferred_element_type=jnp.float32)
        return (mixed.reshape(queries.shape[0], pair_width), log_total)

    mixed, log_total = lax.map(one_pair, jnp.arange(pair_count))
    return (join_pairs(mixed), log_total)


def attend_back(queries, key_rows, value_rows, same_clip, log_total, mixed_grad):
    pair_width = 2 * HEAD_DIM
    pair_count = queries.shape[1] // pair_width
    score_scale = HEAD_DIM ** (-0.5)

    def one_pair(pair_inputs):
        pair_index, pair_total = pair_inputs
        head_query = column_pair(queries, pair_index, pair_width)
        head_keys = column_pair(key_rows, pair_index, pair_width)
        head_values = column_pair(value_rows, pair_index, pair_width)
        head_grad = column_pair(mixed_grad, pair_index, pair_width)
        weights, weight_grad = pair_parts(
            head_query, head_keys, head_values, head_grad, same_clip, pair_total
        )
        value_grad = jnp.einsum(
            "hqk,qhd->khd",
            weights.astype(jnp.bfloat16),
            head_grad,
            preferred_element_type=jnp.float32,
        )
        inner = jnp.sum(weights * weight_grad, axis=-1, keepdims=True)
        score_grad = (weights * (weight_grad - inner)).astype(jnp.bfloat16)
        query_grad = (
            jnp.einsum("hqk,khd->qhd", score_grad, head_keys, preferred_element_type=jnp.float32)
            * score_scale
        )
        key_grad = (
            jnp.einsum("hqk,qhd->khd", score_grad, head_query, preferred_element_type=jnp.float32)
            * score_scale
        )
        return (
            query_grad.reshape(queries.shape[0], pair_width),
            key_grad.reshape(key_rows.shape[0], pair_width),
            value_grad.reshape(key_rows.shape[0], pair_width),
        )

    query_grad, key_grad, value_grad = lax.map(one_pair, (jnp.arange(pair_count), log_total))
    return (join_pairs(query_grad), join_pairs(key_grad), join_pairs(value_grad))


def stacked_member(collected, member_index):
    return jnp.stack([entry[member_index] for entry in collected])


def shards(
    patches,
    clip_of_row,
    position_of_row,
    pos_embed,
    norm1_gain,
    norm1_bias,
    query_bias,
    value_bias,
    out_bias,
    norm2_gain,
    norm2_bias,
    up_bias,
    down_bias,
    qkv_weight,
    out_weight,
    up_weight,
    down_weight,
    cotangent,
):
    (
        position_table,
        gain_one,
        shift_one,
        bias_query,
        bias_value,
        bias_out,
        gain_two,
        shift_two,
        bias_up,
        bias_down,
        weight_qkv,
        weight_out,
    ) = (
        lax.all_gather(pos_embed, ("gx", "gy"), axis=1, tiled=True),
        lax.all_gather(norm1_gain, ("gx", "gy"), axis=1, tiled=True),
        lax.all_gather(norm1_bias, ("gx", "gy"), axis=1, tiled=True),
        lax.all_gather(query_bias, ("gx", "gy"), axis=1, tiled=True),
        lax.all_gather(value_bias, ("gx", "gy"), axis=1, tiled=True),
        lax.all_gather(out_bias, ("gx", "gy"), axis=1, tiled=True),
        lax.all_gather(norm2_gain, ("gx", "gy"), axis=1, tiled=True),
        lax.all_gather(norm2_bias, ("gx", "gy"), axis=1, tiled=True),
        lax.all_gather(up_bias, ("gx", "gy"), axis=1, tiled=True),
        lax.all_gather(down_bias, ("gx", "gy"), axis=1, tiled=True),
        lax.all_gather(qkv_weight, ("gx", "gy"), axis=1, tiled=True),
        lax.all_gather(out_weight, ("gx", "gy"), axis=1, tiled=True),
    )
    block_up, block_down = (
        lax.all_gather(up_weight, "gx", axis=1, tiled=True),
        lax.all_gather(down_weight, "gx", axis=2, tiled=True),
    )
    layer_count = qkv_weight.shape[0]
    features = patches.shape[1]
    row_count = patches.shape[0]
    hidden_width = block_up.shape[2]
    member = lax.axis_index("gy")
    hidden_start = member * hidden_width
    own_clip = lax.dynamic_slice_in_dim(clip_of_row, member * row_count, row_count)
    same_clip = own_clip[:, None] == clip_of_row[None, :]
    state = patches.astype(jnp.float32) + position_table[position_of_row].astype(jnp.float32)
    stored = []
    for layer_index in range(layer_count):
        norm_gain_one = gain_one[layer_index].astype(jnp.float32)
        norm_shift_one = shift_one[layer_index].astype(jnp.float32)
        act_one = layer_norm(state, norm_gain_one, norm_shift_one).astype(jnp.bfloat16)
        projected = jnp.dot(act_one, weight_qkv[layer_index], preferred_element_type=jnp.float32)
        queries = (projected[:, :features] + bias_query[layer_index].astype(jnp.float32)).astype(
            jnp.bfloat16
        )
        key_rows = projected[:, features : 2 * features].astype(jnp.bfloat16)
        value_rows = (
            projected[:, 2 * features :] + bias_value[layer_index].astype(jnp.float32)
        ).astype(jnp.bfloat16)
        all_keys, all_values = (
            lax.all_gather(key_rows, "gy", axis=0, tiled=True),
            lax.all_gather(value_rows, "gy", axis=0, tiled=True),
        )
        mixed, log_total = attend(queries, all_keys, all_values, same_clip)
        attended = mixed.astype(jnp.bfloat16)
        middle = (
            state
            + jnp.dot(attended, weight_out[layer_index], preferred_element_type=jnp.float32)
            + bias_out[layer_index].astype(jnp.float32)
        )
        norm_gain_two = gain_two[layer_index].astype(jnp.float32)
        norm_shift_two = shift_two[layer_index].astype(jnp.float32)
        act_two = layer_norm(middle, norm_gain_two, norm_shift_two).astype(jnp.bfloat16)
        up_columns = lax.dynamic_slice_in_dim(
            bias_up[layer_index], hidden_start, hidden_width
        ).astype(jnp.float32)
        mlp_rows = lax.all_gather(act_two, "gy", axis=0, tiled=True)
        pre_act = (
            jnp.dot(mlp_rows, block_up[layer_index], preferred_element_type=jnp.float32)
            + up_columns
        )
        hidden = jax.nn.gelu(pre_act, approximate=False).astype(jnp.bfloat16)
        partial_out = jnp.dot(hidden, block_down[layer_index], preferred_element_type=jnp.float32)
        mlp_out = lax.psum_scatter(
            partial_out.astype(jnp.bfloat16), "gy", scatter_dimension=0, tiled=True
        ).astype(jnp.float32)
        stored.append(
            (
                state,
                act_one,
                queries,
                key_rows,
                value_rows,
                all_keys,
                all_values,
                log_total,
                attended,
                middle,
                mlp_rows,
                pre_act,
                hidden,
            )
        )
        state = middle + mlp_out + bias_down[layer_index].astype(jnp.float32)
    gradient = cotangent.astype(jnp.float32)
    collected = [None] * layer_count
    for layer_index in reversed(range(layer_count)):
        (
            layer_input,
            act_one,
            queries,
            key_rows,
            value_rows,
            kept_keys,
            kept_values,
            log_total,
            attended,
            middle,
            mlp_rows,
            pre_act,
            hidden,
        ) = stored[layer_index]
        grad_two = gradient.astype(jnp.bfloat16)
        down_bias_part = jnp.sum(grad_two.astype(jnp.float32), axis=0)
        grad_rows = lax.all_gather(grad_two, "gy", axis=0, tiled=True)
        down_part = jnp.einsum("rf,rd->fd", hidden, grad_rows, preferred_element_type=jnp.float32)
        hidden_grad = jnp.einsum(
            "rd,fd->rf", grad_rows, block_down[layer_index], preferred_element_type=jnp.float32
        )
        pre_grad = (hidden_grad * gelu_slope(pre_act)).astype(jnp.bfloat16)
        up_part = jnp.einsum("rd,rf->df", mlp_rows, pre_grad, preferred_element_type=jnp.float32)
        up_columns_grad = jnp.sum(pre_grad.astype(jnp.float32), axis=0)
        up_bias_part = lax.dynamic_update_slice_in_dim(
            jnp.zeros((bias_up.shape[1],), jnp.float32), up_columns_grad, hidden_start, 0
        )
        rows_grad = jnp.einsum(
            "rf,df->rd", pre_grad, block_up[layer_index], preferred_element_type=jnp.float32
        )
        act_two_grad = lax.psum_scatter(
            rows_grad.astype(jnp.bfloat16), "gy", scatter_dimension=0, tiled=True
        ).astype(jnp.float32)
        norm_gain_two = gain_two[layer_index].astype(jnp.float32)
        norm_shift_two = shift_two[layer_index].astype(jnp.float32)
        unused_two, norm_two_pull = jax.vjp(layer_norm, middle, norm_gain_two, norm_shift_two)
        middle_part, gain_two_part, shift_two_part = norm_two_pull(act_two_grad)
        mid_grad = gradient + middle_part
        grad_one = mid_grad.astype(jnp.bfloat16)
        out_bias_part = jnp.sum(grad_one.astype(jnp.float32), axis=0)
        out_part = jnp.einsum("rd,re->de", attended, grad_one, preferred_element_type=jnp.float32)
        mixed_grad = jnp.einsum(
            "re,de->rd", grad_one, weight_out[layer_index], preferred_element_type=jnp.float32
        ).astype(jnp.bfloat16)
        query_grad, key_grad, value_grad = attend_back(
            queries, kept_keys, kept_values, same_clip, log_total, mixed_grad
        )
        key_grad, value_grad = (
            lax.psum_scatter(
                key_grad.astype(jnp.bfloat16), "gy", scatter_dimension=0, tiled=True
            ).astype(jnp.float32),
            lax.psum_scatter(
                value_grad.astype(jnp.bfloat16), "gy", scatter_dimension=0, tiled=True
            ).astype(jnp.float32),
        )
        qkv_grad = jnp.concatenate(
            [
                query_grad.astype(jnp.bfloat16),
                key_grad.astype(jnp.bfloat16),
                value_grad.astype(jnp.bfloat16),
            ],
            axis=1,
        )
        query_bias_part = jnp.sum(qkv_grad[:, :features].astype(jnp.float32), axis=0)
        value_bias_part = jnp.sum(qkv_grad[:, 2 * features :].astype(jnp.float32), axis=0)
        qkv_part = jnp.einsum("rd,re->de", act_one, qkv_grad, preferred_element_type=jnp.float32)
        act_one_grad = jnp.einsum(
            "re,de->rd", qkv_grad, weight_qkv[layer_index], preferred_element_type=jnp.float32
        )
        norm_gain_one = gain_one[layer_index].astype(jnp.float32)
        norm_shift_one = shift_one[layer_index].astype(jnp.float32)
        unused_one, norm_one_pull = jax.vjp(layer_norm, layer_input, norm_gain_one, norm_shift_one)
        input_part, gain_one_part, shift_one_part = norm_one_pull(act_one_grad)
        gradient = mid_grad + input_part
        collected[layer_index] = (
            gain_one_part,
            shift_one_part,
            query_bias_part,
            value_bias_part,
            out_bias_part,
            gain_two_part,
            shift_two_part,
            up_bias_part,
            down_bias_part,
            qkv_part,
            out_part,
            up_part,
            down_part,
        )
    table_part = jax.ops.segment_sum(
        gradient, position_of_row, num_segments=position_table.shape[0]
    )
    (
        pos_embed_grad,
        norm1_gain_grad,
        norm1_bias_grad,
        query_bias_grad,
        value_bias_grad,
        out_bias_grad,
        norm2_gain_grad,
        norm2_bias_grad,
        up_bias_grad,
        down_bias_grad,
        qkv_weight_grad,
        out_weight_grad,
    ) = (
        lax.psum_scatter(table_part, ("gx", "gy"), scatter_dimension=1, tiled=True),
        lax.psum_scatter(
            stacked_member(collected, 0), ("gx", "gy"), scatter_dimension=1, tiled=True
        ),
        lax.psum_scatter(
            stacked_member(collected, 1), ("gx", "gy"), scatter_dimension=1, tiled=True
        ),
        lax.psum_scatter(
            stacked_member(collected, 2), ("gx", "gy"), scatter_dimension=1, tiled=True
        ),
        lax.psum_scatter(
            stacked_member(collected, 3), ("gx", "gy"), scatter_dimension=1, tiled=True
        ),
        lax.psum_scatter(
            stacked_member(collected, 4), ("gx", "gy"), scatter_dimension=1, tiled=True
        ),
        lax.psum_scatter(
            stacked_member(collected, 5), ("gx", "gy"), scatter_dimension=1, tiled=True
        ),
        lax.psum_scatter(
            stacked_member(collected, 6), ("gx", "gy"), scatter_dimension=1, tiled=True
        ),
        lax.psum_scatter(
            stacked_member(collected, 7), ("gx", "gy"), scatter_dimension=1, tiled=True
        ),
        lax.psum_scatter(
            stacked_member(collected, 8), ("gx", "gy"), scatter_dimension=1, tiled=True
        ),
        lax.psum_scatter(
            stacked_member(collected, 9), ("gx", "gy"), scatter_dimension=1, tiled=True
        ),
        lax.psum_scatter(
            stacked_member(collected, 10), ("gx", "gy"), scatter_dimension=1, tiled=True
        ),
    )
    up_stack = stacked_member(collected, 11)
    down_stack = stacked_member(collected, 12)
    up_weight_grad, down_weight_grad = (
        lax.psum_scatter(
            up_stack.astype(jnp.bfloat16), "gx", scatter_dimension=1, tiled=True
        ).astype(jnp.float32),
        lax.psum_scatter(
            down_stack.astype(jnp.bfloat16), "gx", scatter_dimension=2, tiled=True
        ).astype(jnp.float32),
    )
    return (
        state,
        gradient,
        pos_embed_grad,
        norm1_gain_grad,
        norm1_bias_grad,
        query_bias_grad,
        value_bias_grad,
        out_bias_grad,
        norm2_gain_grad,
        norm2_bias_grad,
        up_bias_grad,
        down_bias_grad,
        qkv_weight_grad,
        out_weight_grad,
        up_weight_grad,
        down_weight_grad,
    )


LOG2_E = 1.0 / math.log(2.0)
LANES = 128
BF16 = jnp.bfloat16
F32 = jnp.float32
MESH_ID = pl.DeviceIdType.MESH
VMEM_LIMIT = 60 * 1024 * 1024


def dot_nn(left, right):
    return lax.dot_general(left, right, (((1,), (0,)), ((), ())), preferred_element_type=F32)


def dot_nt(left, right):
    return lax.dot_general(left, right, (((1,), (1,)), ((), ())), preferred_element_type=F32)


def dot_tn(left, right):
    return lax.dot_general(left, right, (((0,), (0,)), ((), ())), preferred_element_type=F32)


def my_place():
    gx = lax.axis_index("gx")
    gy = lax.axis_index("gy")
    return gx // 2, lax.rem(gx, 2), gy // 2, lax.rem(gy, 2)


def device_at(z, x, y, core):
    return (z * 2 + x, y * 2 + core)


def flip_pairs(flip_y, flip_core):
    pairs = []
    for index in range(32):
        gx, gy = divmod(index, 4)
        pairs.append((index, gx * 4 + (gy ^ (2 * flip_y + flip_core))))
    return pairs


def to_partner(value):
    return lax.ppermute(value, ("gx", "gy"), flip_pairs(1, 0))


def to_sibling(value):
    return lax.ppermute(value, ("gx", "gy"), flip_pairs(0, 1))


def greet(place):
    z, x, y, core = place
    barrier = pltpu.get_barrier_semaphore()
    others = [device_at(lax.rem(z + k, 4), x, y, core) for k in (1, 2, 3)]
    others += [device_at(z, 1 - x, y, core), device_at(z, x, 1 - y, core)]
    others += [device_at(z, x, y, 1 - core)]
    for other in others:
        pl.semaphore_signal(barrier, inc=1, device_id=other, device_id_type=MESH_ID)
    pl.semaphore_wait(barrier, len(others))


def remote(src, dst, send_sem, recv_sem, device):
    return pltpu.make_async_remote_copy(
        src_ref=src,
        dst_ref=dst,
        send_sem=send_sem,
        recv_sem=recv_sem,
        device_id=device,
        device_id_type=MESH_ID,
    )


def gather_steps(place, shard, full, half, send, recv, local_sem):
    z, x, y, core = place
    rows = shard.shape[0]
    low, high = pl.ds(0, half), pl.ds(half, rows - half)
    keep = pltpu.make_async_copy(shard, full.at[z, x, y, core], local_sem)
    along_z = [
        remote(
            shard,
            full.at[z, x, y, core],
            send.at[k - 1],
            recv.at[k - 1],
            device_at(lax.rem(z + k, 4), x, y, core),
        )
        for k in (1, 2, 3)
    ]

    def same(ref, slot, device):
        return remote(ref, ref, send.at[slot], recv.at[slot], device)

    to_x = device_at(z, 1 - x, y, core)
    to_y = device_at(z, x, 1 - y, core)
    first = [
        same(full.at[:, x, y, core, low], 3, to_x),
        same(full.at[:, x, y, core, high], 4, to_y),
    ]
    second = [
        same(full.at[:, :, y, core, low], 5, to_y),
        same(full.at[:, x, :, core, high], 6, to_x),
    ]
    third = [same(full.at[:, :, :, core], 7, device_at(z, x, y, 1 - core))]
    return keep, along_z, first, second, third


def gather_kernel(halves, *refs):
    count = len(halves)
    shards = refs[:count]
    fulls = refs[count : 2 * count]
    send, recv, local = refs[2 * count :]
    place = my_place()
    plans = [
        gather_steps(place, shards[g], fulls[g], halves[g], send.at[g], recv.at[g], local.at[g])
        for g in range(count)
    ]

    def start_z(g):
        if g < count:
            keep, along_z = plans[g][:2]
            keep.start()
            for copy in along_z:
                copy.start()

    def start_first(g):
        if g < count:
            keep, along_z, first = plans[g][:3]
            keep.wait()
            for copy in along_z:
                copy.wait_recv()
            for copy in first:
                copy.start()

    def start_second(g):
        for copy in plans[g][2]:
            copy.wait_recv()
        for copy in plans[g][3]:
            copy.start()

    def start_third(g):
        for copy in plans[g][3]:
            copy.wait_recv()
        for copy in plans[g][4]:
            copy.start()

    greet(place)
    start_z(0)
    start_z(1)
    start_first(0)
    for g in range(count):
        start_z(g + 2)
        start_second(g)
        start_first(g + 1)
        start_third(g)
    for g in range(count):
        keep, along_z, first, second, third = plans[g]
        for copy in third:
            copy.wait_recv()
        for copy in along_z + first + second + third:
            copy.wait_send()


def gather_weights(shards, collective_id):
    count = len(shards)
    halves = tuple(shard.shape[0] // 2 for shard in shards)
    return pl.pallas_call(
        functools.partial(gather_kernel, halves),
        out_shape=[jax.ShapeDtypeStruct((4, 2, 2, 2) + shard.shape, BF16) for shard in shards],
        in_specs=[pl.BlockSpec(memory_space=pl.ANY)] * count,
        out_specs=[pl.BlockSpec(memory_space=pl.ANY)] * count,
        scratch_shapes=[
            pltpu.SemaphoreType.DMA((count, 8)),
            pltpu.SemaphoreType.DMA((count, 8)),
            pltpu.SemaphoreType.DMA((count,)),
        ],
        compiler_params=pltpu.CompilerParams(collective_id=collective_id, has_side_effects=True),
        name="gather_weights",
    )(*shards)


def reduce_kernel(shapes, *refs):
    count = len(shapes)
    parts = refs[:count]
    outs = refs[count : 2 * count]
    buffers = refs[2 * count : 2 * count + 6 * count]
    send, recv, local = refs[2 * count + 6 * count :]
    place = my_place()
    z, x, y, core = place
    to_x = device_at(z, 1 - x, y, core)
    to_y = device_at(z, x, 1 - y, core)
    to_core = device_at(z, x, y, 1 - core)
    plans = []
    for g, (rows, columns) in enumerate(shapes):
        half = rows // 2
        low, high = pl.ds(0, half), pl.ds(half, half)
        own, from_core, second_a, second_b, third, fourth = buffers[6 * g : 6 * g + 6]

        def send_to(src, dst, slot, device, g=g):
            return remote(src, dst, send.at[g, slot], recv.at[g, slot], device)

        plans.append(
            (
                pltpu.make_async_copy(parts[g].at[:, :, :, core], own, local.at[g]),
                [send_to(parts[g].at[:, :, :, 1 - core], from_core, 0, to_core)],
                [
                    send_to(own.at[:, :, 1 - y, low], second_a, 1, to_y),
                    send_to(own.at[:, 1 - x, :, high], second_b, 2, to_x),
                ],
                [
                    send_to(own.at[:, 1 - x, y, low], third.at[0], 3, to_x),
                    send_to(own.at[:, x, 1 - y, high], third.at[1], 4, to_y),
                ],
                [
                    send_to(
                        own.at[lax.rem(z + k, 4), x, y],
                        fourth.at[k - 1],
                        4 + k,
                        device_at(lax.rem(z + k, 4), x, y, core),
                    )
                    for k in (1, 2, 3)
                ],
            )
        )

    def added(left, right):
        return (left.astype(F32) + right.astype(F32)).astype(BF16)

    def start_core(g):
        if g < count:
            plans[g][0].start()
            for copy in plans[g][1]:
                copy.start()

    def start_second(g):
        if g >= count:
            return
        own, from_core = buffers[6 * g : 6 * g + 2]
        plans[g][0].wait()
        for copy in plans[g][1]:
            copy.wait_recv()

        def add_one(i, carry):
            a, b, c = i // 4, lax.rem(i // 2, 2), lax.rem(i, 2)
            own[a, b, c] = added(own[a, b, c], from_core[a, b, c])
            return carry

        lax.fori_loop(0, 16, add_one, 0)
        for copy in plans[g][2]:
            copy.start()

    def start_third(g):
        rows = shapes[g][0]
        half = rows // 2
        low, high = pl.ds(0, half), pl.ds(half, half)
        own, unused, second_a, second_b = buffers[6 * g : 6 * g + 4]
        for copy in plans[g][2]:
            copy.wait_recv()

        def add_one(i, carry):
            a, b = i // 2, lax.rem(i, 2)
            own[a, b, y, low] = added(own[a, b, y, low], second_a[a, b])
            own[a, x, b, high] = added(own[a, x, b, high], second_b[a, b])
            return carry

        lax.fori_loop(0, 8, add_one, 0)
        for copy in plans[g][3]:
            copy.start()

    def start_fourth(g):
        rows = shapes[g][0]
        half = rows // 2
        low, high = pl.ds(0, half), pl.ds(half, half)
        own, third = buffers[6 * g], buffers[6 * g + 4]
        for copy in plans[g][3]:
            copy.wait_recv()

        def add_one(a, carry):
            own[a, x, y, low] = added(own[a, x, y, low], third[0, a])
            own[a, x, y, high] = added(own[a, x, y, high], third[1, a])
            return carry

        lax.fori_loop(0, 4, add_one, 0)
        for copy in plans[g][4]:
            copy.start()

    def finish(g):
        own, fourth = buffers[6 * g], buffers[6 * g + 5]
        for copy in plans[g][4]:
            copy.wait_recv()
        total = own[z, x, y].astype(F32)
        for k in range(3):
            total = total + fourth[k].astype(F32)
        outs[g][...] = total

    greet(place)
    start_core(0)
    start_core(1)
    start_second(0)
    for g in range(count):
        start_core(g + 2)
        start_third(g)
        start_second(g + 1)
        start_fourth(g)
        if g > 0:
            finish(g - 1)
    finish(count - 1)
    for g in range(count):
        for copies in plans[g][1:]:
            for copy in copies:
                copy.wait_send()


def reduce_weights(parts, collective_id):
    count = len(parts)
    shapes = tuple(part.shape[-2:] for part in parts)
    scratch = []
    for rows, columns in shapes:
        half = rows // 2
        scratch += [
            pltpu.VMEM((4, 2, 2, rows, columns), BF16),
            pltpu.VMEM((4, 2, 2, rows, columns), BF16),
            pltpu.VMEM((4, 2, half, columns), BF16),
            pltpu.VMEM((4, 2, half, columns), BF16),
            pltpu.VMEM((2, 4, half, columns), BF16),
            pltpu.VMEM((3, rows, columns), BF16),
        ]
    return pl.pallas_call(
        functools.partial(reduce_kernel, shapes),
        out_shape=[jax.ShapeDtypeStruct(shape, F32) for shape in shapes],
        in_specs=[pl.BlockSpec(memory_space=pl.ANY)] * count,
        out_specs=[pl.BlockSpec(memory_space=pltpu.VMEM)] * count,
        scratch_shapes=scratch
        + [
            pltpu.SemaphoreType.DMA((count, 8)),
            pltpu.SemaphoreType.DMA((count, 8)),
            pltpu.SemaphoreType.DMA((count,)),
        ],
        compiler_params=pltpu.CompilerParams(
            collective_id=collective_id, has_side_effects=True, vmem_limit_bytes=VMEM_LIMIT
        ),
        name="reduce_weights",
    )(*parts)


def lane_marks(head):
    lane = lax.broadcasted_iota(jnp.int32, (1, LANES), 1)
    own = (lane // HEAD_DIM == head).astype(F32)
    spare = HEAD_DIM * (1 - head)
    return lane, own, spare


def split_three(column):
    high = column.astype(BF16).astype(F32)
    rest = column - high
    middle = rest.astype(BF16).astype(F32)
    return high, middle, rest - middle


def attention_kernel(block, q_ref, ko_ref, ks_ref, vo_ref, vs_ref, bias_ref, out_ref, exact_ref, lse_ref, keys, values):
    pair = pl.program_id(0)
    rows = q_ref.shape[0]
    values[0:rows] = vo_ref[...]
    values[rows:] = vs_ref[...]
    lanes = lax.broadcasted_iota(jnp.int32, (1, LANES), 1)

    @pl.when(pair == 0)
    def _():
        lse_ref[...] = jnp.zeros_like(lse_ref)

    mixed = [[], []]
    totals = [[], []]
    for head in range(2):
        lane, own, spare = lane_marks(head)
        own16 = own.astype(BF16)
        at_spare = (lane == spare).astype(BF16)
        keys[0:rows] = ko_ref[...] * own16 + bias_ref[0:rows] * at_spare
        keys[rows:] = ks_ref[...] * own16 + bias_ref[rows:] * at_spare
        for start in range(0, rows, block):
            query = q_ref[start : start + block] * own16 + at_spare
            scores = dot_nt(query, keys[...])
            top = jnp.max(scores, axis=-1, keepdims=True)
            weights = jnp.exp2(scores - top)
            total = jnp.sum(weights, axis=-1, keepdims=True)
            summed = dot_nn(weights.astype(BF16), values[...])
            mixed[head].append(summed * (1.0 / total))
            totals[head].append(top + jnp.log2(total))
    for index, start in enumerate(range(0, rows, block)):
        rows_at = slice(start, start + block)
        both = jnp.where(lanes < HEAD_DIM, mixed[0][index], mixed[1][index])
        out_ref[rows_at] = both.astype(BF16)
        exact_ref[rows_at] = both
        held = lse_ref[rows_at]
        held = jnp.where(lanes == 2 * pair, totals[0][index], held)
        lse_ref[rows_at] = jnp.where(lanes == 2 * pair + 1, totals[1][index], held)


def attention_forward(queries, keys_own, keys_sib, values_own, values_sib, bias):
    rows, width = queries.shape
    block = rows // 2
    column = pl.BlockSpec((rows, LANES), lambda pair: (0, pair))
    return pl.pallas_call(
        functools.partial(attention_kernel, block),
        grid=(width // LANES,),
        out_shape=[
            jax.ShapeDtypeStruct((rows, width), BF16),
            jax.ShapeDtypeStruct((rows, width), F32),
            jax.ShapeDtypeStruct((rows, LANES), F32),
        ],
        in_specs=[column] * 5 + [pl.BlockSpec((2 * rows, LANES), lambda pair: (0, 0))],
        out_specs=[column, column, pl.BlockSpec((rows, LANES), lambda pair: (0, 0))],
        scratch_shapes=[pltpu.VMEM((2 * rows, LANES), BF16), pltpu.VMEM((2 * rows, LANES), BF16)],
        compiler_params=pltpu.CompilerParams(vmem_limit_bytes=VMEM_LIMIT),
        cost_estimate=pl.CostEstimate(
            flops=8 * rows * 2 * rows * width, bytes_accessed=12 * rows * width, transcendentals=0
        ),
        name="attention_forward",
    )(queries, keys_own, keys_sib, values_own, values_sib, bias)


def attention_back_kernel(
    q_ref, ko_ref, ks_ref, vo_ref, vs_ref, do_ref, mix_ref, lse_ref, bias_ref,
    dq_ref, dko_ref, dks_ref, dvo_ref, dvs_ref,
):
    pair = pl.program_id(0)
    rows = q_ref.shape[0]
    block = rows // 2
    lanes = lax.broadcasted_iota(jnp.int32, (1, LANES), 1)
    query = q_ref[...]
    grad = do_ref[...]
    product = grad.astype(F32) * mix_ref[...]
    heads = []
    for head in range(2):
        lane, own, spare = lane_marks(head)
        own16 = own.astype(BF16)
        lse = jnp.sum(jnp.where(lanes == 2 * pair + head, lse_ref[...], 0.0), axis=-1, keepdims=True)
        inner = jnp.sum(product * own, axis=-1, keepdims=True)
        lse_parts, inner_parts = split_three(-lse), split_three(-inner)
        query_own = query * own16
        grad_own = grad * own16
        query_aug = jnp.where(lane == spare, 1.0, 0.0)
        grad_aug = jnp.zeros((1, LANES), F32)
        for k in range(3):
            query_aug = jnp.where(lane == spare + 1 + k, lse_parts[k], query_aug)
            grad_aug = jnp.where(lane == spare + 1 + k, inner_parts[k], grad_aug)
        query_aug = query_own + query_aug.astype(BF16)
        grad_aug = grad_own + grad_aug.astype(BF16)
        at_spare = (lane == spare).astype(BF16)
        ones = ((lane > spare) & (lane < spare + 4)).astype(BF16)
        heads.append((own16, at_spare, ones, query_own, grad_own, query_aug, grad_aug))
    query_grad = jnp.zeros((LANES, rows), F32)
    for side, (k_ref, v_ref, dk_ref, dv_ref) in enumerate(
        ((ko_ref, vo_ref, dko_ref, dvo_ref), (ks_ref, vs_ref, dks_ref, dvs_ref))
    ):
        for start in range(0, rows, block):
            at = slice(start, start + block)
            key, value = k_ref[at], v_ref[at]
            shift = bias_ref[side * rows + start : side * rows + start + block]
            key_grad = jnp.zeros((block, LANES), F32)
            value_grad = jnp.zeros((block, LANES), F32)
            for own16, at_spare, ones, query_own, grad_own, query_aug, grad_aug in heads:
                key_own = key * own16
                weights = jnp.exp2(dot_nt(key_own + shift * at_spare + ones, query_aug))
                weight_grad = dot_nt(value * own16 + ones, grad_aug)
                score_grad = (weights * weight_grad).astype(BF16)
                value_grad = value_grad + dot_nn(weights.astype(BF16), grad_own)
                key_grad = key_grad + dot_nn(score_grad, query_own)
                query_grad = query_grad + dot_tn(key_own, score_grad)
            dk_ref[at] = (key_grad * (1.0 / LOG2_E)).astype(BF16)
            dv_ref[at] = value_grad.astype(BF16)
    dq_ref[...] = (jnp.transpose(query_grad) * HEAD_DIM ** (-0.5)).astype(BF16)


def attention_backward(queries, keys_own, keys_sib, values_own, values_sib, mixed_grad, mixed, lse, bias):
    rows, width = queries.shape
    column = pl.BlockSpec((rows, LANES), lambda pair: (0, pair))
    fixed = pl.BlockSpec((rows, LANES), lambda pair: (0, 0))
    return pl.pallas_call(
        attention_back_kernel,
        grid=(width // LANES,),
        out_shape=[jax.ShapeDtypeStruct((rows, width), BF16)] * 5,
        in_specs=[column] * 7 + [fixed, pl.BlockSpec((2 * rows, LANES), lambda pair: (0, 0))],
        out_specs=[column] * 5,
        compiler_params=pltpu.CompilerParams(vmem_limit_bytes=VMEM_LIMIT),
        cost_estimate=pl.CostEstimate(
            flops=20 * rows * 2 * rows * width, bytes_accessed=24 * rows * width, transcendentals=0
        ),
        name="attention_backward",
    )(queries, keys_own, keys_sib, values_own, values_sib, mixed_grad, mixed, lse, bias)


def norm_parts(values):
    row_mean = jnp.mean(values, axis=-1, keepdims=True)
    centred = values - row_mean
    row_var = jnp.mean(centred * centred, axis=-1, keepdims=True)
    rstd = lax.rsqrt(row_var + EPSILON)
    return centred * rstd, rstd


def norm_back(values, gain, grad):
    normed, rstd = norm_parts(values)
    scaled = grad * gain
    first = jnp.mean(scaled, axis=-1, keepdims=True)
    second = jnp.mean(scaled * normed, axis=-1, keepdims=True)
    back = (scaled - first - normed * second) * rstd
    return back, jnp.sum(grad * normed, axis=0), jnp.sum(grad, axis=0)


def split_rows(values):
    high = values.astype(BF16)
    rest = values - high.astype(F32)
    middle = rest.astype(BF16)
    return high, middle, (rest - middle.astype(F32)).astype(BF16)


def chip_shards(
    patches,
    clip_of_row,
    position_of_row,
    pos_embed,
    norm1_gain,
    norm1_bias,
    query_bias,
    value_bias,
    out_bias,
    norm2_gain,
    norm2_bias,
    up_bias,
    down_bias,
    qkv_weight,
    out_weight,
    up_weight,
    down_weight,
    cotangent,
):
    layers, owned, features = qkv_weight.shape[0], qkv_weight.shape[1], patches.shape[1]
    pieces = lax.axis_size("gy")
    piece_rows = patches.shape[0]
    devices = features // owned
    positions = pos_embed.shape[0]
    padded_positions = -(-positions // 256) * 256
    slots = -(-positions // pieces)
    slots = -(-slots // 16) * 16
    rows = 2 * slots
    hidden_width = up_weight.shape[2]
    up_rows = up_weight.shape[1]
    gy = lax.axis_index("gy")
    side, core = gy // 2, lax.rem(gy, 2)

    low_clip, high_clip = jnp.min(clip_of_row), jnp.max(clip_of_row)
    low_is_long = 2 * jnp.sum((clip_of_row == low_clip).astype(jnp.int32)) > clip_of_row.shape[0]
    long_clip = jnp.where(low_is_long, low_clip, high_clip)
    kept_all = ((clip_of_row == long_clip) == (side == 0)).reshape(pieces, piece_rows)
    kept_count = jnp.sum(kept_all.astype(jnp.int32), axis=1)
    kept = lax.dynamic_index_in_dim(kept_all, gy, 0, keepdims=False)
    rank_kept = jnp.cumsum(kept.astype(jnp.int32)) - 1
    rank_sent = jnp.arange(piece_rows, dtype=jnp.int32) - rank_kept - 1
    slot = jnp.arange(slots, dtype=jnp.int32)[:, None]
    pick_kept = (slot == rank_kept[None]) & kept[None]
    pick_sent = (slot == rank_sent[None]) & jnp.logical_not(kept)[None]
    choose = jnp.concatenate([pick_kept, pick_sent], axis=0)
    choose16 = choose.astype(BF16)
    sorted_rows = dot_nn(choose16, jnp.concatenate([patches, cotangent], axis=1)).astype(BF16)
    sorted_positions = jnp.sum(jnp.where(choose, position_of_row[None], 0), axis=1)
    received = to_partner(sorted_rows[slots:])
    received_positions = to_partner(sorted_positions[slots:])
    own_rows = jnp.concatenate([sorted_rows[:slots], received], axis=0)
    row_positions = jnp.concatenate([sorted_positions[:slots], received_positions])
    chip_patches, chip_cotangent = own_rows[:, :features], own_rows[:, features:]

    def slot_bias(of_core):
        mine = lax.dynamic_index_in_dim(kept_count, side * 2 + of_core, 0, keepdims=False)
        theirs = lax.dynamic_index_in_dim(kept_count, (1 - side) * 2 + of_core, 0, keepdims=False)
        steps = jnp.arange(slots, dtype=jnp.int32)
        used = jnp.concatenate([steps < mine, steps < theirs])
        return jnp.where(used, 0.0, MASKED)

    bias = jnp.concatenate([slot_bias(core), slot_bias(1 - core)]).astype(BF16)
    bias = jnp.broadcast_to(bias[:, None], (2 * rows, LANES))

    narrow = jnp.stack(
        [norm1_gain, norm1_bias, query_bias, value_bias, out_bias, norm2_gain, norm2_bias, down_bias],
        axis=1,
    )
    small = jnp.concatenate([narrow.reshape(-1), up_bias.reshape(-1)])
    table_shard = jnp.concatenate(
        [
            jnp.pad(pos_embed.T, ((0, 0), (0, padded_positions - positions))),
            jnp.pad(small[None], ((0, 7), (0, padded_positions - small.shape[0]))),
        ],
        axis=0,
    )
    shards = [table_shard]
    for layer in range(layers):
        qkv = jnp.transpose(qkv_weight[layer].reshape(owned, 3, features), (1, 0, 2))
        shards.append(jnp.concatenate([qkv.reshape(3 * owned, features), out_weight[layer]], axis=0))
        shards.append(jnp.concatenate([up_weight[layer], down_weight[layer].T], axis=0))
    gathered = gather_weights(shards, 0)
    table_all = gathered[0].reshape(devices, owned + 8, padded_positions)
    table = table_all[:, :owned].reshape(features, padded_positions)
    small_all = table_all[:, owned, : small.shape[0]].astype(F32)
    count = narrow.shape[1]
    split = layers * count * owned
    narrow_all = jnp.transpose(
        small_all[:, :split].reshape(devices, layers, count, owned), (1, 2, 0, 3)
    ).reshape(layers, count, features)
    up_bias_all = jnp.transpose(
        small_all[:, split:].reshape(devices, layers, -1), (1, 0, 2)
    ).reshape(layers, -1)

    position_ids = jnp.arange(padded_positions, dtype=jnp.int32)
    lookup = (row_positions[:, None] == position_ids[None]).astype(BF16)
    state = chip_patches.astype(F32) + dot_nt(lookup, table)
    score_scale = HEAD_DIM ** (-0.5) * LOG2_E

    stored = []
    for layer in range(layers):
        gain_one, shift_one, bias_query, bias_value, bias_out, gain_two, shift_two, bias_down = (
            narrow_all[layer, i] for i in range(count)
        )
        attn = gathered[1 + 2 * layer].reshape(devices, 4, owned, features)
        weight_q, weight_k, weight_v, weight_o = (
            attn[:, i].reshape(features, features) for i in range(4)
        )
        mlp = gathered[2 + 2 * layer].reshape(devices // pieces, pieces, 2, up_rows, hidden_width)
        weight_up, weight_down = (
            jnp.transpose(mlp[:, :, i], (0, 2, 1, 3)).reshape(features, pieces * hidden_width)
            for i in range(2)
        )
        normed, unused = norm_parts(state)
        act_one = (normed * gain_one + shift_one).astype(BF16)
        queries = ((dot_nn(act_one, weight_q) + bias_query) * score_scale).astype(BF16)
        key_rows = dot_nn(act_one, weight_k).astype(BF16)
        value_rows = (dot_nn(act_one, weight_v) + bias_value).astype(BF16)
        key_sib, value_sib = to_sibling(key_rows), to_sibling(value_rows)
        mixed, exact, lse = attention_forward(queries, key_rows, key_sib, value_rows, value_sib, bias)
        middle = state + dot_nn(mixed, weight_o) + bias_out
        normed_two, unused = norm_parts(middle)
        act_two = (normed_two * gain_two + shift_two).astype(BF16)
        pre_act = dot_nn(act_two, weight_up) + up_bias_all[layer]
        below = 0.5 * (1.0 + lax.erf(pre_act * SQRT_HALF))
        hidden = (pre_act * below).astype(BF16)
        slope = (below + pre_act * jnp.exp(-0.5 * pre_act * pre_act) * NORMAL_PEAK).astype(BF16)
        layer_out = middle + dot_nn(hidden, weight_down.T) + bias_down
        stored.append(
            (state, act_one, queries, key_rows, key_sib, value_rows, value_sib, mixed, exact, lse, middle,
             act_two, hidden, slope, weight_q, weight_k, weight_v, weight_o, weight_up, weight_down,
             gain_one, gain_two)
        )
        state = layer_out

    def from_chip(values_own, values_back):
        both = jnp.concatenate([values_own, values_back], axis=0)
        parts = split_rows(both)
        return sum(dot_tn(choose16, part) for part in parts)

    activations = from_chip(state[:slots], to_partner(state[slots:]))

    def by_owner(part):
        return part.reshape(devices, owned, part.shape[1])

    def by_blocks(part):
        return jnp.transpose(
            part.reshape(devices // pieces, up_rows, pieces, hidden_width), (0, 2, 1, 3)
        ).reshape(devices, up_rows, hidden_width)

    gradient = chip_cotangent.astype(F32)
    attn_parts, mlp_parts, narrow_parts, up_bias_parts = ([None] * layers for _ in range(4))
    for layer in reversed(range(layers)):
        (before, act_one, queries, key_rows, key_sib, value_rows, value_sib, mixed, exact, lse, middle,
         act_two, hidden, slope, weight_q, weight_k, weight_v, weight_o, weight_up, weight_down,
         gain_one, gain_two) = stored[layer]
        grad_two = gradient.astype(BF16)
        down_bias_part = jnp.sum(grad_two.astype(F32), axis=0)
        down_part = dot_tn(grad_two, hidden)
        pre_grad = (dot_nn(grad_two, weight_down) * slope.astype(F32)).astype(BF16)
        up_part = dot_tn(act_two, pre_grad)
        up_bias_parts[layer] = jnp.sum(pre_grad.astype(F32), axis=0)
        act_two_grad = dot_nt(pre_grad, weight_up)
        mlp_parts[layer] = jnp.concatenate([by_blocks(up_part), by_blocks(down_part)], axis=1).astype(BF16)
        back_two, gain_two_part, shift_two_part = norm_back(middle, gain_two, act_two_grad)
        mid_grad = gradient + back_two
        grad_one = mid_grad.astype(BF16)
        out_bias_part = jnp.sum(grad_one.astype(F32), axis=0)
        out_part = dot_tn(mixed, grad_one)
        mixed_grad = dot_nt(grad_one, weight_o).astype(BF16)
        query_grad, key_own, key_far, value_own, value_far = attention_backward(
            queries, key_rows, key_sib, value_rows, value_sib, mixed_grad, exact, lse, bias
        )
        key_grad = (key_own.astype(F32) + to_sibling(key_far).astype(F32)).astype(BF16)
        value_grad = (value_own.astype(F32) + to_sibling(value_far).astype(F32)).astype(BF16)
        query_bias_part = jnp.sum(query_grad.astype(F32), axis=0)
        value_bias_part = jnp.sum(value_grad.astype(F32), axis=0)
        attn_parts[layer] = jnp.concatenate(
            [by_owner(dot_tn(act_one, g)) for g in (query_grad, key_grad, value_grad)]
            + [by_owner(out_part)],
            axis=1,
        ).astype(BF16)
        act_one_grad = (
            dot_nt(query_grad, weight_q) + dot_nt(key_grad, weight_k) + dot_nt(value_grad, weight_v)
        )
        back_one, gain_one_part, shift_one_part = norm_back(before, gain_one, act_one_grad)
        gradient = mid_grad + back_one
        narrow_parts[layer] = jnp.stack(
            [gain_one_part, shift_one_part, query_bias_part, value_bias_part, out_bias_part,
             gain_two_part, shift_two_part, down_bias_part]
        )
    input_grad = from_chip(gradient[:slots], to_partner(gradient[slots:]))

    table_part = dot_tn(gradient.astype(BF16), lookup)
    narrow_part = jnp.transpose(
        jnp.stack(narrow_parts).reshape(layers, count, devices, owned), (2, 0, 1, 3)
    ).reshape(devices, split)
    up_bias_part = jnp.transpose(
        jnp.stack(up_bias_parts).reshape(layers, devices, -1), (1, 0, 2)
    ).reshape(devices, -1)
    small_part = jnp.concatenate([narrow_part, up_bias_part], axis=1)[:, None]
    table_parts = jnp.concatenate(
        [
            by_owner(table_part),
            jnp.pad(small_part, ((0, 0), (0, 7), (0, padded_positions - small_part.shape[2]))),
        ],
        axis=1,
    ).astype(BF16)
    grouped = []
    for layer in reversed(range(layers)):
        grouped += [mlp_parts[layer], attn_parts[layer]]
    grouped.append(table_parts)
    sums = reduce_weights([part.reshape((4, 2, 2, 2) + part.shape[1:]) for part in grouped], 1)
    table_sum = sums[-1]
    pos_embed_grad = table_sum[:owned, :positions].T
    small_sum = table_sum[owned, : small.shape[0]]
    narrow_sum = small_sum[:split].reshape(layers, count, owned)
    up_bias_grad = small_sum[split:].reshape(layers, -1)
    mlp_sums = sums[-3::-2]
    attn_sums = sums[-2::-2]
    qkv_weight_grad = jnp.stack(
        [
            jnp.transpose(part[: 3 * owned].reshape(3, owned, features), (1, 0, 2)).reshape(owned, -1)
            for part in attn_sums
        ]
    )
    out_weight_grad = jnp.stack([part[3 * owned :] for part in attn_sums])
    up_weight_grad = jnp.stack([part[:up_rows] for part in mlp_sums])
    down_weight_grad = jnp.stack([part[up_rows:].T for part in mlp_sums])
    return (
        activations,
        input_grad,
        pos_embed_grad,
        *(narrow_sum[:, i] for i in range(7)),
        up_bias_grad,
        narrow_sum[:, 7],
        qkv_weight_grad,
        out_weight_grad,
        up_weight_grad,
        down_weight_grad,
    )


def solution(mesh):
    return jax.shard_map(
        chip_shards if mesh.shape["gx"] == 8 and mesh.shape["gy"] == 4 else shards,
        mesh=mesh,
        in_specs=(
            P(("gx", "gy"), None),
            P("gx"),
            P(("gx", "gy")),
            P(None, ("gx", "gy")),
            P(None, ("gx", "gy")),
            P(None, ("gx", "gy")),
            P(None, ("gx", "gy")),
            P(None, ("gx", "gy")),
            P(None, ("gx", "gy")),
            P(None, ("gx", "gy")),
            P(None, ("gx", "gy")),
            P(None, ("gx", "gy")),
            P(None, ("gx", "gy")),
            P(None, ("gx", "gy"), None),
            P(None, ("gx", "gy"), None),
            P(None, "gx", "gy"),
            P(None, "gy", "gx"),
            P(("gx", "gy"), None),
        ),
        out_specs=(
            P(("gx", "gy"), None),
            P(("gx", "gy"), None),
            P(None, ("gx", "gy")),
            P(None, ("gx", "gy")),
            P(None, ("gx", "gy")),
            P(None, ("gx", "gy")),
            P(None, ("gx", "gy")),
            P(None, ("gx", "gy")),
            P(None, ("gx", "gy")),
            P(None, ("gx", "gy")),
            P(None, ("gx", "gy")),
            P(None, ("gx", "gy")),
            P(None, ("gx", "gy"), None),
            P(None, ("gx", "gy"), None),
            P(None, "gx", "gy"),
            P(None, "gy", "gx"),
        ),
        check_vma=False,
    )
```

```python
import functools
import math

import jax
import jax.numpy as jnp
from jax import lax
from jax.experimental import pallas as pl
from jax.experimental.pallas import tpu as pltpu
from jax.sharding import PartitionSpec as P

HEAD_DIM = 64


EPSILON = 1e-06
SQRT_HALF = 1.0 / math.sqrt(2.0)
NORMAL_PEAK = 1.0 / math.sqrt(2.0 * math.pi)
MASKED = -1e30


def layer_norm(values, norm_gain, norm_shift):
    row_mean = jnp.mean(values, axis=-1, keepdims=True)
    centred = values - row_mean
    row_var = jnp.mean(centred * centred, axis=-1, keepdims=True)
    return centred * lax.rsqrt(row_var + EPSILON) * norm_gain + norm_shift


def gelu_slope(pre_act):
    return (
        0.5 * (1.0 + lax.erf(pre_act * SQRT_HALF))
        + pre_act * jnp.exp(-0.5 * pre_act * pre_act) * NORMAL_PEAK
    )


def column_pair(matrix, pair_index, pair_width):
    block = lax.dynamic_slice_in_dim(matrix, pair_index * pair_width, pair_width, 1)
    return block.reshape(matrix.shape[0], 2, pair_width // 2)


def join_pairs(stacked):
    return jnp.transpose(stacked, (1, 0, 2)).reshape(
        stacked.shape[1], stacked.shape[0] * stacked.shape[2]
    )


def pair_scores(head_query, head_keys, same_clip):
    scores = jnp.einsum(
        "qhd,khd->hqk", head_query, head_keys, preferred_element_type=jnp.float32
    ) * HEAD_DIM ** (-0.5)
    return jnp.where(same_clip[None], scores, MASKED)


def pair_parts(head_query, head_keys, head_values, head_grad, same_clip, pair_total):
    scores = pair_scores(head_query, head_keys, same_clip)
    weights = jnp.exp(scores - pair_total)
    weight_grad = jnp.einsum(
        "qhd,khd->hqk", head_grad, head_values, preferred_element_type=jnp.float32
    )
    return (weights, weight_grad)


def attend(queries, key_rows, value_rows, same_clip):
    pair_width = 2 * HEAD_DIM
    pair_count = queries.shape[1] // pair_width

    def one_pair(pair_index):
        head_query = column_pair(queries, pair_index, pair_width)
        head_keys = column_pair(key_rows, pair_index, pair_width)
        head_values = column_pair(value_rows, pair_index, pair_width)
        scores = pair_scores(head_query, head_keys, same_clip)
        row_max = jnp.max(scores, axis=-1, keepdims=True)
        log_total = row_max + jnp.log(jnp.sum(jnp.exp(scores - row_max), axis=-1, keepdims=True))
        weights = jnp.exp(scores - log_total).astype(jnp.bfloat16)
        mixed = jnp.einsum("hqk,khd->qhd", weights, head_values, preferred_element_type=jnp.float32)
        return (mixed.reshape(queries.shape[0], pair_width), log_total)

    mixed, log_total = lax.map(one_pair, jnp.arange(pair_count))
    return (join_pairs(mixed), log_total)


def attend_back(queries, key_rows, value_rows, same_clip, log_total, mixed_grad):
    pair_width = 2 * HEAD_DIM
    pair_count = queries.shape[1] // pair_width
    score_scale = HEAD_DIM ** (-0.5)

    def one_pair(pair_inputs):
        pair_index, pair_total = pair_inputs
        head_query = column_pair(queries, pair_index, pair_width)
        head_keys = column_pair(key_rows, pair_index, pair_width)
        head_values = column_pair(value_rows, pair_index, pair_width)
        head_grad = column_pair(mixed_grad, pair_index, pair_width)
        weights, weight_grad = pair_parts(
            head_query, head_keys, head_values, head_grad, same_clip, pair_total
        )
        value_grad = jnp.einsum(
            "hqk,qhd->khd",
            weights.astype(jnp.bfloat16),
            head_grad,
            preferred_element_type=jnp.float32,
        )
        inner = jnp.sum(weights * weight_grad, axis=-1, keepdims=True)
        score_grad = (weights * (weight_grad - inner)).astype(jnp.bfloat16)
        query_grad = (
            jnp.einsum("hqk,khd->qhd", score_grad, head_keys, preferred_element_type=jnp.float32)
            * score_scale
        )
        key_grad = (
            jnp.einsum("hqk,qhd->khd", score_grad, head_query, preferred_element_type=jnp.float32)
            * score_scale
        )
        return (
            query_grad.reshape(queries.shape[0], pair_width),
            key_grad.reshape(key_rows.shape[0], pair_width),
            value_grad.reshape(key_rows.shape[0], pair_width),
        )

    query_grad, key_grad, value_grad = lax.map(one_pair, (jnp.arange(pair_count), log_total))
    return (join_pairs(query_grad), join_pairs(key_grad), join_pairs(value_grad))


def stacked_member(collected, member_index):
    return jnp.stack([entry[member_index] for entry in collected])


def shards(
    patches,
    clip_of_row,
    position_of_row,
    pos_embed,
    norm1_gain,
    norm1_bias,
    query_bias,
    value_bias,
    out_bias,
    norm2_gain,
    norm2_bias,
    up_bias,
    down_bias,
    qkv_weight,
    out_weight,
    up_weight,
    down_weight,
    cotangent,
):
    (
        position_table,
        gain_one,
        shift_one,
        bias_query,
        bias_value,
        bias_out,
        gain_two,
        shift_two,
        bias_up,
        bias_down,
        weight_qkv,
        weight_out,
    ) = (
        lax.all_gather(pos_embed, ("gx", "gy"), axis=1, tiled=True),
        lax.all_gather(norm1_gain, ("gx", "gy"), axis=1, tiled=True),
        lax.all_gather(norm1_bias, ("gx", "gy"), axis=1, tiled=True),
        lax.all_gather(query_bias, ("gx", "gy"), axis=1, tiled=True),
        lax.all_gather(value_bias, ("gx", "gy"), axis=1, tiled=True),
        lax.all_gather(out_bias, ("gx", "gy"), axis=1, tiled=True),
        lax.all_gather(norm2_gain, ("gx", "gy"), axis=1, tiled=True),
        lax.all_gather(norm2_bias, ("gx", "gy"), axis=1, tiled=True),
        lax.all_gather(up_bias, ("gx", "gy"), axis=1, tiled=True),
        lax.all_gather(down_bias, ("gx", "gy"), axis=1, tiled=True),
        lax.all_gather(qkv_weight, ("gx", "gy"), axis=1, tiled=True),
        lax.all_gather(out_weight, ("gx", "gy"), axis=1, tiled=True),
    )
    block_up, block_down = (
        lax.all_gather(up_weight, "gx", axis=1, tiled=True),
        lax.all_gather(down_weight, "gx", axis=2, tiled=True),
    )
    layer_count = qkv_weight.shape[0]
    features = patches.shape[1]
    row_count = patches.shape[0]
    hidden_width = block_up.shape[2]
    member = lax.axis_index("gy")
    hidden_start = member * hidden_width
    own_clip = lax.dynamic_slice_in_dim(clip_of_row, member * row_count, row_count)
    same_clip = own_clip[:, None] == clip_of_row[None, :]
    state = patches.astype(jnp.float32) + position_table[position_of_row].astype(jnp.float32)
    stored = []
    for layer_index in range(layer_count):
        norm_gain_one = gain_one[layer_index].astype(jnp.float32)
        norm_shift_one = shift_one[layer_index].astype(jnp.float32)
        act_one = layer_norm(state, norm_gain_one, norm_shift_one).astype(jnp.bfloat16)
        projected = jnp.dot(act_one, weight_qkv[layer_index], preferred_element_type=jnp.float32)
        queries = (projected[:, :features] + bias_query[layer_index].astype(jnp.float32)).astype(
            jnp.bfloat16
        )
        key_rows = projected[:, features : 2 * features].astype(jnp.bfloat16)
        value_rows = (
            projected[:, 2 * features :] + bias_value[layer_index].astype(jnp.float32)
        ).astype(jnp.bfloat16)
        all_keys, all_values = (
            lax.all_gather(key_rows, "gy", axis=0, tiled=True),
            lax.all_gather(value_rows, "gy", axis=0, tiled=True),
        )
        mixed, log_total = attend(queries, all_keys, all_values, same_clip)
        attended = mixed.astype(jnp.bfloat16)
        middle = (
            state
            + jnp.dot(attended, weight_out[layer_index], preferred_element_type=jnp.float32)
            + bias_out[layer_index].astype(jnp.float32)
        )
        norm_gain_two = gain_two[layer_index].astype(jnp.float32)
        norm_shift_two = shift_two[layer_index].astype(jnp.float32)
        act_two = layer_norm(middle, norm_gain_two, norm_shift_two).astype(jnp.bfloat16)
        up_columns = lax.dynamic_slice_in_dim(
            bias_up[layer_index], hidden_start, hidden_width
        ).astype(jnp.float32)
        mlp_rows = lax.all_gather(act_two, "gy", axis=0, tiled=True)
        pre_act = (
            jnp.dot(mlp_rows, block_up[layer_index], preferred_element_type=jnp.float32)
            + up_columns
        )
        hidden = jax.nn.gelu(pre_act, approximate=False).astype(jnp.bfloat16)
        partial_out = jnp.dot(hidden, block_down[layer_index], preferred_element_type=jnp.float32)
        mlp_out = lax.psum_scatter(
            partial_out.astype(jnp.bfloat16), "gy", scatter_dimension=0, tiled=True
        ).astype(jnp.float32)
        stored.append(
            (
                state,
                act_one,
                queries,
                key_rows,
                value_rows,
                all_keys,
                all_values,
                log_total,
                attended,
                middle,
                mlp_rows,
                pre_act,
                hidden,
            )
        )
        state = middle + mlp_out + bias_down[layer_index].astype(jnp.float32)
    gradient = cotangent.astype(jnp.float32)
    collected = [None] * layer_count
    for layer_index in reversed(range(layer_count)):
        (
            layer_input,
            act_one,
            queries,
            key_rows,
            value_rows,
            kept_keys,
            kept_values,
            log_total,
            attended,
            middle,
            mlp_rows,
            pre_act,
            hidden,
        ) = stored[layer_index]
        grad_two = gradient.astype(jnp.bfloat16)
        down_bias_part = jnp.sum(grad_two.astype(jnp.float32), axis=0)
        grad_rows = lax.all_gather(grad_two, "gy", axis=0, tiled=True)
        down_part = jnp.einsum("rf,rd->fd", hidden, grad_rows, preferred_element_type=jnp.float32)
        hidden_grad = jnp.einsum(
            "rd,fd->rf", grad_rows, block_down[layer_index], preferred_element_type=jnp.float32
        )
        pre_grad = (hidden_grad * gelu_slope(pre_act)).astype(jnp.bfloat16)
        up_part = jnp.einsum("rd,rf->df", mlp_rows, pre_grad, preferred_element_type=jnp.float32)
        up_columns_grad = jnp.sum(pre_grad.astype(jnp.float32), axis=0)
        up_bias_part = lax.dynamic_update_slice_in_dim(
            jnp.zeros((bias_up.shape[1],), jnp.float32), up_columns_grad, hidden_start, 0
        )
        rows_grad = jnp.einsum(
            "rf,df->rd", pre_grad, block_up[layer_index], preferred_element_type=jnp.float32
        )
        act_two_grad = lax.psum_scatter(
            rows_grad.astype(jnp.bfloat16), "gy", scatter_dimension=0, tiled=True
        ).astype(jnp.float32)
        norm_gain_two = gain_two[layer_index].astype(jnp.float32)
        norm_shift_two = shift_two[layer_index].astype(jnp.float32)
        unused_two, norm_two_pull = jax.vjp(layer_norm, middle, norm_gain_two, norm_shift_two)
        middle_part, gain_two_part, shift_two_part = norm_two_pull(act_two_grad)
        mid_grad = gradient + middle_part
        grad_one = mid_grad.astype(jnp.bfloat16)
        out_bias_part = jnp.sum(grad_one.astype(jnp.float32), axis=0)
        out_part = jnp.einsum("rd,re->de", attended, grad_one, preferred_element_type=jnp.float32)
        mixed_grad = jnp.einsum(
            "re,de->rd", grad_one, weight_out[layer_index], preferred_element_type=jnp.float32
        ).astype(jnp.bfloat16)
        query_grad, key_grad, value_grad = attend_back(
            queries, kept_keys, kept_values, same_clip, log_total, mixed_grad
        )
        key_grad, value_grad = (
            lax.psum_scatter(
                key_grad.astype(jnp.bfloat16), "gy", scatter_dimension=0, tiled=True
            ).astype(jnp.float32),
            lax.psum_scatter(
                value_grad.astype(jnp.bfloat16), "gy", scatter_dimension=0, tiled=True
            ).astype(jnp.float32),
        )
        qkv_grad = jnp.concatenate(
            [
                query_grad.astype(jnp.bfloat16),
                key_grad.astype(jnp.bfloat16),
                value_grad.astype(jnp.bfloat16),
            ],
            axis=1,
        )
        query_bias_part = jnp.sum(qkv_grad[:, :features].astype(jnp.float32), axis=0)
        value_bias_part = jnp.sum(qkv_grad[:, 2 * features :].astype(jnp.float32), axis=0)
        qkv_part = jnp.einsum("rd,re->de", act_one, qkv_grad, preferred_element_type=jnp.float32)
        act_one_grad = jnp.einsum(
            "re,de->rd", qkv_grad, weight_qkv[layer_index], preferred_element_type=jnp.float32
        )
        norm_gain_one = gain_one[layer_index].astype(jnp.float32)
        norm_shift_one = shift_one[layer_index].astype(jnp.float32)
        unused_one, norm_one_pull = jax.vjp(layer_norm, layer_input, norm_gain_one, norm_shift_one)
        input_part, gain_one_part, shift_one_part = norm_one_pull(act_one_grad)
        gradient = mid_grad + input_part
        collected[layer_index] = (
            gain_one_part,
            shift_one_part,
            query_bias_part,
            value_bias_part,
            out_bias_part,
            gain_two_part,
            shift_two_part,
            up_bias_part,
            down_bias_part,
            qkv_part,
            out_part,
            up_part,
            down_part,
        )
    table_part = jax.ops.segment_sum(
        gradient, position_of_row, num_segments=position_table.shape[0]
    )
    (
        pos_embed_grad,
        norm1_gain_grad,
        norm1_bias_grad,
        query_bias_grad,
        value_bias_grad,
        out_bias_grad,
        norm2_gain_grad,
        norm2_bias_grad,
        up_bias_grad,
        down_bias_grad,
        qkv_weight_grad,
        out_weight_grad,
    ) = (
        lax.psum_scatter(table_part, ("gx", "gy"), scatter_dimension=1, tiled=True),
        lax.psum_scatter(
            stacked_member(collected, 0), ("gx", "gy"), scatter_dimension=1, tiled=True
        ),
        lax.psum_scatter(
            stacked_member(collected, 1), ("gx", "gy"), scatter_dimension=1, tiled=True
        ),
        lax.psum_scatter(
            stacked_member(collected, 2), ("gx", "gy"), scatter_dimension=1, tiled=True
        ),
        lax.psum_scatter(
            stacked_member(collected, 3), ("gx", "gy"), scatter_dimension=1, tiled=True
        ),
        lax.psum_scatter(
            stacked_member(collected, 4), ("gx", "gy"), scatter_dimension=1, tiled=True
        ),
        lax.psum_scatter(
            stacked_member(collected, 5), ("gx", "gy"), scatter_dimension=1, tiled=True
        ),
        lax.psum_scatter(
            stacked_member(collected, 6), ("gx", "gy"), scatter_dimension=1, tiled=True
        ),
        lax.psum_scatter(
            stacked_member(collected, 7), ("gx", "gy"), scatter_dimension=1, tiled=True
        ),
        lax.psum_scatter(
            stacked_member(collected, 8), ("gx", "gy"), scatter_dimension=1, tiled=True
        ),
        lax.psum_scatter(
            stacked_member(collected, 9), ("gx", "gy"), scatter_dimension=1, tiled=True
        ),
        lax.psum_scatter(
            stacked_member(collected, 10), ("gx", "gy"), scatter_dimension=1, tiled=True
        ),
    )
    up_stack = stacked_member(collected, 11)
    down_stack = stacked_member(collected, 12)
    up_weight_grad, down_weight_grad = (
        lax.psum_scatter(
            up_stack.astype(jnp.bfloat16), "gx", scatter_dimension=1, tiled=True
        ).astype(jnp.float32),
        lax.psum_scatter(
            down_stack.astype(jnp.bfloat16), "gx", scatter_dimension=2, tiled=True
        ).astype(jnp.float32),
    )
    return (
        state,
        gradient,
        pos_embed_grad,
        norm1_gain_grad,
        norm1_bias_grad,
        query_bias_grad,
        value_bias_grad,
        out_bias_grad,
        norm2_gain_grad,
        norm2_bias_grad,
        up_bias_grad,
        down_bias_grad,
        qkv_weight_grad,
        out_weight_grad,
        up_weight_grad,
        down_weight_grad,
    )


LOG2_E = 1.0 / math.log(2.0)
LANES = 128
BF16 = jnp.bfloat16
F32 = jnp.float32
MESH_ID = pl.DeviceIdType.MESH
VMEM_LIMIT = 60 * 1024 * 1024


def dot_nn(left, right):
    return lax.dot_general(left, right, (((1,), (0,)), ((), ())), preferred_element_type=F32)


def dot_nt(left, right):
    return lax.dot_general(left, right, (((1,), (1,)), ((), ())), preferred_element_type=F32)


def dot_tn(left, right):
    return lax.dot_general(left, right, (((0,), (0,)), ((), ())), preferred_element_type=F32)


def my_place():
    gx = lax.axis_index("gx")
    gy = lax.axis_index("gy")
    return gx // 2, lax.rem(gx, 2), gy // 2, lax.rem(gy, 2)


def device_at(z, x, y, core):
    return (z * 2 + x, y * 2 + core)


def flip_pairs(flip_y, flip_core):
    pairs = []
    for index in range(32):
        gx, gy = divmod(index, 4)
        pairs.append((index, gx * 4 + (gy ^ (2 * flip_y + flip_core))))
    return pairs


def to_partner(value):
    return lax.ppermute(value, ("gx", "gy"), flip_pairs(1, 0))


def to_sibling(value):
    return lax.ppermute(value, ("gx", "gy"), flip_pairs(0, 1))


class Copy:
    def __init__(self, describe):
        self.describe = describe

    def start(self):
        self.describe().start()

    def wait(self):
        self.describe().wait()

    def wait_recv(self):
        self.describe().wait_recv()

    def wait_send(self):
        self.describe().wait_send()


def remote(src, dst, send_sem, recv_sem, device):
    return Copy(
        lambda: pltpu.make_async_remote_copy(
            src_ref=src,
            dst_ref=dst,
            send_sem=send_sem,
            recv_sem=recv_sem,
            device_id=device,
            device_id_type=MESH_ID,
        )
    )


def local_copy(src, dst, sem):
    return Copy(lambda: pltpu.make_async_copy(src, dst, sem))


def block_at(ref, order, z, x, y, *rest):
    place = (z, x, y) if order == "zxy" else (y, z, x)
    return ref.at[(*place, *rest)]


def full_at(ref, order, z, x, y, core, *rest):
    place = (z, x, y, core) if order == "zxy" else (y, core, z, x)
    return ref.at[(*place, *rest)]


def added(left, right):
    return (left.astype(F32) + right.astype(F32)).astype(BF16)


def hbm():
    return pl.BlockSpec(memory_space=pl.ANY)


def vmem():
    return pl.BlockSpec(memory_space=pltpu.VMEM)


def dma_sems(count):
    return pltpu.SemaphoreType.DMA((count,))


class GatherZ:
    space = out_space = pltpu.VMEM

    def __init__(self, shard):
        self.rows, self.columns = shard.shape
        self.outs = [((4, self.rows, self.columns), BF16)]
        self.scratch = [dma_sems(3), dma_sems(3), dma_sems(1)]

    def copies(self, place, refs):
        shard, out, send, recv, local = refs
        z, x, y, core = place
        keep = local_copy(shard, out.at[z], local.at[0])
        return keep, [
            remote(
                shard, out.at[z], send.at[k], recv.at[k], device_at(lax.rem(z + k + 1, 4), x, y, core)
            )
            for k in range(3)
        ]

    def step(self, number, place, refs):
        keep, copies = self.copies(place, refs)
        if number == 0:
            keep.start()
            for copy in copies:
                copy.start()
        else:
            keep.wait()
            for copy in copies:
                copy.wait()


class GatherXY:
    space, out_space = pltpu.VMEM, pl.ANY

    def __init__(self, column, order):
        unused, self.rows, self.columns = column.shape
        self.order = order
        shape = (4, 2, 2, 2) if order == "zxy" else (2, 2, 4, 2)
        self.outs = [((*shape, self.rows, self.columns), BF16)]
        self.scratch = [dma_sems(5), dma_sems(5), dma_sems(1)]

    def copies(self, place, refs):
        column, full, send, recv, local = refs
        z, x, y, core = place
        half = self.rows // 2
        low, high = pl.ds(0, half), pl.ds(half, half)
        every = slice(None)

        def at(*where):
            return full_at(full, self.order, *where)

        def copy(slot, src, dst, device):
            return remote(src, dst, send.at[slot], recv.at[slot], device)

        to_x, to_y = device_at(z, 1 - x, y, core), device_at(z, x, 1 - y, core)
        here = at(every, x, y, core)
        keep = local_copy(column, here, local.at[0])
        first = [
            copy(0, column.at[:, low], at(every, x, y, core, low), to_x),
            copy(1, column.at[:, high], at(every, x, y, core, high), to_y),
        ]
        two_low, two_high = at(every, every, y, core, low), at(every, x, every, core, high)
        second = [copy(2, two_low, two_low, to_y), copy(3, two_high, two_high, to_x)]
        all_here = at(every, every, every, core)
        third = [copy(4, all_here, all_here, device_at(z, x, y, 1 - core))]
        return keep, first, second, third

    def step(self, number, place, refs):
        keep, first, second, third = self.copies(place, refs)
        if number == 0:
            keep.start()
            for copy in first:
                copy.start()
        elif number == 1:
            keep.wait()
            for copy in first:
                copy.wait_recv()
            for copy in second:
                copy.start()
        elif number == 2:
            for copy in second:
                copy.wait_recv()
            for copy in third:
                copy.start()
        else:
            for copy in third:
                copy.wait_recv()
            for copy in first + second + third:
                copy.wait_send()


class SumCore:
    space = out_space = pltpu.VMEM

    def __init__(self, part):
        self.rows, self.columns = part.shape[-2:]
        shape = (4, 2, 2, self.rows, self.columns)
        self.outs = [(shape, BF16)]
        self.scratch = [pltpu.VMEM(shape, BF16), dma_sems(1), dma_sems(1)]

    def step(self, number, place, refs):
        part, out, arrived, send, recv = refs
        z, x, y, core = place
        copy = remote(
            part.at[:, :, :, 1 - core], arrived, send.at[0], recv.at[0], device_at(z, x, y, 1 - core)
        )
        if number == 0:
            copy.start()
        else:
            copy.wait()

            def add_one(i, carry):
                a, b, c = i // 4, lax.rem(i // 2, 2), lax.rem(i, 2)
                out[a, b, c] = added(part[a, b, c, core], arrived[a, b, c])
                return carry

            lax.fori_loop(0, 16, add_one, 0)


class SumXY:
    space = out_space = pltpu.VMEM

    def __init__(self, part, order):
        self.rows, self.columns = part.shape[-2:]
        self.order = order
        half = self.rows // 2
        by_x = (4, 2, half, self.columns)
        by_y = by_x if order == "zxy" else (2, 4, half, self.columns)
        self.outs = [((4, self.rows, self.columns), BF16)]
        self.scratch = [
            pltpu.VMEM(by_x, BF16),
            pltpu.VMEM(by_y, BF16),
            pltpu.VMEM(by_x, BF16),
            pltpu.VMEM(by_y, BF16),
            pltpu.VMEM((2, 4, half, self.columns), BF16),
            dma_sems(4),
            dma_sems(4),
        ]

    def step(self, number, place, refs):
        part, out, in_a, in_b, sum_a, sum_b, third, send, recv = refs
        z, x, y, core = place
        half = self.rows // 2
        low, high = pl.ds(0, half), pl.ds(half, half)
        every = slice(None)
        to_x, to_y = device_at(z, 1 - x, y, core), device_at(z, x, 1 - y, core)

        def at(*where):
            return block_at(part, self.order, *where)

        def by_y(ref, a, b):
            return ref.at[a, b] if self.order == "zxy" else ref.at[b, a]

        def copy(slot, src, dst, device):
            return remote(src, dst, send.at[slot], recv.at[slot], device)

        first = [
            copy(0, at(every, every, 1 - y, low), in_a, to_y),
            copy(1, at(every, 1 - x, every, high), in_b, to_x),
        ]
        second = [
            copy(2, sum_a.at[:, 1 - x], third.at[0], to_x),
            copy(3, by_y(sum_b, every, 1 - y), third.at[1], to_y),
        ]
        if number == 0:
            for one in first:
                one.start()
        elif number == 1:
            for one in first:
                one.wait_recv()

            def add_one(i, carry):
                a, b = i // 2, lax.rem(i, 2)
                sum_a[a, b] = added(at(a, b, y, low)[...], in_a[a, b])
                by_y(sum_b, a, b)[...] = added(at(a, x, b, high)[...], by_y(in_b, a, b)[...])
                return carry

            lax.fori_loop(0, 8, add_one, 0)
            for one in second:
                one.start()
        else:
            for one in second:
                one.wait_recv()

            def add_two(a, carry):
                out[a, low] = added(sum_a[a, x], third[0, a])
                out[a, high] = added(by_y(sum_b, a, y)[...], third[1, a])
                return carry

            lax.fori_loop(0, 4, add_two, 0)
            for one in first + second:
                one.wait_send()


class SumZ:
    space = out_space = pltpu.VMEM

    def __init__(self, part):
        unused, self.rows, self.columns = part.shape
        self.outs = [((self.rows, self.columns), F32)]
        self.scratch = [pltpu.VMEM((3, self.rows, self.columns), BF16), dma_sems(3), dma_sems(3)]

    def step(self, number, place, refs):
        part, out, arrived, send, recv = refs
        z, x, y, core = place
        copies = []
        for k in range(3):
            to_z = lax.rem(z + k + 1, 4)
            copies.append(
                remote(
                    part.at[to_z], arrived.at[k], send.at[k], recv.at[k], device_at(to_z, x, y, core)
                )
            )
        if number == 0:
            for copy in copies:
                copy.start()
        else:
            for copy in copies:
                copy.wait()
            total = part[z].astype(F32)
            for k in range(3):
                total = total + arrived[k].astype(F32)
            out[...] = total


class Carried:
    def __init__(self, *entries):
        self.stages = [entry[0] for entry in entries]
        self.links = [entry[1] if isinstance(entry[1], int) else None for entry in entries]
        self.arrays = [entry[1] for entry in entries if not isinstance(entry[1], int)]
        self.events = [entry[2] for entry in entries]
        self.in_specs = [
            pl.BlockSpec(memory_space=stage.space)
            for stage, link in zip(self.stages, self.links)
            if link is None
        ]
        self.out_shape = [jax.ShapeDtypeStruct(*out) for stage in self.stages for out in stage.outs]
        self.out_specs = [pl.BlockSpec(memory_space=stage.out_space) for stage in self.stages]
        self.scratch = [item for stage in self.stages for item in stage.scratch]

    def run(self, event, place, ins, outs, scratch):
        at, taken = 0, 0
        for index, stage in enumerate(self.stages):
            size = len(stage.scratch)
            if self.links[index] is None:
                source = ins[taken]
                taken += 1
            else:
                source = outs[self.links[index]]
            refs = (source, outs[index], *scratch[at : at + size])
            at += size
            for number, when in enumerate(self.events[index]):
                if when == event:
                    stage.step(number, place, refs)

    def first(self):
        return min((when for events in self.events for when in events), default=None)


def greet_signal(place):
    z, x, y, core = place
    barrier = pltpu.get_barrier_semaphore()
    others = [device_at(lax.rem(z + k, 4), x, y, core) for k in (1, 2, 3)]
    others += [device_at(z, 1 - x, y, core), device_at(z, x, 1 - y, core)]
    others += [device_at(z, x, y, 1 - core)]
    for other in others:
        pl.semaphore_signal(barrier, inc=1, device_id=other, device_id_type=MESH_ID)


def greet_wait():
    pl.semaphore_wait(pltpu.get_barrier_semaphore(), 6)


def comm_kernel(steps, count, ins, *refs):
    total = len(ins)
    named = [entry for entry in ins if not isinstance(entry, int)]
    in_refs = list(refs[: len(named)])
    out_refs = refs[len(named) : len(named) + total]
    scratch = refs[len(named) + total :]
    place = my_place()
    greet_signal(place)
    greet_wait()
    bound, at, taken = [], 0, 0
    for index, stage in enumerate(count):
        if isinstance(ins[index], int):
            source = out_refs[ins[index]]
        else:
            source = in_refs[taken]
            taken += 1
        size = len(stage.scratch)
        bound.append((source, out_refs[index], *scratch[at : at + size]))
        at += size
    for index, number in steps:
        count[index].step(number, place, bound[index])


def run_stages(stages, ins, steps, collective_id, name):
    named = [entry for entry in ins if not isinstance(entry, int)]
    specs = [
        pl.BlockSpec(memory_space=stage.space)
        for stage, entry in zip(stages, ins)
        if not isinstance(entry, int)
    ]
    marks = tuple(entry if isinstance(entry, int) else None for entry in ins)
    return pl.pallas_call(
        functools.partial(comm_kernel, steps, stages, marks),
        out_shape=[jax.ShapeDtypeStruct(*stage.outs[0]) for stage in stages],
        in_specs=specs,
        out_specs=[pl.BlockSpec(memory_space=stage.out_space) for stage in stages],
        scratch_shapes=[item for stage in stages for item in stage.scratch],
        compiler_params=pltpu.CompilerParams(
            collective_id=collective_id, has_side_effects=True, vmem_limit_bytes=VMEM_LIMIT
        ),
        name=name,
    )(*named)


def carrying(
    body, carried, steps, collective_id, name, in_specs, out_specs, out_shape, scratch, flops, args,
    own_greet=False,
):
    n_in, n_out, n_scratch = len(in_specs), len(out_specs), len(scratch)
    carry_in, carry_out = len(carried.in_specs), len(carried.out_specs)
    greets = -1 if own_greet else carried.first()

    def kernel(*refs):
        ins, refs = refs[:n_in], refs[n_in:]
        c_ins, refs = refs[:carry_in], refs[carry_in:]
        outs, refs = refs[:n_out], refs[n_out:]
        c_outs, refs = refs[:carry_out], refs[carry_out:]
        own, c_scratch = refs[:n_scratch], refs[n_scratch:]
        step = pl.program_id(0)
        place = my_place()

        def event(number):
            if greets is not None and number == greets:
                greet_wait()
            carried.run(number, place, c_ins, c_outs, c_scratch)

        if greets is not None:
            pl.when(step == 0)(lambda: greet_signal(place))
        numbers = sorted({when for events in carried.events for when in events})
        if 0 in numbers:
            pl.when(step == 0)(functools.partial(event, 0))
        body(step, place, *ins, *outs, *own)
        for number in numbers:
            if number > 0:
                pl.when(step == number - 1)(functools.partial(event, number))

    params = {"vmem_limit_bytes": VMEM_LIMIT}
    if greets is not None:
        params.update(collective_id=collective_id, has_side_effects=True)
    results = pl.pallas_call(
        kernel,
        grid=(steps,),
        out_shape=[*out_shape, *carried.out_shape],
        in_specs=[*in_specs, *carried.in_specs],
        out_specs=[*out_specs, *carried.out_specs],
        scratch_shapes=[*scratch, *carried.scratch],
        compiler_params=pltpu.CompilerParams(**params),
        cost_estimate=pl.CostEstimate(flops=flops, bytes_accessed=flops // 300, transcendentals=0),
        name=name,
    )(*args, *carried.arrays)
    return results[:n_out], results[n_out:]


def lane_marks(head):
    lane = lax.broadcasted_iota(jnp.int32, (1, LANES), 1)
    own = (lane // HEAD_DIM == head).astype(F32)
    spare = HEAD_DIM * (1 - head)
    return lane, own, spare


def split_three(column):
    high = column.astype(BF16).astype(F32)
    rest = column - high
    middle = rest.astype(BF16).astype(F32)
    return high, middle, rest - middle


def attention_body(block, pair, place, q_ref, ko_ref, ks_ref, vo_ref, vs_ref, bias_ref, out_ref, exact_ref, lse_ref, keys, values):
    rows = q_ref.shape[0]
    values[0:rows] = vo_ref[...]
    values[rows:] = vs_ref[...]
    lanes = lax.broadcasted_iota(jnp.int32, (1, LANES), 1)

    @pl.when(pair == 0)
    def _():
        lse_ref[...] = jnp.zeros_like(lse_ref)

    mixed = [[], []]
    totals = [[], []]
    for head in range(2):
        lane, own, spare = lane_marks(head)
        own16 = own.astype(BF16)
        at_spare = (lane == spare).astype(BF16)
        keys[0:rows] = ko_ref[...] * own16 + bias_ref[0:rows] * at_spare
        keys[rows:] = ks_ref[...] * own16 + bias_ref[rows:] * at_spare
        for start in range(0, rows, block):
            query = q_ref[start : start + block] * own16 + at_spare
            scores = dot_nt(query, keys[...])
            top = jnp.max(scores, axis=-1, keepdims=True)
            weights = jnp.exp2(scores - top)
            total = jnp.sum(weights, axis=-1, keepdims=True)
            summed = dot_nn(weights.astype(BF16), values[...])
            mixed[head].append(summed * (1.0 / total))
            totals[head].append(top + jnp.log2(total))
    for index, start in enumerate(range(0, rows, block)):
        rows_at = slice(start, start + block)
        both = jnp.where(lanes < HEAD_DIM, mixed[0][index], mixed[1][index])
        out_ref[rows_at] = both.astype(BF16)
        exact_ref[rows_at] = both
        held = lse_ref[rows_at]
        held = jnp.where(lanes == 2 * pair, totals[0][index], held)
        lse_ref[rows_at] = jnp.where(lanes == 2 * pair + 1, totals[1][index], held)


def attention_forward(queries, keys_own, keys_sib, values_own, values_sib, bias, carried, collective_id):
    rows, width = queries.shape
    column = pl.BlockSpec((rows, LANES), lambda pair: (0, pair))
    return carrying(
        functools.partial(attention_body, rows // 2),
        carried,
        width // LANES,
        collective_id,
        "attention_forward",
        [column] * 5 + [pl.BlockSpec((2 * rows, LANES), lambda pair: (0, 0))],
        [column, column, pl.BlockSpec((rows, LANES), lambda pair: (0, 0))],
        [
            jax.ShapeDtypeStruct((rows, width), BF16),
            jax.ShapeDtypeStruct((rows, width), F32),
            jax.ShapeDtypeStruct((rows, LANES), F32),
        ],
        [pltpu.VMEM((2 * rows, LANES), BF16), pltpu.VMEM((2 * rows, LANES), BF16)],
        8 * rows * 2 * rows * width,
        (queries, keys_own, keys_sib, values_own, values_sib, bias),
    )


def attention_back_body(
    pair, place, q_ref, ko_ref, ks_ref, vo_ref, vs_ref, do_ref, mix_ref, lse_ref, bias_ref,
    dq_ref, dko_ref, dks_ref, dvo_ref, dvs_ref,
):
    rows = q_ref.shape[0]
    block = rows // 2
    lanes = lax.broadcasted_iota(jnp.int32, (1, LANES), 1)
    query = q_ref[...]
    grad = do_ref[...]
    product = grad.astype(F32) * mix_ref[...]
    heads = []
    for head in range(2):
        lane, own, spare = lane_marks(head)
        own16 = own.astype(BF16)
        lse = jnp.sum(jnp.where(lanes == 2 * pair + head, lse_ref[...], 0.0), axis=-1, keepdims=True)
        inner = jnp.sum(product * own, axis=-1, keepdims=True)
        lse_parts, inner_parts = split_three(-lse), split_three(-inner)
        query_own = query * own16
        grad_own = grad * own16
        query_aug = jnp.where(lane == spare, 1.0, 0.0)
        grad_aug = jnp.zeros((1, LANES), F32)
        for k in range(3):
            query_aug = jnp.where(lane == spare + 1 + k, lse_parts[k], query_aug)
            grad_aug = jnp.where(lane == spare + 1 + k, inner_parts[k], grad_aug)
        query_aug = query_own + query_aug.astype(BF16)
        grad_aug = grad_own + grad_aug.astype(BF16)
        at_spare = (lane == spare).astype(BF16)
        ones = ((lane > spare) & (lane < spare + 4)).astype(BF16)
        heads.append((own16, at_spare, ones, query_own, grad_own, query_aug, grad_aug))
    query_grad = jnp.zeros((LANES, rows), F32)
    for side, (k_ref, v_ref, dk_ref, dv_ref) in enumerate(
        ((ko_ref, vo_ref, dko_ref, dvo_ref), (ks_ref, vs_ref, dks_ref, dvs_ref))
    ):
        for start in range(0, rows, block):
            at = slice(start, start + block)
            key, value = k_ref[at], v_ref[at]
            shift = bias_ref[side * rows + start : side * rows + start + block]
            key_grad = jnp.zeros((block, LANES), F32)
            value_grad = jnp.zeros((block, LANES), F32)
            for own16, at_spare, ones, query_own, grad_own, query_aug, grad_aug in heads:
                key_own = key * own16
                weights = jnp.exp2(dot_nt(key_own + shift * at_spare + ones, query_aug))
                weight_grad = dot_nt(value * own16 + ones, grad_aug)
                score_grad = (weights * weight_grad).astype(BF16)
                value_grad = value_grad + dot_nn(weights.astype(BF16), grad_own)
                key_grad = key_grad + dot_nn(score_grad, query_own)
                query_grad = query_grad + dot_tn(key_own, score_grad)
            dk_ref[at] = (key_grad * (1.0 / LOG2_E)).astype(BF16)
            dv_ref[at] = value_grad.astype(BF16)
    dq_ref[...] = (jnp.transpose(query_grad) * HEAD_DIM ** (-0.5)).astype(BF16)


def attention_backward(
    queries, keys_own, keys_sib, values_own, values_sib, mixed_grad, mixed, lse, bias, carried, collective_id
):
    rows, width = queries.shape
    column = pl.BlockSpec((rows, LANES), lambda pair: (0, pair))
    fixed = pl.BlockSpec((rows, LANES), lambda pair: (0, 0))
    return carrying(
        attention_back_body,
        carried,
        width // LANES,
        collective_id,
        "attention_backward",
        [column] * 7 + [fixed, pl.BlockSpec((2 * rows, LANES), lambda pair: (0, 0))],
        [column] * 5,
        [jax.ShapeDtypeStruct((rows, width), BF16)] * 5,
        [],
        20 * rows * 2 * rows * width,
        (queries, keys_own, keys_sib, values_own, values_sib, mixed_grad, mixed, lse, bias),
    )


def norm_parts(values):
    row_mean = jnp.mean(values, axis=-1, keepdims=True)
    centred = values - row_mean
    row_var = jnp.mean(centred * centred, axis=-1, keepdims=True)
    rstd = lax.rsqrt(row_var + EPSILON)
    return centred * rstd, rstd


def norm_back(values, gain, grad):
    normed, rstd = norm_parts(values)
    scaled = grad * gain
    first = jnp.mean(scaled, axis=-1, keepdims=True)
    second = jnp.mean(scaled * normed, axis=-1, keepdims=True)
    back = (scaled - first - normed * second) * rstd
    return back, jnp.sum(grad * normed, axis=0, keepdims=True), jnp.sum(grad, axis=0, keepdims=True)


def feed_forward_body(
    step, place, mid_ref, gain_ref, shift_ref, up_bias_ref, down_bias_ref, weight_ref,
    out_ref, hidden_ref, slope_ref, act_ref, total_ref,
):
    rows, features = mid_ref.shape
    half = rows // 2
    up_rows = weight_ref.shape[4] // 2
    halves = [slice(0, half), slice(half, rows)]

    @pl.when(step == 0)
    def _():
        for at in halves:
            values = mid_ref[at]
            normed, unused = norm_parts(values)
            act_ref[at] = (normed * gain_ref[...] + shift_ref[...]).astype(BF16)
            total_ref[at] = values + down_bias_ref[...]

    weight_up = weight_ref[0, 0, :, :, 0:up_rows, :].reshape(features, features)
    weight_down = weight_ref[0, 0, :, :, up_rows:, :].reshape(features, features)
    for at in halves:
        pre_act = dot_nn(act_ref[at], weight_up) + up_bias_ref[0]
        below = 0.5 * (1.0 + lax.erf(pre_act * SQRT_HALF))
        hidden = (pre_act * below).astype(BF16)
        hidden_ref[at] = hidden
        slope = below + pre_act * jnp.exp(-0.5 * pre_act * pre_act) * NORMAL_PEAK
        slope_ref[at] = slope.astype(BF16)
        total_ref[at] += dot_nt(hidden, weight_down)

    @pl.when(step == pl.num_programs(0) - 1)
    def _():
        out_ref[...] = total_ref[...]


def whole(shape):
    return pl.BlockSpec(shape, lambda step: (0,) * len(shape), pipeline_mode=pl.Buffered(1))


def feed_forward(middle, gain, shift, up_bias, down_bias, weights, carried, collective_id):
    rows, features = middle.shape
    blocks = weights.shape[0] * weights.shape[1]
    column = pl.BlockSpec((rows, features), lambda step: (0, step))
    line = whole((1, features))
    return carrying(
        feed_forward_body,
        carried,
        blocks,
        collective_id,
        "feed_forward",
        [
            whole((rows, features)),
            line,
            line,
            pl.BlockSpec((1, 1, features), lambda step: (step, 0, 0)),
            line,
            pl.BlockSpec((1, 1) + weights.shape[2:], lambda step: (step // 2, lax.rem(step, 2), 0, 0, 0, 0)),
        ],
        [whole((rows, features)), column, column],
        [
            jax.ShapeDtypeStruct((rows, features), F32),
            jax.ShapeDtypeStruct((rows, blocks * features), BF16),
            jax.ShapeDtypeStruct((rows, blocks * features), BF16),
        ],
        [pltpu.VMEM((rows, features), BF16), pltpu.VMEM((rows, features), F32)],
        4 * rows * features * features * blocks,
        (middle, gain, shift, up_bias, down_bias, weights),
    )


def feed_forward_back_body(
    step, place, grad_ref, mid_ref, gain_ref, shift_ref, hidden_ref, slope_ref, weight_ref,
    out_ref, line_ref, up_bias_ref, part_ref,
    grad16_ref, act_t_ref, grad_t_ref, pre_grad_ref, total_ref, sent_ref, arrived_ref, send, recv,
):
    z, x, y, core = place
    rows, features = mid_ref.shape
    half = rows // 2
    up_rows = weight_ref.shape[4] // 2
    halves = [slice(0, half), slice(half, rows)]
    to_core = device_at(z, x, y, 1 - core)

    def to_sibling_core(block):
        return remote(sent_ref.at[block], arrived_ref.at[block], send.at[block], recv.at[block], to_core)

    @pl.when(step == 0)
    def _():
        normed, unused = norm_parts(mid_ref[...])
        act_t_ref[...] = jnp.transpose(normed * gain_ref[...] + shift_ref[...]).astype(BF16)
        grad16_ref[...] = grad_ref[...].astype(BF16)
        grad_t_ref[...] = jnp.transpose(grad_ref[...]).astype(BF16)
        total_ref[...] = jnp.zeros_like(total_ref)

    weight_up = weight_ref[0, 0, :, :, 0:up_rows, :].reshape(features, features)
    weight_down = weight_ref[0, 0, :, :, up_rows:, :].reshape(features, features)
    lines = jnp.zeros((1, features), F32)
    for at in halves:
        hidden_grad = dot_nn(grad16_ref[at], weight_down)
        pre_grad = (hidden_grad * slope_ref[0, at].astype(F32)).astype(BF16)
        pre_grad_ref[at] = pre_grad
        lines = lines + jnp.sum(pre_grad.astype(F32), axis=0, keepdims=True)
        total_ref[at] += dot_nt(pre_grad, weight_up)
    up_bias_ref[0] = lines

    def parts(store):
        deep = 2 * up_rows
        for a in range(4):
            at = slice(a * deep, (a + 1) * deep)
            store(a, slice(0, up_rows), dot_nn(act_t_ref[at], pre_grad_ref[...]))
            store(a, slice(up_rows, deep), dot_nn(grad_t_ref[at], hidden_ref[0]))

    @pl.when(step < 2)
    def _():
        def store(a, at, value):
            sent_ref[step, a, :, at, :] = value.reshape(2, up_rows, features).astype(BF16)

        parts(store)
        pl.when(step == 0)(greet_wait)
        to_sibling_core(step).start()

    @pl.when(step >= 2)
    def _():
        block = step - 2
        to_sibling_core(block).wait_recv()

        def store(a, at, value):
            other = arrived_ref[block, a, :, at, :].astype(F32)
            part_ref[block, a, :, at, :] = (value.reshape(2, up_rows, features) + other).astype(BF16)

        parts(store)

    @pl.when(step == 3)
    def _():
        gain_sum = jnp.zeros((1, features), F32)
        shift_sum = jnp.zeros((1, features), F32)
        down_sum = jnp.zeros((1, features), F32)
        for at in halves:
            back, gain_part, shift_part = norm_back(mid_ref[at], gain_ref[...], total_ref[at])
            out_ref[at] = grad_ref[at] + back
            gain_sum, shift_sum = gain_sum + gain_part, shift_sum + shift_part
            down_sum = down_sum + jnp.sum(grad16_ref[at].astype(F32), axis=0, keepdims=True)
        line_ref[0:1] = gain_sum
        line_ref[1:2] = shift_sum
        line_ref[2:3] = down_sum
        for block in range(2):
            to_sibling_core(block).wait_send()


def feed_forward_backward(grad, middle, gain, shift, hidden, slope, weights, carried, collective_id):
    rows, features = middle.shape
    blocks = weights.shape[0] * weights.shape[1]
    deep = weights.shape[4]
    line = whole((1, features))

    def block_of(step):
        core = lax.rem(lax.axis_index("gy"), 2)
        return lax.rem(step, 2), jnp.where(step < 2, 1 - core, core)

    def column_of(step):
        y, core = block_of(step)
        return 0, y * 2 + core

    def weight_of(step):
        y, core = block_of(step)
        return y, core, 0, 0, 0, 0

    column = pl.BlockSpec((1, rows, features), lambda step: (column_of(step)[1], 0, 0))
    pair = (2, 4, 2, deep, features)
    return carrying(
        feed_forward_back_body,
        carried,
        blocks,
        collective_id,
        "feed_forward_backward",
        [
            whole((rows, features)),
            whole((rows, features)),
            line,
            line,
            column,
            column,
            pl.BlockSpec((1, 1) + weights.shape[2:], weight_of),
        ],
        [
            whole((rows, features)),
            whole((8, features)),
            pl.BlockSpec((1, 1, features), lambda step: (column_of(step)[1], 0, 0)),
            whole(pair),
        ],
        [
            jax.ShapeDtypeStruct((rows, features), F32),
            jax.ShapeDtypeStruct((8, features), F32),
            jax.ShapeDtypeStruct((blocks, 1, features), F32),
            jax.ShapeDtypeStruct(pair, BF16),
        ],
        [
            pltpu.VMEM((rows, features), BF16),
            pltpu.VMEM((features, rows), BF16),
            pltpu.VMEM((features, rows), BF16),
            pltpu.VMEM((rows, features), BF16),
            pltpu.VMEM((rows, features), F32),
            pltpu.VMEM(pair, BF16),
            pltpu.VMEM(pair, BF16),
            dma_sems(2),
            dma_sems(2),
        ],
        8 * rows * features * features * blocks,
        (grad, middle, gain, shift, hidden, slope, weights),
        own_greet=True,
    )


class Gather:
    def __init__(self, place, shard, full, order, start, rows, send, recv, local):
        z, x, y, core = place
        half = rows // 2
        every = slice(None)
        both, low, high = pl.ds(start, rows), pl.ds(start, half), pl.ds(start + half, half)

        def at(*where):
            return full_at(full, order, *where)

        def copy(slot, src, dst, device):
            return remote(src, dst, send.at[slot], recv.at[slot], device)

        def same(slot, ref, device):
            return copy(slot, ref, ref, device)

        to_x, to_y = device_at(z, 1 - x, y, core), device_at(z, x, 1 - y, core)
        own = at(z, x, y, core, both)
        self.keep = local_copy(shard.at[both], own, local)
        self.along_z = [
            copy(k, shard.at[both], own, device_at(lax.rem(z + k + 1, 4), x, y, core)) for k in range(3)
        ]
        self.first = [
            same(3, at(every, x, y, core, low), to_x),
            same(4, at(every, x, y, core, high), to_y),
        ]
        self.second = [
            same(5, at(every, every, y, core, low), to_y),
            same(6, at(every, x, every, core, high), to_x),
        ]
        self.third = [same(7, at(every, every, every, core, both), device_at(z, x, y, 1 - core))]

    def start_z(self):
        self.keep.start()
        for copy in self.along_z:
            copy.start()

    def start_first(self):
        self.keep.wait()
        for copy in self.along_z:
            copy.wait_recv()
        for copy in self.first:
            copy.start()

    def start_second(self):
        for copy in self.first:
            copy.wait_recv()
        for copy in self.second:
            copy.start()

    def start_third(self):
        for copy in self.second:
            copy.wait_recv()
        for copy in self.third:
            copy.start()

    def finish(self):
        for copy in self.third:
            copy.wait_recv()

    def drain(self):
        for copy in self.along_z + self.first + self.second + self.third:
            copy.wait_send()


class GatherChain:
    def __init__(self, gathers):
        self.gathers = gathers

    def begin(self):
        for gather in self.gathers[:2]:
            gather.start_z()

    def follow(self):
        for index in range(2):
            self.gathers[index].start_first()
            self.gathers[index + 2].start_z()
        self.gathers[0].start_second()

    def turn(self, index):
        count = len(self.gathers)
        self.gathers[index].start_third()
        if index + 1 < count:
            self.gathers[index + 1].start_second()
        if index + 2 < count:
            self.gathers[index + 2].start_first()
        if index + 4 < count:
            self.gathers[index + 4].start_z()

    def finish(self, index):
        self.gathers[index].finish()

    def drain(self):
        for gather in self.gathers:
            gather.drain()


def spread_matrix(width, columns):
    row = lax.broadcasted_iota(jnp.int32, (LANES, columns), 0)
    lane = lax.broadcasted_iota(jnp.int32, (LANES, columns), 1)
    return (row == lax.rem(lane, width)).astype(F32).astype(BF16)


def forward_kernel(sizes, *refs):
    layers, count, owned, up_rows = sizes
    (choose, patches, cotangent, pos_kept, pos_sent, bias, table_shard), refs = refs[:7], refs[7:]
    attn_shards, refs = refs[:layers], refs[layers:]
    mlp_shards, refs = refs[:layers], refs[layers:]
    (final, chip_cot, pos_back, narrow, up_bias), refs = refs[:5], refs[5:]
    mlp_fulls, refs = refs[:layers], refs[layers:]
    kept, refs = refs[: 12 * layers], refs[12 * layers :]
    (
        table_full, attn_full, table, weights, mlp_block, sorted_rows, arrived_rows, middle, act, query,
        key, value, key_sib, value_sib, exact, mixed, lse, hidden, slope, keys, values,
        send, recv, local, swap_send, swap_recv, save_sem, load_sem,
    ) = refs
    state = final
    place = my_place()
    z, x, y, core = place
    rows, features = state.shape
    slots = rows // 2
    halves = [slice(0, slots), slice(slots, rows)]
    blocks = mlp_fulls[0].shape[0] * mlp_fulls[0].shape[1]
    to_y, to_core = device_at(z, x, 1 - y, core), device_at(z, x, y, 1 - core)
    score_scale = HEAD_DIM ** (-0.5) * LOG2_E

    def gather(slot, shard, full, order, start, size):
        return Gather(
            place, shard, full, order, start, size, send.at[slot], recv.at[slot], local.at[slot]
        )

    gathers = [gather(0, table_shard, table_full, "zxy", 0, table_shard.shape[0])]
    for layer in range(layers):
        slot = 1 + 3 * layer
        gathers.append(gather(slot, attn_shards[layer], attn_full.at[layer], "zxy", 0, 4 * owned))
        for part in range(2):
            gathers.append(
                gather(
                    slot + 1 + part, mlp_shards[layer], mlp_fulls[layer], "yzx", part * up_rows, up_rows
                )
            )
    chain = GatherChain(gathers)

    def swap(slot, src, dst, device):
        return remote(src, dst, swap_send.at[slot], swap_recv.at[slot], device)

    greet_signal(place)
    greet_wait()
    chain.begin()
    send_pos = swap(0, pos_sent, pos_back, to_y)
    send_pos.start()
    sorted_rows[...] = dot_nn(choose[...], patches[...]).astype(BF16)
    send_rows = swap(1, sorted_rows.at[halves[1]], arrived_rows, to_y)
    send_rows.start()
    chain.follow()
    chip_cot[halves[0]] = dot_nn(choose[halves[0]], cotangent[...]).astype(BF16)
    chain.turn(0)
    send_pos.wait()
    send_rows.wait()
    chain.finish(0)

    devices = 32
    for a in range(4):
        block = table_full[a].reshape(8, owned + 8, table.shape[1]).astype(F32)
        table[a * 8 * owned : (a + 1) * 8 * owned] = (
            block[:, :owned].reshape(8 * owned, table.shape[1]).astype(BF16)
        )
    lane = lax.broadcasted_iota(jnp.int32, (devices, 1, features), 2)
    device = lax.broadcasted_iota(jnp.int32, (devices, 1, features), 0)
    for b in range(3):
        width = owned if b < 2 else 4 * owned
        packed = table_full[:, :, :, :, owned:, b * LANES : (b + 1) * LANES]
        packed = packed.reshape(devices * 8, LANES)
        wide = dot_nn(packed, spread_matrix(width, features)).reshape(devices, 8, features)
        if b < 2:
            wide = jnp.where(lane // owned == device, wide, 0.0)
            narrow[8 * b : 8 * b + 8] = jnp.sum(wide, axis=0)
        else:
            wide = jnp.where(lane // width == lax.rem(device, 8), wide, 0.0)
            up_bias[...] = jnp.sum(wide.reshape(4, 8, 8, features), axis=1)

    position = lax.broadcasted_iota(jnp.int32, (slots, table.shape[1]), 1).astype(F32)
    for at, pos, row_ref in ((halves[0], pos_kept, sorted_rows), (halves[1], pos_back, arrived_rows)):
        column = jnp.transpose(jnp.broadcast_to(pos[0:1, 0:slots], (LANES, slots)))[:, 0:1]
        lookup = (position == column).astype(F32).astype(BF16)
        state[at] = row_ref[0:slots].astype(F32) + dot_nt(lookup, table[...])

    def save(layer, index, ref):
        return local_copy(ref, kept[12 * layer + index], save_sem.at[index])

    def save_block(layer, index, block):
        ref = (hidden, slope)[index - 10].at[lax.rem(block, 2)]
        return local_copy(ref, kept[12 * layer + index].at[block], save_sem.at[index + 2 * lax.rem(block, 2)])

    def load_block(layer, block):
        slot = lax.rem(block, 2)
        return local_copy(
            mlp_fulls[layer].at[block // 2, lax.rem(block, 2)], mlp_block.at[slot], load_sem.at[slot]
        )

    def attend_pair(pair, layer):
        at_lanes = pl.ds(pl.multiple_of(pair * LANES, LANES), LANES)
        values[halves[0]] = value[halves[0], at_lanes]
        values[halves[1]] = value[halves[1], at_lanes]
        values[rows : rows + slots] = value_sib[layer, halves[0], at_lanes]
        values[rows + slots :] = value_sib[layer, halves[1], at_lanes]
        lanes = lax.broadcasted_iota(jnp.int32, (1, LANES), 1)
        results = [[], []]
        totals = [[], []]
        for head in range(2):
            lane, own, spare = lane_marks(head)
            own16 = own.astype(BF16)
            at_spare = (lane == spare).astype(BF16)
            keys[0:rows] = key[:, at_lanes] * own16 + bias[0:rows] * at_spare
            keys[rows:] = key_sib[layer, :, at_lanes] * own16 + bias[rows:] * at_spare
            for at in halves:
                scores = dot_nt(query[at, at_lanes] * own16 + at_spare, keys[...])
                top = jnp.max(scores, axis=-1, keepdims=True)
                weight = jnp.exp2(scores - top)
                total = jnp.sum(weight, axis=-1, keepdims=True)
                results[head].append(dot_nn(weight.astype(BF16), values[...]) * (1.0 / total))
                totals[head].append(top + jnp.log2(total))
        for index, at in enumerate(halves):
            both = jnp.where(lanes < HEAD_DIM, results[0][index], results[1][index])
            mixed[at, at_lanes] = both.astype(BF16)
            exact[at, at_lanes] = both
            held = lse[at]
            held = jnp.where(lanes == 2 * pair, totals[0][index], held)
            lse[at] = jnp.where(lanes == 2 * pair + 1, totals[1][index], held)

    def saved_refs(layer):
        return (query, key, value, key_sib.at[layer], value_sib.at[layer], exact)

    lse[...] = jnp.zeros_like(lse)
    for layer in range(layers):
        after = layer > 0
        base = count * layer

        def line(index):
            return narrow[base + index : base + index + 1]

        save(layer, 0, state).start()
        for at in halves:
            normed, unused = norm_parts(state[at])
            act[at] = (normed * line(0) + line(1)).astype(BF16)
        if not after:
            chain.turn(1)
        chain.finish(1 + 3 * layer)
        if after:
            save(layer - 1, 1, weights).wait()
        for a in range(4):
            block = attn_full[layer, a].reshape(8, 4 * owned, features).astype(F32)
            for index in range(4):
                part = block[:, index * owned : (index + 1) * owned].reshape(8 * owned, features)
                weights[index, a * 8 * owned : (a + 1) * 8 * owned] = part.astype(BF16)
        save(layer, 1, weights).start()
        if after:
            for index in range(2, 8):
                save(layer - 1, index, saved_refs(layer - 1)[index - 2]).wait()
            save(layer - 1, 8, lse).wait()
        for at in halves:
            key[at] = dot_nn(act[at], weights[1]).astype(BF16)
        swap(2 + 2 * layer, key, key_sib.at[layer], to_core).start()
        for at in halves:
            value[at] = (dot_nn(act[at], weights[2]) + line(3)).astype(BF16)
        swap(3 + 2 * layer, value, value_sib.at[layer], to_core).start()
        for at in halves:
            query[at] = ((dot_nn(act[at], weights[0]) + line(2)) * score_scale).astype(BF16)
        swap(2 + 2 * layer, key, key_sib.at[layer], to_core).wait()
        swap(3 + 2 * layer, value, value_sib.at[layer], to_core).wait()

        def one_pair(pair, carry, layer=layer):
            attend_pair(pair, layer)
            when = 2 if layer == 0 else 0
            pl.when(pair == when)(lambda: chain.turn(2 + 3 * layer))
            return carry

        lax.fori_loop(0, features // LANES, one_pair, 0)
        for index in range(2, 8):
            save(layer, index, saved_refs(layer)[index - 2]).start()
        save(layer, 8, lse).start()
        if after:
            save(layer - 1, 9, middle).wait()
        for at in halves:
            total = state[at] + dot_nn(mixed[at], weights[3]) + line(4)
            middle[at] = total
            normed, unused = norm_parts(total)
            act[at] = (normed * line(5) + line(6)).astype(BF16)
        save(layer, 9, middle).start()
        save(layer, 0, state).wait()
        for at in halves:
            state[at] = middle[at] + line(7)
        chain.turn(3 + 3 * layer)
        chain.finish(2 + 3 * layer)
        chain.finish(3 + 3 * layer)
        load_block(layer, 0).start()
        if layer == layers - 1:
            sorted_back = swap(2 + 2 * layers, sorted_rows.at[halves[1]], chip_cot.at[halves[1]], to_y)
            sorted_rows[halves[1]] = dot_nn(choose[halves[1]], cotangent[...]).astype(BF16)
            sorted_back.start()

        def one_block(block, carry, layer=layer):
            slot = lax.rem(block, 2)
            pl.when(block + 1 < blocks)(lambda: load_block(layer, block + 1).start())
            load_block(layer, block).wait()

            @pl.when(block >= 2)
            def _():
                save_block(layer, 10, block - 2).wait()
                save_block(layer, 11, block - 2).wait()

            weight_up = mlp_block[slot, :, :, 0:up_rows, :].reshape(features, features)
            weight_down = mlp_block[slot, :, :, up_rows:, :].reshape(features, features)
            shift = up_bias[block, layer : layer + 1]
            for at in halves:
                pre_act = dot_nn(act[at], weight_up) + shift
                below = 0.5 * (1.0 + lax.erf(pre_act * SQRT_HALF))
                hidden_part = (pre_act * below).astype(BF16)
                hidden[slot, at] = hidden_part
                bend = below + pre_act * jnp.exp(-0.5 * pre_act * pre_act) * NORMAL_PEAK
                slope[slot, at] = bend.astype(BF16)
                state[at] += dot_nt(hidden_part, weight_down)
            save_block(layer, 10, block).start()
            save_block(layer, 11, block).start()
            return carry

        lax.fori_loop(0, blocks, one_block, 0)
        for block in (blocks - 2, blocks - 1):
            save_block(layer, 10, block).wait()
            save_block(layer, 11, block).wait()
        if layer < layers - 1:
            chain.turn(4 + 3 * layer)
    last = layers - 1
    swap(2 + 2 * layers, sorted_rows.at[halves[1]], chip_cot.at[halves[1]], to_y).wait()
    save(last, 1, weights).wait()
    for index in range(2, 8):
        save(last, index, saved_refs(last)[index - 2]).wait()
    save(last, 8, lse).wait()
    save(last, 9, middle).wait()
    chain.drain()


def forward(choose, patches, cotangent, pos_kept, pos_sent, bias, table_shard, attn_shards, mlp_shards, count, owned, collective_id):
    layers = len(attn_shards)
    rows, features = choose.shape[0], patches.shape[1]
    deep = mlp_shards[0].shape[0]
    blocks = 4
    wide = (rows, features)

    def like(shape, dtype):
        return jax.ShapeDtypeStruct(shape, dtype)

    saved = [
        like(wide, F32), like((4, features, features), BF16), *[like(wide, BF16)] * 5, like(wide, F32),
        like((rows, LANES), F32), like(wide, F32), *[like((blocks,) + wide, BF16)] * 2,
    ]
    out_shape = [
        like(wide, F32), like(wide, BF16), like(pos_sent.shape, F32), like((layers * count, features), F32),
        like((blocks, 8, features), F32),
        *[like((2, 2, 4, 2, deep, features), BF16)] * layers,
        *(saved * layers),
    ]
    groups = 1 + 3 * layers
    half16 = pltpu.VMEM((rows // 2, features), BF16)
    wide16, wide32 = pltpu.VMEM(wide, BF16), pltpu.VMEM(wide, F32)
    each16 = pltpu.VMEM((layers,) + wide, BF16)
    scratch = [
        pltpu.VMEM((4, 2, 2, 2) + table_shard.shape, BF16),
        pltpu.VMEM((layers, 4, 2, 2, 2, 4 * owned, features), BF16),
        pltpu.VMEM((features, table_shard.shape[1]), BF16),
        pltpu.VMEM((4, features, features), BF16),
        pltpu.VMEM((2, 4, 2, deep, features), BF16),
        wide16, half16, wide32, wide16, wide16, wide16, wide16, each16, each16, wide32, wide16,
        pltpu.VMEM((rows, LANES), F32),
        pltpu.VMEM((2,) + wide, BF16),
        pltpu.VMEM((2,) + wide, BF16),
        pltpu.VMEM((2 * rows, LANES), BF16),
        pltpu.VMEM((2 * rows, LANES), BF16),
        pltpu.SemaphoreType.DMA((groups, 8)),
        pltpu.SemaphoreType.DMA((groups, 8)),
        dma_sems(groups),
        dma_sems(3 + 2 * layers),
        dma_sems(3 + 2 * layers),
        dma_sems(14),
        dma_sems(2),
    ]
    args = (choose, patches, cotangent, pos_kept, pos_sent, bias, table_shard, *attn_shards, *mlp_shards)
    results = pl.pallas_call(
        functools.partial(forward_kernel, (layers, count, owned, deep // 2)),
        out_shape=out_shape,
        in_specs=[vmem()] * len(args),
        out_specs=[vmem()] * 5 + [hbm()] * (len(out_shape) - 5),
        scratch_shapes=scratch,
        compiler_params=pltpu.CompilerParams(
            collective_id=collective_id, has_side_effects=True, vmem_limit_bytes=VMEM_LIMIT
        ),
        name="forward",
    )(*args)
    mlp_fulls = results[5 : 5 + layers]
    kept = results[5 + layers :]
    return results[:5], mlp_fulls, [kept[12 * i : 12 * i + 12] for i in range(layers)]


def split_rows(values):
    high = values.astype(BF16)
    rest = values - high.astype(F32)
    middle = rest.astype(BF16)
    return high, middle, (rest - middle.astype(F32)).astype(BF16)


def chip_shards(
    patches,
    clip_of_row,
    position_of_row,
    pos_embed,
    norm1_gain,
    norm1_bias,
    query_bias,
    value_bias,
    out_bias,
    norm2_gain,
    norm2_bias,
    up_bias,
    down_bias,
    qkv_weight,
    out_weight,
    up_weight,
    down_weight,
    cotangent,
):
    layers, owned, features = qkv_weight.shape[0], qkv_weight.shape[1], patches.shape[1]
    pieces = lax.axis_size("gy")
    piece_rows = patches.shape[0]
    devices = features // owned
    positions = pos_embed.shape[0]
    padded_positions = -(-positions // 256) * 256
    slots = -(-positions // pieces)
    slots = -(-slots // 16) * 16
    rows = 2 * slots
    hidden_width = up_weight.shape[2]
    up_rows = up_weight.shape[1]
    gy = lax.axis_index("gy")
    side, core = gy // 2, lax.rem(gy, 2)

    low_clip, high_clip = jnp.min(clip_of_row), jnp.max(clip_of_row)
    low_is_long = 2 * jnp.sum((clip_of_row == low_clip).astype(jnp.int32)) > clip_of_row.shape[0]
    long_clip = jnp.where(low_is_long, low_clip, high_clip)
    kept_all = ((clip_of_row == long_clip) == (side == 0)).reshape(pieces, piece_rows)
    kept_count = jnp.sum(kept_all.astype(jnp.int32), axis=1)
    kept = lax.dynamic_index_in_dim(kept_all, gy, 0, keepdims=False)
    rank_kept = jnp.cumsum(kept.astype(jnp.int32)) - 1
    rank_sent = jnp.arange(piece_rows, dtype=jnp.int32) - rank_kept - 1
    slot = jnp.arange(slots, dtype=jnp.int32)[:, None]
    pick_kept = (slot == rank_kept[None]) & kept[None]
    pick_sent = (slot == rank_sent[None]) & jnp.logical_not(kept)[None]
    choose = jnp.concatenate([pick_kept, pick_sent], axis=0)
    choose16 = choose.astype(BF16)
    sorted_positions = jnp.sum(jnp.where(choose, position_of_row[None], 0), axis=1).astype(F32)
    pos_kept, pos_sent = (
        jnp.broadcast_to(jnp.pad(part, (0, -slots % LANES))[None], (8, slots + -slots % LANES))
        for part in (sorted_positions[:slots], sorted_positions[slots:])
    )

    def slot_bias(of_core):
        mine = lax.dynamic_index_in_dim(kept_count, side * 2 + of_core, 0, keepdims=False)
        theirs = lax.dynamic_index_in_dim(kept_count, (1 - side) * 2 + of_core, 0, keepdims=False)
        steps = jnp.arange(slots, dtype=jnp.int32)
        used = jnp.concatenate([steps < mine, steps < theirs])
        return jnp.where(used, 0.0, MASKED)

    bias = jnp.concatenate([slot_bias(core), slot_bias(1 - core)]).astype(BF16)
    bias = jnp.broadcast_to(bias[:, None], (2 * rows, LANES))

    narrow = jnp.stack(
        [norm1_gain, norm1_bias, query_bias, value_bias, out_bias, norm2_gain, norm2_bias, down_bias],
        axis=1,
    )
    count = narrow.shape[1]
    small = jnp.concatenate(
        [
            jnp.pad(narrow.reshape(layers * count, owned), ((0, 0), (0, LANES - owned))),
            jnp.pad(up_bias, ((0, 8 - layers), (0, LANES - up_bias.shape[1]))),
        ],
        axis=0,
    )
    small = jnp.transpose(small.reshape(layers + 1, 8, LANES), (1, 0, 2)).reshape(8, -1)
    table_shard = jnp.concatenate(
        [
            jnp.pad(pos_embed.T, ((0, 0), (0, padded_positions - positions))),
            jnp.pad(small, ((0, 0), (0, padded_positions - small.shape[1]))),
        ],
        axis=0,
    )
    attn_shards, mlp_shards = [], []
    for layer in range(layers):
        qkv = jnp.transpose(qkv_weight[layer].reshape(owned, 3, features), (1, 0, 2))
        attn_shards.append(jnp.concatenate([qkv.reshape(3 * owned, features), out_weight[layer]], axis=0))
        mlp_shards.append(jnp.concatenate([up_weight[layer], down_weight[layer].T], axis=0))
    (state, chip_cotangent, pos_back, narrow_all, unused_up), mlp_fulls, stored = forward(
        choose16, patches, cotangent, pos_kept, pos_sent, bias, table_shard, attn_shards, mlp_shards,
        count, owned, 0,
    )
    row_positions = jnp.concatenate([pos_kept[0, :slots], pos_back[0, :slots]])
    position_ids = jnp.arange(padded_positions, dtype=jnp.int32).astype(F32)
    lookup = (row_positions[:, None] == position_ids[None]).astype(BF16)
    split = layers * count * owned

    def from_chip(values_own, values_back):
        both = jnp.concatenate([values_own, values_back], axis=0)
        parts = split_rows(both)
        return sum(dot_tn(choose16, part) for part in parts)

    activations = from_chip(state[:slots], to_partner(state[slots:]))

    def by_owner(part):
        return part.reshape(devices, owned, part.shape[1])

    gradient = chip_cotangent.astype(F32)
    narrow_parts, up_bias_parts = ([None] * layers for _ in range(2))
    mlp_sums, attn_sums = ([None] * layers for _ in range(2))
    mlp_done = attn_part = None
    for layer in reversed(range(layers)):
        (before, weights, queries, key_rows, value_rows, key_sib, value_sib, exact, lse, middle,
         hidden, slope) = stored[layer]
        weight_q, weight_k, weight_v, weight_o = (weights[i] for i in range(4))
        mlp_full = mlp_fulls[layer]
        gain_one, shift_one, gain_two, shift_two = (narrow_all[count * layer + i] for i in (0, 1, 5, 6))
        act_one = (norm_parts(before)[0] * gain_one + shift_one).astype(BF16)
        mixed = exact.astype(BF16)
        ids = 8 + 3 * layer
        entries = []
        if layer < layers - 1:
            core_sum = jax.ShapeDtypeStruct(*SumCore(attn_part).outs[0])
            entries = [
                (SumCore(attn_part), attn_part, (1, 2)),
                (SumXY(core_sum, "zxy"), 0, (2, 3, 4)),
                (SumZ(mlp_done), mlp_done, (1, 4)),
            ]
        (mid_grad, lines, up_lines, mlp_part), carried = feed_forward_backward(
            gradient, middle, gain_two[None], shift_two[None], hidden, slope, mlp_full,
            Carried(*entries), ids,
        )
        gain_two_part, shift_two_part, down_bias_part = lines[0], lines[1], lines[2]
        up_bias_parts[layer] = up_lines.reshape(-1)
        entries = [(SumXY(mlp_part, "yzx"), mlp_part, (0, 4, 6))]
        if layer < layers - 1:
            mlp_sums[layer + 1] = carried[2]
            entries.append((SumZ(carried[1]), carried[1], (0, 6)))
        grad_one = mid_grad.astype(BF16)
        out_bias_part = jnp.sum(grad_one.astype(F32), axis=0)
        out_part = dot_tn(mixed, grad_one)
        mixed_grad = dot_nt(grad_one, weight_o).astype(BF16)
        (query_grad, key_own, key_far, value_own, value_far), carried = attention_backward(
            queries, key_rows, key_sib, value_rows, value_sib, mixed_grad, exact, lse, bias,
            Carried(*entries), ids + 1,
        )
        mlp_done = carried[0]
        if layer < layers - 1:
            attn_sums[layer + 1] = carried[1]
        key_grad = (key_own.astype(F32) + to_sibling(key_far).astype(F32)).astype(BF16)
        value_grad = (value_own.astype(F32) + to_sibling(value_far).astype(F32)).astype(BF16)
        query_bias_part = jnp.sum(query_grad.astype(F32), axis=0)
        value_bias_part = jnp.sum(value_grad.astype(F32), axis=0)
        attn_part = jnp.concatenate(
            [by_owner(dot_tn(act_one, g)) for g in (query_grad, key_grad, value_grad)]
            + [by_owner(out_part)],
            axis=1,
        ).astype(BF16).reshape(4, 2, 2, 2, 4 * owned, features)
        act_one_grad = (
            dot_nt(query_grad, weight_q) + dot_nt(key_grad, weight_k) + dot_nt(value_grad, weight_v)
        )
        back_one, gain_one_part, shift_one_part = norm_back(before, gain_one, act_one_grad)
        gradient = mid_grad + back_one
        narrow_parts[layer] = jnp.stack(
            [gain_one_part[0], shift_one_part[0], query_bias_part, value_bias_part, out_bias_part,
             gain_two_part, shift_two_part, down_bias_part]
        )
    input_grad = from_chip(gradient[:slots], to_partner(gradient[slots:]))

    table_part = dot_tn(gradient.astype(BF16), lookup)
    narrow_part = jnp.transpose(
        jnp.stack(narrow_parts).reshape(layers, count, devices, owned), (2, 0, 1, 3)
    ).reshape(devices, split)
    up_bias_part = jnp.transpose(
        jnp.stack(up_bias_parts).reshape(layers, devices, -1), (1, 0, 2)
    ).reshape(devices, -1)
    small_part = jnp.concatenate([narrow_part, up_bias_part], axis=1)[:, None]
    table_parts = jnp.concatenate(
        [
            by_owner(table_part),
            jnp.pad(small_part, ((0, 0), (0, 7), (0, padded_positions - small_part.shape[2]))),
        ],
        axis=1,
    ).astype(BF16)
    table_parts = table_parts.reshape((4, 2, 2, 2) + table_parts.shape[1:])
    cores = [SumCore(attn_part), SumCore(table_parts)]
    core_sums = [jax.ShapeDtypeStruct(*stage.outs[0]) for stage in cores]
    crosses = [SumXY(core_sums[0], "zxy"), SumXY(core_sums[1], "zxy")]
    cross_sums = [jax.ShapeDtypeStruct(*stage.outs[0]) for stage in crosses]
    ends = [SumZ(mlp_done), SumZ(cross_sums[0]), SumZ(cross_sums[1])]
    sums = run_stages(
        [*cores, *crosses, *ends],
        [attn_part, table_parts, 0, 1, mlp_done, 2, 3],
        [(0, 0), (1, 0), (4, 0), (0, 1), (2, 0), (1, 1), (3, 0), (2, 1), (3, 1), (2, 2), (5, 0), (3, 2)]
        + [(6, 0), (4, 1), (5, 1), (6, 1)],
        14,
        "sum_last",
    )
    mlp_sums[0], attn_sums[0], table_sum = sums[4], sums[5], sums[6]
    pos_embed_grad = table_sum[:owned, :positions].T
    small_sum = table_sum[owned, : small_part.shape[2]]
    narrow_sum = small_sum[:split].reshape(layers, count, owned)
    up_bias_grad = small_sum[split:].reshape(layers, -1)
    qkv_weight_grad = jnp.stack(
        [
            jnp.transpose(part[: 3 * owned].reshape(3, owned, features), (1, 0, 2)).reshape(owned, -1)
            for part in attn_sums
        ]
    )
    out_weight_grad = jnp.stack([part[3 * owned :] for part in attn_sums])
    up_weight_grad = jnp.stack([part[:up_rows] for part in mlp_sums])
    down_weight_grad = jnp.stack([part[up_rows:].T for part in mlp_sums])
    return (
        activations,
        input_grad,
        pos_embed_grad,
        *(narrow_sum[:, i] for i in range(7)),
        up_bias_grad,
        narrow_sum[:, 7],
        qkv_weight_grad,
        out_weight_grad,
        up_weight_grad,
        down_weight_grad,
    )


def solution(mesh):
    return jax.shard_map(
        chip_shards if mesh.shape["gx"] == 8 and mesh.shape["gy"] == 4 else shards,
        mesh=mesh,
        in_specs=(
            P(("gx", "gy"), None),
            P("gx"),
            P(("gx", "gy")),
            P(None, ("gx", "gy")),
            P(None, ("gx", "gy")),
            P(None, ("gx", "gy")),
            P(None, ("gx", "gy")),
            P(None, ("gx", "gy")),
            P(None, ("gx", "gy")),
            P(None, ("gx", "gy")),
            P(None, ("gx", "gy")),
            P(None, ("gx", "gy")),
            P(None, ("gx", "gy")),
            P(None, ("gx", "gy"), None),
            P(None, ("gx", "gy"), None),
            P(None, "gx", "gy"),
            P(None, "gy", "gx"),
            P(("gx", "gy"), None),
        ),
        out_specs=(
            P(("gx", "gy"), None),
            P(("gx", "gy"), None),
            P(None, ("gx", "gy")),
            P(None, ("gx", "gy")),
            P(None, ("gx", "gy")),
            P(None, ("gx", "gy")),
            P(None, ("gx", "gy")),
            P(None, ("gx", "gy")),
            P(None, ("gx", "gy")),
            P(None, ("gx", "gy")),
            P(None, ("gx", "gy")),
            P(None, ("gx", "gy")),
            P(None, ("gx", "gy"), None),
            P(None, ("gx", "gy"), None),
            P(None, "gx", "gy"),
            P(None, "gy", "gx"),
        ),
        check_vma=False,
    )
```

```python
import functools
import math

import jax
import jax.numpy as jnp
from jax import lax
from jax.experimental import pallas as pl
from jax.experimental.pallas import tpu as pltpu
from jax.sharding import PartitionSpec as P

HEAD_DIM = 64


EPSILON = 1e-06
SQRT_HALF = 1.0 / math.sqrt(2.0)
NORMAL_PEAK = 1.0 / math.sqrt(2.0 * math.pi)
MASKED = -1e30


def layer_norm(values, norm_gain, norm_shift):
    row_mean = jnp.mean(values, axis=-1, keepdims=True)
    centred = values - row_mean
    row_var = jnp.mean(centred * centred, axis=-1, keepdims=True)
    return centred * lax.rsqrt(row_var + EPSILON) * norm_gain + norm_shift


def gelu_slope(pre_act):
    return (
        0.5 * (1.0 + lax.erf(pre_act * SQRT_HALF))
        + pre_act * jnp.exp(-0.5 * pre_act * pre_act) * NORMAL_PEAK
    )


def column_pair(matrix, pair_index, pair_width):
    block = lax.dynamic_slice_in_dim(matrix, pair_index * pair_width, pair_width, 1)
    return block.reshape(matrix.shape[0], 2, pair_width // 2)


def join_pairs(stacked):
    return jnp.transpose(stacked, (1, 0, 2)).reshape(
        stacked.shape[1], stacked.shape[0] * stacked.shape[2]
    )


def pair_scores(head_query, head_keys, same_clip):
    scores = jnp.einsum(
        "qhd,khd->hqk", head_query, head_keys, preferred_element_type=jnp.float32
    ) * HEAD_DIM ** (-0.5)
    return jnp.where(same_clip[None], scores, MASKED)


def pair_parts(head_query, head_keys, head_values, head_grad, same_clip, pair_total):
    scores = pair_scores(head_query, head_keys, same_clip)
    weights = jnp.exp(scores - pair_total)
    weight_grad = jnp.einsum(
        "qhd,khd->hqk", head_grad, head_values, preferred_element_type=jnp.float32
    )
    return (weights, weight_grad)


def attend(queries, key_rows, value_rows, same_clip):
    pair_width = 2 * HEAD_DIM
    pair_count = queries.shape[1] // pair_width

    def one_pair(pair_index):
        head_query = column_pair(queries, pair_index, pair_width)
        head_keys = column_pair(key_rows, pair_index, pair_width)
        head_values = column_pair(value_rows, pair_index, pair_width)
        scores = pair_scores(head_query, head_keys, same_clip)
        row_max = jnp.max(scores, axis=-1, keepdims=True)
        log_total = row_max + jnp.log(jnp.sum(jnp.exp(scores - row_max), axis=-1, keepdims=True))
        weights = jnp.exp(scores - log_total).astype(jnp.bfloat16)
        mixed = jnp.einsum("hqk,khd->qhd", weights, head_values, preferred_element_type=jnp.float32)
        return (mixed.reshape(queries.shape[0], pair_width), log_total)

    mixed, log_total = lax.map(one_pair, jnp.arange(pair_count))
    return (join_pairs(mixed), log_total)


def attend_back(queries, key_rows, value_rows, same_clip, log_total, mixed_grad):
    pair_width = 2 * HEAD_DIM
    pair_count = queries.shape[1] // pair_width
    score_scale = HEAD_DIM ** (-0.5)

    def one_pair(pair_inputs):
        pair_index, pair_total = pair_inputs
        head_query = column_pair(queries, pair_index, pair_width)
        head_keys = column_pair(key_rows, pair_index, pair_width)
        head_values = column_pair(value_rows, pair_index, pair_width)
        head_grad = column_pair(mixed_grad, pair_index, pair_width)
        weights, weight_grad = pair_parts(
            head_query, head_keys, head_values, head_grad, same_clip, pair_total
        )
        value_grad = jnp.einsum(
            "hqk,qhd->khd",
            weights.astype(jnp.bfloat16),
            head_grad,
            preferred_element_type=jnp.float32,
        )
        inner = jnp.sum(weights * weight_grad, axis=-1, keepdims=True)
        score_grad = (weights * (weight_grad - inner)).astype(jnp.bfloat16)
        query_grad = (
            jnp.einsum("hqk,khd->qhd", score_grad, head_keys, preferred_element_type=jnp.float32)
            * score_scale
        )
        key_grad = (
            jnp.einsum("hqk,qhd->khd", score_grad, head_query, preferred_element_type=jnp.float32)
            * score_scale
        )
        return (
            query_grad.reshape(queries.shape[0], pair_width),
            key_grad.reshape(key_rows.shape[0], pair_width),
            value_grad.reshape(key_rows.shape[0], pair_width),
        )

    query_grad, key_grad, value_grad = lax.map(one_pair, (jnp.arange(pair_count), log_total))
    return (join_pairs(query_grad), join_pairs(key_grad), join_pairs(value_grad))


def stacked_member(collected, member_index):
    return jnp.stack([entry[member_index] for entry in collected])


def shards(
    patches,
    clip_of_row,
    position_of_row,
    pos_embed,
    norm1_gain,
    norm1_bias,
    query_bias,
    value_bias,
    out_bias,
    norm2_gain,
    norm2_bias,
    up_bias,
    down_bias,
    qkv_weight,
    out_weight,
    up_weight,
    down_weight,
    cotangent,
):
    (
        position_table,
        gain_one,
        shift_one,
        bias_query,
        bias_value,
        bias_out,
        gain_two,
        shift_two,
        bias_up,
        bias_down,
        weight_qkv,
        weight_out,
    ) = (
        lax.all_gather(pos_embed, ("gx", "gy"), axis=1, tiled=True),
        lax.all_gather(norm1_gain, ("gx", "gy"), axis=1, tiled=True),
        lax.all_gather(norm1_bias, ("gx", "gy"), axis=1, tiled=True),
        lax.all_gather(query_bias, ("gx", "gy"), axis=1, tiled=True),
        lax.all_gather(value_bias, ("gx", "gy"), axis=1, tiled=True),
        lax.all_gather(out_bias, ("gx", "gy"), axis=1, tiled=True),
        lax.all_gather(norm2_gain, ("gx", "gy"), axis=1, tiled=True),
        lax.all_gather(norm2_bias, ("gx", "gy"), axis=1, tiled=True),
        lax.all_gather(up_bias, ("gx", "gy"), axis=1, tiled=True),
        lax.all_gather(down_bias, ("gx", "gy"), axis=1, tiled=True),
        lax.all_gather(qkv_weight, ("gx", "gy"), axis=1, tiled=True),
        lax.all_gather(out_weight, ("gx", "gy"), axis=1, tiled=True),
    )
    block_up, block_down = (
        lax.all_gather(up_weight, "gx", axis=1, tiled=True),
        lax.all_gather(down_weight, "gx", axis=2, tiled=True),
    )
    layer_count = qkv_weight.shape[0]
    features = patches.shape[1]
    row_count = patches.shape[0]
    hidden_width = block_up.shape[2]
    member = lax.axis_index("gy")
    hidden_start = member * hidden_width
    own_clip = lax.dynamic_slice_in_dim(clip_of_row, member * row_count, row_count)
    same_clip = own_clip[:, None] == clip_of_row[None, :]
    state = patches.astype(jnp.float32) + position_table[position_of_row].astype(jnp.float32)
    stored = []
    for layer_index in range(layer_count):
        norm_gain_one = gain_one[layer_index].astype(jnp.float32)
        norm_shift_one = shift_one[layer_index].astype(jnp.float32)
        act_one = layer_norm(state, norm_gain_one, norm_shift_one).astype(jnp.bfloat16)
        projected = jnp.dot(act_one, weight_qkv[layer_index], preferred_element_type=jnp.float32)
        queries = (projected[:, :features] + bias_query[layer_index].astype(jnp.float32)).astype(
            jnp.bfloat16
        )
        key_rows = projected[:, features : 2 * features].astype(jnp.bfloat16)
        value_rows = (
            projected[:, 2 * features :] + bias_value[layer_index].astype(jnp.float32)
        ).astype(jnp.bfloat16)
        all_keys, all_values = (
            lax.all_gather(key_rows, "gy", axis=0, tiled=True),
            lax.all_gather(value_rows, "gy", axis=0, tiled=True),
        )
        mixed, log_total = attend(queries, all_keys, all_values, same_clip)
        attended = mixed.astype(jnp.bfloat16)
        middle = (
            state
            + jnp.dot(attended, weight_out[layer_index], preferred_element_type=jnp.float32)
            + bias_out[layer_index].astype(jnp.float32)
        )
        norm_gain_two = gain_two[layer_index].astype(jnp.float32)
        norm_shift_two = shift_two[layer_index].astype(jnp.float32)
        act_two = layer_norm(middle, norm_gain_two, norm_shift_two).astype(jnp.bfloat16)
        up_columns = lax.dynamic_slice_in_dim(
            bias_up[layer_index], hidden_start, hidden_width
        ).astype(jnp.float32)
        mlp_rows = lax.all_gather(act_two, "gy", axis=0, tiled=True)
        pre_act = (
            jnp.dot(mlp_rows, block_up[layer_index], preferred_element_type=jnp.float32)
            + up_columns
        )
        hidden = jax.nn.gelu(pre_act, approximate=False).astype(jnp.bfloat16)
        partial_out = jnp.dot(hidden, block_down[layer_index], preferred_element_type=jnp.float32)
        mlp_out = lax.psum_scatter(
            partial_out.astype(jnp.bfloat16), "gy", scatter_dimension=0, tiled=True
        ).astype(jnp.float32)
        stored.append(
            (
                state,
                act_one,
                queries,
                key_rows,
                value_rows,
                all_keys,
                all_values,
                log_total,
                attended,
                middle,
                mlp_rows,
                pre_act,
                hidden,
            )
        )
        state = middle + mlp_out + bias_down[layer_index].astype(jnp.float32)
    gradient = cotangent.astype(jnp.float32)
    collected = [None] * layer_count
    for layer_index in reversed(range(layer_count)):
        (
            layer_input,
            act_one,
            queries,
            key_rows,
            value_rows,
            kept_keys,
            kept_values,
            log_total,
            attended,
            middle,
            mlp_rows,
            pre_act,
            hidden,
        ) = stored[layer_index]
        grad_two = gradient.astype(jnp.bfloat16)
        down_bias_part = jnp.sum(grad_two.astype(jnp.float32), axis=0)
        grad_rows = lax.all_gather(grad_two, "gy", axis=0, tiled=True)
        down_part = jnp.einsum("rf,rd->fd", hidden, grad_rows, preferred_element_type=jnp.float32)
        hidden_grad = jnp.einsum(
            "rd,fd->rf", grad_rows, block_down[layer_index], preferred_element_type=jnp.float32
        )
        pre_grad = (hidden_grad * gelu_slope(pre_act)).astype(jnp.bfloat16)
        up_part = jnp.einsum("rd,rf->df", mlp_rows, pre_grad, preferred_element_type=jnp.float32)
        up_columns_grad = jnp.sum(pre_grad.astype(jnp.float32), axis=0)
        up_bias_part = lax.dynamic_update_slice_in_dim(
            jnp.zeros((bias_up.shape[1],), jnp.float32), up_columns_grad, hidden_start, 0
        )
        rows_grad = jnp.einsum(
            "rf,df->rd", pre_grad, block_up[layer_index], preferred_element_type=jnp.float32
        )
        act_two_grad = lax.psum_scatter(
            rows_grad.astype(jnp.bfloat16), "gy", scatter_dimension=0, tiled=True
        ).astype(jnp.float32)
        norm_gain_two = gain_two[layer_index].astype(jnp.float32)
        norm_shift_two = shift_two[layer_index].astype(jnp.float32)
        unused_two, norm_two_pull = jax.vjp(layer_norm, middle, norm_gain_two, norm_shift_two)
        middle_part, gain_two_part, shift_two_part = norm_two_pull(act_two_grad)
        mid_grad = gradient + middle_part
        grad_one = mid_grad.astype(jnp.bfloat16)
        out_bias_part = jnp.sum(grad_one.astype(jnp.float32), axis=0)
        out_part = jnp.einsum("rd,re->de", attended, grad_one, preferred_element_type=jnp.float32)
        mixed_grad = jnp.einsum(
            "re,de->rd", grad_one, weight_out[layer_index], preferred_element_type=jnp.float32
        ).astype(jnp.bfloat16)
        query_grad, key_grad, value_grad = attend_back(
            queries, kept_keys, kept_values, same_clip, log_total, mixed_grad
        )
        key_grad, value_grad = (
            lax.psum_scatter(
                key_grad.astype(jnp.bfloat16), "gy", scatter_dimension=0, tiled=True
            ).astype(jnp.float32),
            lax.psum_scatter(
                value_grad.astype(jnp.bfloat16), "gy", scatter_dimension=0, tiled=True
            ).astype(jnp.float32),
        )
        qkv_grad = jnp.concatenate(
            [
                query_grad.astype(jnp.bfloat16),
                key_grad.astype(jnp.bfloat16),
                value_grad.astype(jnp.bfloat16),
            ],
            axis=1,
        )
        query_bias_part = jnp.sum(qkv_grad[:, :features].astype(jnp.float32), axis=0)
        value_bias_part = jnp.sum(qkv_grad[:, 2 * features :].astype(jnp.float32), axis=0)
        qkv_part = jnp.einsum("rd,re->de", act_one, qkv_grad, preferred_element_type=jnp.float32)
        act_one_grad = jnp.einsum(
            "re,de->rd", qkv_grad, weight_qkv[layer_index], preferred_element_type=jnp.float32
        )
        norm_gain_one = gain_one[layer_index].astype(jnp.float32)
        norm_shift_one = shift_one[layer_index].astype(jnp.float32)
        unused_one, norm_one_pull = jax.vjp(layer_norm, layer_input, norm_gain_one, norm_shift_one)
        input_part, gain_one_part, shift_one_part = norm_one_pull(act_one_grad)
        gradient = mid_grad + input_part
        collected[layer_index] = (
            gain_one_part,
            shift_one_part,
            query_bias_part,
            value_bias_part,
            out_bias_part,
            gain_two_part,
            shift_two_part,
            up_bias_part,
            down_bias_part,
            qkv_part,
            out_part,
            up_part,
            down_part,
        )
    table_part = jax.ops.segment_sum(
        gradient, position_of_row, num_segments=position_table.shape[0]
    )
    (
        pos_embed_grad,
        norm1_gain_grad,
        norm1_bias_grad,
        query_bias_grad,
        value_bias_grad,
        out_bias_grad,
        norm2_gain_grad,
        norm2_bias_grad,
        up_bias_grad,
        down_bias_grad,
        qkv_weight_grad,
        out_weight_grad,
    ) = (
        lax.psum_scatter(table_part, ("gx", "gy"), scatter_dimension=1, tiled=True),
        lax.psum_scatter(
            stacked_member(collected, 0), ("gx", "gy"), scatter_dimension=1, tiled=True
        ),
        lax.psum_scatter(
            stacked_member(collected, 1), ("gx", "gy"), scatter_dimension=1, tiled=True
        ),
        lax.psum_scatter(
            stacked_member(collected, 2), ("gx", "gy"), scatter_dimension=1, tiled=True
        ),
        lax.psum_scatter(
            stacked_member(collected, 3), ("gx", "gy"), scatter_dimension=1, tiled=True
        ),
        lax.psum_scatter(
            stacked_member(collected, 4), ("gx", "gy"), scatter_dimension=1, tiled=True
        ),
        lax.psum_scatter(
            stacked_member(collected, 5), ("gx", "gy"), scatter_dimension=1, tiled=True
        ),
        lax.psum_scatter(
            stacked_member(collected, 6), ("gx", "gy"), scatter_dimension=1, tiled=True
        ),
        lax.psum_scatter(
            stacked_member(collected, 7), ("gx", "gy"), scatter_dimension=1, tiled=True
        ),
        lax.psum_scatter(
            stacked_member(collected, 8), ("gx", "gy"), scatter_dimension=1, tiled=True
        ),
        lax.psum_scatter(
            stacked_member(collected, 9), ("gx", "gy"), scatter_dimension=1, tiled=True
        ),
        lax.psum_scatter(
            stacked_member(collected, 10), ("gx", "gy"), scatter_dimension=1, tiled=True
        ),
    )
    up_stack = stacked_member(collected, 11)
    down_stack = stacked_member(collected, 12)
    up_weight_grad, down_weight_grad = (
        lax.psum_scatter(
            up_stack.astype(jnp.bfloat16), "gx", scatter_dimension=1, tiled=True
        ).astype(jnp.float32),
        lax.psum_scatter(
            down_stack.astype(jnp.bfloat16), "gx", scatter_dimension=2, tiled=True
        ).astype(jnp.float32),
    )
    return (
        state,
        gradient,
        pos_embed_grad,
        norm1_gain_grad,
        norm1_bias_grad,
        query_bias_grad,
        value_bias_grad,
        out_bias_grad,
        norm2_gain_grad,
        norm2_bias_grad,
        up_bias_grad,
        down_bias_grad,
        qkv_weight_grad,
        out_weight_grad,
        up_weight_grad,
        down_weight_grad,
    )


LOG2_E = 1.0 / math.log(2.0)
LANES = 128
BF16 = jnp.bfloat16
F32 = jnp.float32
MESH_ID = pl.DeviceIdType.MESH
VMEM_LIMIT = 60 * 1024 * 1024


def dot_nn(left, right):
    return lax.dot_general(left, right, (((1,), (0,)), ((), ())), preferred_element_type=F32)


def dot_nt(left, right):
    return lax.dot_general(left, right, (((1,), (1,)), ((), ())), preferred_element_type=F32)


def dot_tn(left, right):
    return lax.dot_general(left, right, (((0,), (0,)), ((), ())), preferred_element_type=F32)


def my_place():
    gx = lax.axis_index("gx")
    gy = lax.axis_index("gy")
    return gx // 2, lax.rem(gx, 2), gy // 2, lax.rem(gy, 2)


def device_at(z, x, y, core):
    return (z * 2 + x, y * 2 + core)


class Copy:
    def __init__(self, describe):
        self.describe = describe

    def start(self):
        self.describe().start()

    def wait(self):
        self.describe().wait()

    def wait_recv(self):
        self.describe().wait_recv()

    def wait_send(self):
        self.describe().wait_send()


def remote(src, dst, send_sem, recv_sem, device):
    return Copy(
        lambda: pltpu.make_async_remote_copy(
            src_ref=src,
            dst_ref=dst,
            send_sem=send_sem,
            recv_sem=recv_sem,
            device_id=device,
            device_id_type=MESH_ID,
        )
    )


def local_copy(src, dst, sem):
    return Copy(lambda: pltpu.make_async_copy(src, dst, sem))


def full_at(ref, order, z, x, y, core, *rest):
    place = (z, x, y, core) if order == "zxy" else (y, core, z, x)
    return ref.at[(*place, *rest)]


def hbm():
    return pl.BlockSpec(memory_space=pl.ANY)


def vmem():
    return pl.BlockSpec(memory_space=pltpu.VMEM)


def dma_sems(count):
    return pltpu.SemaphoreType.DMA((count,))


def added(left, right):
    return (left.astype(F32) + right.astype(F32)).astype(BF16)


def greet_signal(place):
    z, x, y, core = place
    barrier = pltpu.get_barrier_semaphore()
    others = [device_at(lax.rem(z + k, 4), x, y, core) for k in (1, 2, 3)]
    others += [device_at(z, 1 - x, y, core), device_at(z, x, 1 - y, core)]
    others += [device_at(z, x, y, 1 - core)]
    for other in others:
        pl.semaphore_signal(barrier, inc=1, device_id=other, device_id_type=MESH_ID)


def greet_wait():
    pl.semaphore_wait(pltpu.get_barrier_semaphore(), 6)


def lane_marks(head):
    lane = lax.broadcasted_iota(jnp.int32, (1, LANES), 1)
    own = (lane // HEAD_DIM == head).astype(F32)
    spare = HEAD_DIM * (1 - head)
    return lane, own, spare


def split_three(column):
    high = column.astype(BF16).astype(F32)
    rest = column - high
    middle = rest.astype(BF16).astype(F32)
    return high, middle, rest - middle


def norm_parts(values):
    row_mean = jnp.mean(values, axis=-1, keepdims=True)
    centred = values - row_mean
    row_var = jnp.mean(centred * centred, axis=-1, keepdims=True)
    rstd = lax.rsqrt(row_var + EPSILON)
    return centred * rstd, rstd


def norm_back(values, gain, grad):
    normed, rstd = norm_parts(values)
    scaled = grad * gain
    first = jnp.mean(scaled, axis=-1, keepdims=True)
    second = jnp.mean(scaled * normed, axis=-1, keepdims=True)
    back = (scaled - first - normed * second) * rstd
    return back, jnp.sum(grad * normed, axis=0, keepdims=True), jnp.sum(grad, axis=0, keepdims=True)


class Gather:
    def __init__(self, place, shard, full, order, start, rows, send, recv, local):
        z, x, y, core = place
        half = rows // 2
        every = slice(None)
        both, low, high = pl.ds(start, rows), pl.ds(start, half), pl.ds(start + half, half)

        def at(*where):
            return full_at(full, order, *where)

        def copy(slot, src, dst, device):
            return remote(src, dst, send.at[slot], recv.at[slot], device)

        def same(slot, ref, device):
            return copy(slot, ref, ref, device)

        to_x, to_y = device_at(z, 1 - x, y, core), device_at(z, x, 1 - y, core)
        own = at(z, x, y, core, both)
        self.keep = local_copy(shard.at[both], own, local)
        self.along_z = [
            copy(k, shard.at[both], own, device_at(lax.rem(z + k + 1, 4), x, y, core)) for k in range(3)
        ]
        self.first = [
            same(3, at(every, x, y, core, low), to_x),
            same(4, at(every, x, y, core, high), to_y),
        ]
        self.second = [
            same(5, at(every, every, y, core, low), to_y),
            same(6, at(every, x, every, core, high), to_x),
        ]
        self.third = [same(7, at(every, every, every, core, both), device_at(z, x, y, 1 - core))]

    def start_z(self):
        self.keep.start()
        for copy in self.along_z:
            copy.start()

    def start_first(self):
        self.keep.wait()
        for copy in self.along_z:
            copy.wait_recv()
        for copy in self.first:
            copy.start()

    def start_second(self):
        for copy in self.first:
            copy.wait_recv()
        for copy in self.second:
            copy.start()

    def start_third(self):
        for copy in self.second:
            copy.wait_recv()
        for copy in self.third:
            copy.start()

    def finish(self):
        for copy in self.third:
            copy.wait_recv()

    def drain(self):
        for copy in self.along_z + self.first + self.second + self.third:
            copy.wait_send()


class GatherChain:
    def __init__(self, gathers):
        self.gathers = gathers

    def begin(self):
        for gather in self.gathers[:2]:
            gather.start_z()

    def follow(self):
        for index in range(2):
            self.gathers[index].start_first()
            self.gathers[index + 2].start_z()
        self.gathers[0].start_second()

    def turn(self, index):
        count = len(self.gathers)
        self.gathers[index].start_third()
        if index + 1 < count:
            self.gathers[index + 1].start_second()
        if index + 2 < count:
            self.gathers[index + 2].start_first()
        if index + 4 < count:
            self.gathers[index + 4].start_z()

    def finish(self, index):
        self.gathers[index].finish()

    def drain(self):
        for gather in self.gathers:
            gather.drain()


def spread_matrix(width, columns):
    row = lax.broadcasted_iota(jnp.int32, (LANES, columns), 0)
    lane = lax.broadcasted_iota(jnp.int32, (LANES, columns), 1)
    return (row == lax.rem(lane, width)).astype(F32).astype(BF16)


def forward_kernel(sizes, *refs):
    layers, count, owned, up_rows = sizes
    (choose, patches, cotangent, pos_kept, pos_sent, bias, table_shard), refs = refs[:7], refs[7:]
    attn_shards, refs = refs[:layers], refs[layers:]
    mlp_shards, refs = refs[:layers], refs[layers:]
    (final, chip_cot, pos_back, narrow, up_bias), refs = refs[:5], refs[5:]
    mlp_fulls, refs = refs[:layers], refs[layers:]
    kept, refs = refs[: 12 * layers], refs[12 * layers :]
    (
        table_full, attn_full, table, weights, mlp_block, sorted_rows, arrived_rows, middle, act, query,
        key, value, key_sib, value_sib, exact, mixed, lse, hidden, slope, keys, values,
        send, recv, local, swap_send, swap_recv, save_sem, load_sem,
    ) = refs
    state = final
    place = my_place()
    z, x, y, core = place
    rows, features = state.shape
    slots = rows // 2
    halves = [slice(0, slots), slice(slots, rows)]
    blocks = mlp_fulls[0].shape[0] * mlp_fulls[0].shape[1]
    to_y, to_core = device_at(z, x, 1 - y, core), device_at(z, x, y, 1 - core)
    score_scale = HEAD_DIM ** (-0.5) * LOG2_E

    def gather(slot, shard, full, order, start, size):
        return Gather(
            place, shard, full, order, start, size, send.at[slot], recv.at[slot], local.at[slot]
        )

    gathers = [gather(0, table_shard, table_full, "zxy", 0, table_shard.shape[0])]
    for layer in range(layers):
        slot = 1 + 3 * layer
        gathers.append(gather(slot, attn_shards[layer], attn_full.at[layer], "zxy", 0, 4 * owned))
        for part in range(2):
            gathers.append(
                gather(
                    slot + 1 + part, mlp_shards[layer], mlp_fulls[layer], "yzx", part * up_rows, up_rows
                )
            )
    chain = GatherChain(gathers)

    def swap(slot, src, dst, device):
        return remote(src, dst, swap_send.at[slot], swap_recv.at[slot], device)

    greet_signal(place)
    greet_wait()
    chain.begin()
    send_pos = swap(0, pos_sent, pos_back, to_y)
    send_pos.start()
    sorted_rows[...] = dot_nn(choose[...], patches[...]).astype(BF16)
    send_rows = swap(1, sorted_rows.at[halves[1]], arrived_rows, to_y)
    send_rows.start()
    chain.follow()
    chip_cot[halves[0]] = dot_nn(choose[halves[0]], cotangent[...]).astype(BF16)
    chain.turn(0)
    send_pos.wait()
    send_rows.wait()
    chain.finish(0)

    devices = 32
    for a in range(4):
        block = table_full[a].reshape(8, owned + 8, table.shape[1]).astype(F32)
        table[a * 8 * owned : (a + 1) * 8 * owned] = (
            block[:, :owned].reshape(8 * owned, table.shape[1]).astype(BF16)
        )
    lane = lax.broadcasted_iota(jnp.int32, (devices, 1, features), 2)
    device = lax.broadcasted_iota(jnp.int32, (devices, 1, features), 0)
    for b in range(3):
        width = owned if b < 2 else 4 * owned
        packed = table_full[:, :, :, :, owned:, b * LANES : (b + 1) * LANES]
        packed = packed.reshape(devices * 8, LANES)
        wide = dot_nn(packed, spread_matrix(width, features)).reshape(devices, 8, features)
        if b < 2:
            wide = jnp.where(lane // owned == device, wide, 0.0)
            narrow[8 * b : 8 * b + 8] = jnp.sum(wide, axis=0)
        else:
            wide = jnp.where(lane // width == lax.rem(device, 8), wide, 0.0)
            up_bias[...] = jnp.sum(wide.reshape(4, 8, 8, features), axis=1)

    position = lax.broadcasted_iota(jnp.int32, (slots, table.shape[1]), 1).astype(F32)
    for at, pos, row_ref in ((halves[0], pos_kept, sorted_rows), (halves[1], pos_back, arrived_rows)):
        column = jnp.transpose(jnp.broadcast_to(pos[0:1, 0:slots], (LANES, slots)))[:, 0:1]
        lookup = (position == column).astype(F32).astype(BF16)
        state[at] = row_ref[0:slots].astype(F32) + dot_nt(lookup, table[...])

    def save(layer, index, ref):
        return local_copy(ref, kept[12 * layer + index], save_sem.at[index])

    def save_block(layer, index, block):
        ref = (hidden, slope)[index - 10].at[lax.rem(block, 2)]
        return local_copy(ref, kept[12 * layer + index].at[block], save_sem.at[index + 2 * lax.rem(block, 2)])

    def load_block(layer, block):
        slot = lax.rem(block, 2)
        return local_copy(
            mlp_fulls[layer].at[block // 2, lax.rem(block, 2)], mlp_block.at[slot], load_sem.at[slot]
        )

    def attend_pair(pair, layer):
        at_lanes = pl.ds(pl.multiple_of(pair * LANES, LANES), LANES)
        values[halves[0]] = value[halves[0], at_lanes]
        values[halves[1]] = value[halves[1], at_lanes]
        values[rows : rows + slots] = value_sib[layer, halves[0], at_lanes]
        values[rows + slots :] = value_sib[layer, halves[1], at_lanes]
        lanes = lax.broadcasted_iota(jnp.int32, (1, LANES), 1)
        results = [[], []]
        totals = [[], []]
        for head in range(2):
            lane, own, spare = lane_marks(head)
            own16 = own.astype(BF16)
            at_spare = (lane == spare).astype(BF16)
            keys[0:rows] = key[:, at_lanes] * own16 + bias[0:rows] * at_spare
            keys[rows:] = key_sib[layer, :, at_lanes] * own16 + bias[rows:] * at_spare
            for at in halves:
                scores = dot_nt(query[at, at_lanes] * own16 + at_spare, keys[...])
                top = jnp.max(scores, axis=-1, keepdims=True)
                weight = jnp.exp2(scores - top)
                total = jnp.sum(weight, axis=-1, keepdims=True)
                results[head].append(dot_nn(weight.astype(BF16), values[...]) * (1.0 / total))
                totals[head].append(top + jnp.log2(total))
        for index, at in enumerate(halves):
            both = jnp.where(lanes < HEAD_DIM, results[0][index], results[1][index])
            mixed[at, at_lanes] = both.astype(BF16)
            exact[at, at_lanes] = both
            held = lse[at]
            held = jnp.where(lanes == 2 * pair, totals[0][index], held)
            lse[at] = jnp.where(lanes == 2 * pair + 1, totals[1][index], held)

    def saved_refs(layer):
        return (query, key, value, key_sib.at[layer], value_sib.at[layer], exact)

    lse[...] = jnp.zeros_like(lse)
    for layer in range(layers):
        after = layer > 0
        base = count * layer

        def line(index):
            return narrow[base + index : base + index + 1]

        save(layer, 0, state).start()
        for at in halves:
            normed, unused = norm_parts(state[at])
            act[at] = (normed * line(0) + line(1)).astype(BF16)
        if not after:
            chain.turn(1)
        chain.finish(1 + 3 * layer)
        if after:
            save(layer - 1, 1, weights).wait()
        for a in range(4):
            block = attn_full[layer, a].reshape(8, 4 * owned, features).astype(F32)
            for index in range(4):
                part = block[:, index * owned : (index + 1) * owned].reshape(8 * owned, features)
                weights[index, a * 8 * owned : (a + 1) * 8 * owned] = part.astype(BF16)
        save(layer, 1, weights).start()
        if after:
            for index in range(2, 8):
                save(layer - 1, index, saved_refs(layer - 1)[index - 2]).wait()
            save(layer - 1, 8, lse).wait()
        for at in halves:
            key[at] = dot_nn(act[at], weights[1]).astype(BF16)
        swap(2 + 2 * layer, key, key_sib.at[layer], to_core).start()
        for at in halves:
            value[at] = (dot_nn(act[at], weights[2]) + line(3)).astype(BF16)
        swap(3 + 2 * layer, value, value_sib.at[layer], to_core).start()
        for at in halves:
            query[at] = ((dot_nn(act[at], weights[0]) + line(2)) * score_scale).astype(BF16)
        swap(2 + 2 * layer, key, key_sib.at[layer], to_core).wait()
        swap(3 + 2 * layer, value, value_sib.at[layer], to_core).wait()

        def one_pair(pair, carry, layer=layer):
            attend_pair(pair, layer)
            when = 2 if layer == 0 else 0
            pl.when(pair == when)(lambda: chain.turn(2 + 3 * layer))
            return carry

        lax.fori_loop(0, features // LANES, one_pair, 0)
        for index in range(2, 8):
            save(layer, index, saved_refs(layer)[index - 2]).start()
        save(layer, 8, lse).start()
        if after:
            save(layer - 1, 9, middle).wait()
        for at in halves:
            total = state[at] + dot_nn(mixed[at], weights[3]) + line(4)
            middle[at] = total
            normed, unused = norm_parts(total)
            act[at] = (normed * line(5) + line(6)).astype(BF16)
        save(layer, 9, middle).start()
        save(layer, 0, state).wait()
        for at in halves:
            state[at] = middle[at] + line(7)
        chain.turn(3 + 3 * layer)
        chain.finish(2 + 3 * layer)
        chain.finish(3 + 3 * layer)
        load_block(layer, 0).start()
        if layer == layers - 1:
            sorted_back = swap(2 + 2 * layers, sorted_rows.at[halves[1]], chip_cot.at[halves[1]], to_y)
            sorted_rows[halves[1]] = dot_nn(choose[halves[1]], cotangent[...]).astype(BF16)
            sorted_back.start()

        def one_block(block, carry, layer=layer):
            slot = lax.rem(block, 2)
            pl.when(block + 1 < blocks)(lambda: load_block(layer, block + 1).start())
            load_block(layer, block).wait()

            @pl.when(block >= 2)
            def _():
                save_block(layer, 10, block - 2).wait()
                save_block(layer, 11, block - 2).wait()

            weight_up = mlp_block[slot, :, :, 0:up_rows, :].reshape(features, features)
            weight_down = mlp_block[slot, :, :, up_rows:, :].reshape(features, features)
            shift = up_bias[block, layer : layer + 1]
            for at in halves:
                pre_act = dot_nn(act[at], weight_up) + shift
                below = 0.5 * (1.0 + lax.erf(pre_act * SQRT_HALF))
                hidden_part = (pre_act * below).astype(BF16)
                hidden[slot, at] = hidden_part
                bend = below + pre_act * jnp.exp(-0.5 * pre_act * pre_act) * NORMAL_PEAK
                slope[slot, at] = bend.astype(BF16)
                state[at] += dot_nt(hidden_part, weight_down)
            save_block(layer, 10, block).start()
            save_block(layer, 11, block).start()
            return carry

        lax.fori_loop(0, blocks, one_block, 0)
        for block in (blocks - 2, blocks - 1):
            save_block(layer, 10, block).wait()
            save_block(layer, 11, block).wait()
        if layer < layers - 1:
            chain.turn(4 + 3 * layer)
    last = layers - 1
    swap(2 + 2 * layers, sorted_rows.at[halves[1]], chip_cot.at[halves[1]], to_y).wait()
    save(last, 1, weights).wait()
    for index in range(2, 8):
        save(last, index, saved_refs(last)[index - 2]).wait()
    save(last, 8, lse).wait()
    save(last, 9, middle).wait()
    chain.drain()


def forward(choose, patches, cotangent, pos_kept, pos_sent, bias, table_shard, attn_shards, mlp_shards, count, owned, collective_id):
    layers = len(attn_shards)
    rows, features = choose.shape[0], patches.shape[1]
    deep = mlp_shards[0].shape[0]
    blocks = 4
    wide = (rows, features)

    def like(shape, dtype):
        return jax.ShapeDtypeStruct(shape, dtype)

    saved = [
        like(wide, F32), like((4, features, features), BF16), *[like(wide, BF16)] * 5, like(wide, F32),
        like((rows, LANES), F32), like(wide, F32), *[like((blocks,) + wide, BF16)] * 2,
    ]
    out_shape = [
        like(wide, F32), like(wide, BF16), like(pos_sent.shape, F32), like((layers * count, features), F32),
        like((blocks, 8, features), F32),
        *[like((2, 2, 4, 2, deep, features), BF16)] * layers,
        *(saved * layers),
    ]
    groups = 1 + 3 * layers
    half16 = pltpu.VMEM((rows // 2, features), BF16)
    wide16, wide32 = pltpu.VMEM(wide, BF16), pltpu.VMEM(wide, F32)
    each16 = pltpu.VMEM((layers,) + wide, BF16)
    scratch = [
        pltpu.VMEM((4, 2, 2, 2) + table_shard.shape, BF16),
        pltpu.VMEM((layers, 4, 2, 2, 2, 4 * owned, features), BF16),
        pltpu.VMEM((features, table_shard.shape[1]), BF16),
        pltpu.VMEM((4, features, features), BF16),
        pltpu.VMEM((2, 4, 2, deep, features), BF16),
        wide16, half16, wide32, wide16, wide16, wide16, wide16, each16, each16, wide32, wide16,
        pltpu.VMEM((rows, LANES), F32),
        pltpu.VMEM((2,) + wide, BF16),
        pltpu.VMEM((2,) + wide, BF16),
        pltpu.VMEM((2 * rows, LANES), BF16),
        pltpu.VMEM((2 * rows, LANES), BF16),
        pltpu.SemaphoreType.DMA((groups, 8)),
        pltpu.SemaphoreType.DMA((groups, 8)),
        dma_sems(groups),
        dma_sems(3 + 2 * layers),
        dma_sems(3 + 2 * layers),
        dma_sems(14),
        dma_sems(2),
    ]
    args = (choose, patches, cotangent, pos_kept, pos_sent, bias, table_shard, *attn_shards, *mlp_shards)
    results = pl.pallas_call(
        functools.partial(forward_kernel, (layers, count, owned, deep // 2)),
        out_shape=out_shape,
        in_specs=[vmem()] * len(args),
        out_specs=[vmem()] * 5 + [hbm()] * (len(out_shape) - 5),
        scratch_shapes=scratch,
        compiler_params=pltpu.CompilerParams(
            collective_id=collective_id, has_side_effects=True, vmem_limit_bytes=VMEM_LIMIT
        ),
        name="forward",
    )(*args)
    mlp_fulls = results[5 : 5 + layers]
    kept = results[5 + layers :]
    return results[:5], mlp_fulls, [kept[12 * i : 12 * i + 12] for i in range(layers)]


class Sum:
    def __init__(self, place, part, out, rows, in_low, in_high, second, last, send, recv):
        z, x, y, core = place
        self.place, self.part, self.out = place, part, out
        self.in_low, self.in_high, self.second_in, self.last_in = in_low, in_high, second, last
        split = rows // 32 * 16 if rows % 32 == 0 else rows - 16
        self.low, self.high, self.rows = pl.ds(0, split), pl.ds(split, rows - split), pl.ds(0, rows)
        self.low_at, self.high_at = pl.ds(0, split), pl.ds(0, rows - split)
        self.finished = False
        every = slice(None)

        def copy(slot, src, dst, device):
            return remote(src, dst, send.at[slot], recv.at[slot], device)

        to_x, to_y = device_at(z, 1 - x, y, core), device_at(z, x, 1 - y, core)
        self.first = [
            copy(0, part.at[1 - y, :, :, self.low], in_low.at[:, :, self.low_at], to_y),
            copy(1, part.at[:, :, 1 - x, self.high], in_high.at[:, :, self.high_at], to_x),
        ]
        self.second = [
            copy(2, part.at[y, :, 1 - x, self.low], second.at[0, :, self.low_at], to_x),
            copy(3, part.at[1 - y, :, x, self.high], second.at[1, :, self.high_at], to_y),
        ]
        self.third = []
        for k in range(3):
            to_z = lax.rem(z + k + 1, 4)
            self.third.append(
                copy(4 + k, part.at[y, to_z, x, self.rows], last.at[k, self.rows], device_at(to_z, x, y, core))
            )

    def start(self):
        for copy in self.first:
            copy.start()

    def cross(self):
        z, x, y, core = self.place
        part, low, high = self.part, self.low, self.high
        for copy in self.first:
            copy.wait()

        def add_one(i, carry):
            a, b = i // 2, lax.rem(i, 2)
            part[y, a, b, low] = added(part[y, a, b, low], self.in_low[a, b, self.low_at])
            part[b, a, x, high] = added(part[b, a, x, high], self.in_high[b, a, self.high_at])
            return carry

        lax.fori_loop(0, 8, add_one, 0)
        for copy in self.second:
            copy.start()

    def along_z(self, before):
        z, x, y, core = self.place
        part, low, high = self.part, self.low, self.high
        for copy in self.second:
            copy.wait()

        def add_one(a, carry):
            part[y, a, x, low] = added(part[y, a, x, low], self.second_in[0, a, self.low_at])
            part[y, a, x, high] = added(part[y, a, x, high], self.second_in[1, a, self.high_at])
            return carry

        lax.fori_loop(0, 4, add_one, 0)
        if before is not None:
            before.finish()
        for copy in self.third:
            copy.start()

    def finish(self):
        if self.finished:
            return
        self.finished = True
        z, x, y, core = self.place
        for copy in self.third:
            copy.wait()
        total = self.part[y, z, x, self.rows].astype(F32)
        for k in range(3):
            total = total + self.last_in[k, self.rows].astype(F32)
        self.out[...] = total


def attend_pair_back(pair, wide, exact, lse, bias):
    rows = lse.shape[0]
    block = rows // 2
    at_lanes = pl.ds(pl.multiple_of(pair * LANES, LANES), LANES)
    lanes = lax.broadcasted_iota(jnp.int32, (1, LANES), 1)
    query = wide[0, :, at_lanes]
    grad = wide[5, :, at_lanes]
    product = grad.astype(F32) * exact[:, at_lanes]
    heads = []
    for head in range(2):
        lane, own, spare = lane_marks(head)
        own16 = own.astype(BF16)
        total = jnp.sum(jnp.where(lanes == 2 * pair + head, lse[...], 0.0), axis=-1, keepdims=True)
        inner = jnp.sum(product * own, axis=-1, keepdims=True)
        lse_parts, inner_parts = split_three(-total), split_three(-inner)
        query_own = query * own16
        grad_own = grad * own16
        query_aug = jnp.where(lane == spare, 1.0, 0.0)
        grad_aug = jnp.zeros((1, LANES), F32)
        for k in range(3):
            query_aug = jnp.where(lane == spare + 1 + k, lse_parts[k], query_aug)
            grad_aug = jnp.where(lane == spare + 1 + k, inner_parts[k], grad_aug)
        query_aug = query_own + query_aug.astype(BF16)
        grad_aug = grad_own + grad_aug.astype(BF16)
        at_spare = (lane == spare).astype(BF16)
        ones = ((lane > spare) & (lane < spare + 4)).astype(BF16)
        heads.append((own16, at_spare, ones, query_own, grad_own, query_aug, grad_aug))
    query_grad = jnp.zeros((LANES, rows), F32)
    for side in range(2):
        at_key, at_value = (1, 2) if side == 0 else (3, 4)
        for start in range(0, rows, block):
            at = slice(start, start + block)
            key, value = wide[at_key, at, at_lanes], wide[at_value, at, at_lanes]
            shift = bias[side * rows + start : side * rows + start + block]
            key_grad = jnp.zeros((block, LANES), F32)
            value_grad = jnp.zeros((block, LANES), F32)
            for own16, at_spare, ones, query_own, grad_own, query_aug, grad_aug in heads:
                key_own = key * own16
                weights = jnp.exp2(dot_nt(key_own + shift * at_spare + ones, query_aug))
                weight_grad = dot_nt(value * own16 + ones, grad_aug)
                score_grad = (weights * weight_grad).astype(BF16)
                value_grad = value_grad + dot_nn(weights.astype(BF16), grad_own)
                key_grad = key_grad + dot_nn(score_grad, query_own)
                query_grad = query_grad + dot_tn(key_own, score_grad)
            wide[at_key, at, at_lanes] = (key_grad * (1.0 / LOG2_E)).astype(BF16)
            wide[at_value, at, at_lanes] = value_grad.astype(BF16)
    wide[0, :, at_lanes] = (jnp.transpose(query_grad) * HEAD_DIM ** (-0.5)).astype(BF16)


def backward_kernel(sizes, *refs):
    layers, count, owned, up_rows = sizes
    (chip_cot, narrow, bias, pos_kept, pos_back, final), refs = refs[:6], refs[6:]
    mlp_fulls, refs = refs[:layers], refs[layers:]
    kept, refs = refs[: 12 * layers], refs[12 * layers :]
    (grad, final_back, grad_back), refs = refs[:3], refs[3:]
    sums, refs = refs[: 3 * layers + 1], refs[3 * layers + 1 :]
    (
        wide, middle, before, total, lse, weights, mlp_block, act_t, grad_t, sent, arrived, arrived_attn,
        part_mlp, part_attn, in_low, in_high, second_in, last_in, lines, up_lines,
        sum_send, sum_recv, core_send, core_recv, far_send, far_recv, swap_send, swap_recv, load_sem, block_sem,
    ) = refs
    place = my_place()
    z, x, y, core = place
    rows, features = grad.shape
    slots = rows // 2
    halves = [slice(0, slots), slice(slots, rows)]
    to_y, to_core = device_at(z, x, 1 - y, core), device_at(z, x, y, 1 - core)
    blocks = 4
    top = layers - 1
    exact = total

    def group(index, part, size):
        slot = index % 2
        return Sum(
            place, part, sums[index], size, in_low.at[slot], in_high.at[slot], second_in.at[slot],
            last_in.at[slot], sum_send.at[index], sum_recv.at[index],
        )

    groups = []
    for layer in range(layers):
        groups += [group(3 * layer + i, part_mlp.at[i], up_rows) for i in range(2)]
        groups.append(group(3 * layer + 2, part_attn, 4 * owned))
    groups.append(group(3 * layers, part_mlp.at[0], 2 * owned))

    def along_z(index):
        groups[index].along_z(groups[index - 1] if index > 0 else None)

    def load(layer, index, ref, slot):
        return local_copy(kept[12 * layer + index], ref, load_sem.at[slot])

    def place_of(step):
        return lax.rem(step, 2), jnp.where(step < 2, 1 - core, core)

    def load_block(layer, step):
        row, column = place_of(step)
        slot = lax.rem(step, 2)
        block = row * 2 + column
        return [
            local_copy(mlp_fulls[layer].at[row, column], mlp_block.at[slot], block_sem.at[slot]),
            local_copy(kept[12 * layer + 10].at[block], wide.at[slot], block_sem.at[2 + slot]),
            local_copy(kept[12 * layer + 11].at[block], wide.at[2 + slot], block_sem.at[4 + slot]),
        ]

    def to_sibling_block(slot, src, dst):
        return remote(src, dst, core_send.at[slot], core_recv.at[slot], to_core)

    swap_final = remote(
        final.at[pl.ds(slots, slots)], final_back, swap_send.at[0], swap_recv.at[0], to_y
    )
    swap_grad = remote(wide.at[3, pl.ds(0, slots)], grad_back, swap_send.at[1], swap_recv.at[1], to_y)

    greet_signal(place)
    load(top, 9, middle, 0).start()
    for copy in load_block(top, 0):
        copy.start()
    lines[...] = jnp.zeros_like(lines)
    up_lines[...] = jnp.zeros_like(up_lines)
    grad[...] = chip_cot[...].astype(F32)

    for layer in reversed(range(layers)):
        base = count * layer
        first = 3 * (top - layer)
        load(layer, 0, before, 1).start()
        load(layer, 1, weights, 2).start()

        def line(index, base=base):
            return narrow[base + index : base + index + 1]

        def note(index, value, base=base):
            lines[base + index : base + index + 1] = value

        load(layer, 9, middle, 0).wait()
        normed, unused = norm_parts(middle[...])
        act_t[...] = jnp.transpose(normed * line(5) + line(6)).astype(BF16)
        wide[5] = grad[...].astype(BF16)
        grad_t[...] = jnp.transpose(grad[...]).astype(BF16)
        total[...] = jnp.zeros_like(total)
        if layer == top:
            greet_wait()
            swap_final.start()

        def one_block(step, carry, layer=layer, first=first):
            slot = lax.rem(step, 2)

            @pl.when(step + 1 < blocks)
            def _():
                for copy in load_block(layer, step + 1):
                    copy.start()

            for copy in load_block(layer, step):
                copy.wait()
            weight_up = mlp_block[slot, :, :, 0:up_rows, :].reshape(features, features)
            weight_down = mlp_block[slot, :, :, up_rows:, :].reshape(features, features)
            row, column = place_of(step)
            sums_up = jnp.zeros((1, features), F32)
            for at in halves:
                hidden_grad = dot_nn(wide[5, at], weight_down)
                pre_grad = (hidden_grad * wide[2 + slot, at].astype(F32)).astype(BF16)
                wide[4, at] = pre_grad
                sums_up = sums_up + jnp.sum(pre_grad.astype(F32), axis=0, keepdims=True)
                total[at] += dot_nt(pre_grad, weight_up)
            up_lines[row * 2 + column, layer : layer + 1] = sums_up

            def parts(store):
                deep = 2 * up_rows
                for a in range(4):
                    at = slice(a * deep, (a + 1) * deep)
                    store(0, a, dot_nn(act_t[at], wide[4]).reshape(2, up_rows, features))
                    store(1, a, dot_nn(grad_t[at], wide[slot]).reshape(2, up_rows, features))

            @pl.when(step < 2)
            def _():
                def store(i, a, value):
                    sent[i, a] = value.astype(BF16)

                @pl.when(step == 1)
                def _():
                    to_sibling_block(0, sent, arrived.at[0]).wait_send()

                parts(store)
                to_sibling_block(step, sent, arrived.at[step]).start()

            @pl.when(step >= 2)
            def _():
                @pl.when(step == 2)
                def _():
                    to_sibling_block(1, sent, arrived.at[1]).wait_send()

                to_sibling_block(step - 2, sent, arrived.at[step - 2]).wait_recv()

                def store(i, a, value):
                    other = arrived[step - 2, i, a].astype(F32)
                    part_mlp[i, step - 2, a] = (value + other).astype(BF16)

                parts(store)

            if layer < top:
                pl.when(step == 0)(groups[first - 1].cross)
                pl.when(step == 1)(groups[first - 2].finish)
                pl.when(step == 3)(lambda: along_z(first - 1))
            return carry

        lax.fori_loop(0, blocks, one_block, 0)
        for i in range(2):
            groups[first + i].start()
        gain_sum = jnp.zeros((1, features), F32)
        shift_sum = jnp.zeros((1, features), F32)
        down_sum = jnp.zeros((1, features), F32)
        out_sum = jnp.zeros((1, features), F32)
        for index in range(5):
            load(layer, 2 + index, wide.at[index], 3 + index).start()
        load(layer, 8, lse, 9).start()
        for at in halves:
            down_sum = down_sum + jnp.sum(wide[5, at].astype(F32), axis=0, keepdims=True)
            back, gain_part, shift_part = norm_back(middle[at], line(5), total[at])
            mid_grad = grad[at] + back
            grad[at] = mid_grad
            mid_grad = mid_grad.astype(BF16)
            wide[5, at] = mid_grad
            out_sum = out_sum + jnp.sum(mid_grad.astype(F32), axis=0, keepdims=True)
            gain_sum, shift_sum = gain_sum + gain_part, shift_sum + shift_part
        load(layer, 7, exact, 8).start()
        if layer > 0:
            load(layer - 1, 9, middle, 0).start()
        note(5, gain_sum)
        note(6, shift_sum)
        note(7, down_sum)
        note(4, out_sum)

        load(layer, 1, weights, 2).wait()
        for at in halves:
            wide[5, at] = dot_nt(wide[5, at], weights[3]).astype(BF16)
        for index in range(5):
            load(layer, 2 + index, wide.at[index], 3 + index).wait()
        load(layer, 7, exact, 8).wait()
        load(layer, 8, lse, 9).wait()

        def far_copies(pair):
            at_lanes = pl.ds(pl.multiple_of(pair * LANES, LANES), LANES)
            return [
                remote(
                    wide.at[3 + i, :, at_lanes], wide.at[6 + i, :, at_lanes],
                    far_send.at[i, pair], far_recv.at[i, pair], to_core,
                )
                for i in range(2)
            ]

        def one_pair(pair, carry, first=first):
            attend_pair_back(pair, wide, exact, lse, bias)
            for copy in far_copies(pair):
                copy.start()
            pl.when(pair == 1)(groups[first].cross)
            pl.when(pair == 2)(groups[first + 1].cross)
            pl.when(pair == 4)(lambda: along_z(first))
            return carry

        pairs = features // LANES
        lax.fori_loop(0, pairs, one_pair, 0)
        grad_t[...] = jnp.transpose(exact[...]).astype(BF16)
        load(layer, 0, before, 1).wait()
        normed, unused = norm_parts(before[...])
        act_t[...] = jnp.transpose(normed * line(0) + line(1)).astype(BF16)
        note(2, jnp.sum(wide[0].astype(F32), axis=0, keepdims=True))
        along_z(first + 1)

        def wait_far(pair, carry):
            for copy in far_copies(pair):
                copy.wait()
            return carry

        lax.fori_loop(0, pairs, wait_far, 0)
        value_sum = jnp.zeros((1, features), F32)
        for at in halves:
            wide[1, at] = added(wide[1, at], wide[6, at])
            value_grad = added(wide[2, at], wide[7, at])
            wide[2, at] = value_grad
            value_sum = value_sum + jnp.sum(value_grad.astype(F32), axis=0, keepdims=True)
            wide[5, at] = grad[at].astype(BF16)
        note(3, value_sum)

        def split_places(a, at, value):
            for i in range(2):
                for j in range(2):
                    mine = jnp.where(core == 0, value[i, j, 0], value[i, j, 1])
                    others = jnp.where(core == 0, value[i, j, 1], value[i, j, 0])
                    part_attn[j, a, i, at] = mine
                    sent[j, a, i, at] = others

        for a in range(4):
            at = slice(a * 8 * owned, (a + 1) * 8 * owned)
            for i in range(2):
                pair_of = (
                    (dot_nn(act_t[at], wide[0]), dot_nn(act_t[at], wide[1]))
                    if i == 0
                    else (dot_nn(act_t[at], wide[2]), dot_nn(grad_t[at], wide[5]))
                )
                value = jnp.concatenate(
                    [one.reshape(2, 2, 2, owned, features) for one in pair_of], axis=3
                )
                split_places(a, slice(2 * owned * i, 2 * owned * (i + 1)), value.astype(BF16))
        to_sibling_block(2, sent, arrived_attn).start()
        for at in halves:
            act_grad = dot_nt(wide[0, at], weights[0])
            act_grad = act_grad + dot_nt(wide[1, at], weights[1])
            total[at] = act_grad + dot_nt(wide[2, at], weights[2])
        to_sibling_block(2, sent, arrived_attn).wait()

        def add_core(i, carry):
            a, b, c = i // 8, lax.rem(i // 2, 4), lax.rem(i, 2)
            part_attn[a, b, c] = added(part_attn[a, b, c], arrived_attn[a, b, c])
            return carry

        lax.fori_loop(0, 16, add_core, 0)
        groups[first + 2].start()
        if layer > 0:
            for copy in load_block(layer - 1, 0):
                copy.start()
        gain_sum = jnp.zeros((1, features), F32)
        shift_sum = jnp.zeros((1, features), F32)
        for at in halves:
            back, gain_part, shift_part = norm_back(before[at], line(0), total[at])
            grad[at] = grad[at] + back
            gain_sum, shift_sum = gain_sum + gain_part, shift_sum + shift_part
        note(0, gain_sum)
        note(1, shift_sum)

    wide[3, 0:slots] = grad[halves[1]].astype(BF16)
    swap_grad.start()
    groups[3 * layers - 1].cross()
    grad_t[...] = jnp.transpose(grad[...]).astype(BF16)
    side = features - LANES
    for i in range(2):
        position = lax.broadcasted_iota(jnp.int32, (slots, side), 1).astype(F32) + float(i * side)
        for at, pos in ((halves[0], pos_kept), (halves[1], pos_back)):
            column = jnp.transpose(jnp.broadcast_to(pos[0:1, 0:slots], (LANES, slots)))[:, 0:1]
            weights[i, at, 0:side] = (position == column).astype(F32).astype(BF16)
    lane = lax.broadcasted_iota(jnp.int32, (8, 1, features), 2)
    device = lax.broadcasted_iota(jnp.int32, (8, 1, features), 0)
    for a in range(4):
        at = slice(a * 8 * owned, (a + 1) * 8 * owned)
        left, right = (
            dot_nn(grad_t[at], weights[i, 0:rows, 0:side]).reshape(8, owned, side) for i in range(2)
        )
        own = jnp.where(lane // owned == device + 8 * a, lines[...][None], 0.0)
        narrow_rows = dot_nt(
            own.reshape(8 * layers * count, features).astype(BF16), spread_matrix(owned, features)
        ).reshape(8, layers * count, LANES)
        own = jnp.where(lane // (4 * owned) == device, up_lines[a][None], 0.0)
        up_rows_here = dot_nt(
            own.reshape(64, features).astype(BF16), spread_matrix(4 * owned, features)
        ).reshape(8, 8, LANES)
        spare = jnp.zeros((8, 2 * owned - layers * count - 8, LANES), F32)
        value = jnp.concatenate(
            [
                jnp.concatenate([left, right], axis=1),
                jnp.concatenate([narrow_rows, up_rows_here, spare], axis=1),
            ],
            axis=2,
        )
        value = value.astype(BF16).reshape(2, 2, 2, 2 * owned, features)
        for i in range(2):
            for j in range(2):
                mine = jnp.where(core == 0, value[i, j, 0], value[i, j, 1])
                others = jnp.where(core == 0, value[i, j, 1], value[i, j, 0])
                part_mlp[0, j, a, i, 0 : 2 * owned] = mine
                sent[j, a, i, 0 : 2 * owned] = others
    short = pl.ds(0, 2 * owned)
    send_table = to_sibling_block(3, sent.at[:, :, :, short], arrived.at[0, :, :, :, short])
    send_table.start()
    along_z(3 * layers - 1)
    send_table.wait()

    def add_table(i, carry):
        a, b, c = i // 8, lax.rem(i // 2, 4), lax.rem(i, 2)
        part_mlp[0, a, b, c, short] = added(part_mlp[0, a, b, c, short], arrived[0, a, b, c, short])
        return carry

    lax.fori_loop(0, 16, add_table, 0)
    table_group = groups[3 * layers]
    table_group.start()
    table_group.cross()
    along_z(3 * layers)
    table_group.finish()
    swap_final.wait()
    swap_grad.wait()


def backward(chip_cot, narrow, bias, pos_kept, pos_back, final, mlp_fulls, kept, count, owned, collective_id):
    layers = len(mlp_fulls)
    rows, features = final.shape
    deep = mlp_fulls[0].shape[4]
    up_rows = deep // 2
    wide = (rows, features)

    def like(shape, dtype):
        return jax.ShapeDtypeStruct(shape, dtype)

    out_shape = [like(wide, F32), like((rows // 2, features), F32), like((rows // 2, features), BF16)]
    for layer in range(layers):
        out_shape += [like((up_rows, features), F32)] * 2 + [like((4 * owned, features), F32)]
    out_shape.append(like((2 * owned, features), F32))
    most = max(up_rows, 4 * owned)
    half = most // 2
    places = (2, 4, 2, most, features)
    wide32 = pltpu.VMEM(wide, F32)
    turned = pltpu.VMEM((features, rows), BF16)
    groups = 3 * layers + 1
    scratch = [
        pltpu.VMEM((8,) + wide, BF16),
        wide32, wide32, wide32,
        pltpu.VMEM((rows, LANES), F32),
        pltpu.VMEM((4, features, features), BF16),
        pltpu.VMEM((2, 4, 2, deep, features), BF16),
        turned, turned,
        pltpu.VMEM(places, BF16),
        pltpu.VMEM((2,) + places, BF16),
        pltpu.VMEM(places, BF16),
        pltpu.VMEM((2,) + places, BF16),
        pltpu.VMEM(places, BF16),
        pltpu.VMEM((2, 4, 2, half, features), BF16),
        pltpu.VMEM((2, 2, 4, half, features), BF16),
        pltpu.VMEM((2, 2, 4, half, features), BF16),
        pltpu.VMEM((2, 3, most, features), BF16),
        pltpu.VMEM((layers * count, features), F32),
        pltpu.VMEM((4, 8, features), F32),
        pltpu.SemaphoreType.DMA((groups, 7)),
        pltpu.SemaphoreType.DMA((groups, 7)),
        dma_sems(4),
        dma_sems(4),
        pltpu.SemaphoreType.DMA((2, features // LANES)),
        pltpu.SemaphoreType.DMA((2, features // LANES)),
        dma_sems(2),
        dma_sems(2),
        dma_sems(10),
        dma_sems(6),
    ]
    flat = [ref for layer in kept for ref in layer]
    args = (chip_cot, narrow, bias, pos_kept, pos_back, final, *mlp_fulls, *flat)
    results = pl.pallas_call(
        functools.partial(backward_kernel, (layers, count, owned, up_rows)),
        out_shape=out_shape,
        in_specs=[vmem()] * 5 + [hbm()] * (len(args) - 5),
        out_specs=[vmem()] * len(out_shape),
        scratch_shapes=scratch,
        compiler_params=pltpu.CompilerParams(
            collective_id=collective_id, has_side_effects=True, vmem_limit_bytes=VMEM_LIMIT
        ),
        name="backward",
    )(*args)
    return results[:3], results[3:]


def split_rows(values):
    high = values.astype(BF16)
    rest = values - high.astype(F32)
    middle = rest.astype(BF16)
    return high, middle, (rest - middle.astype(F32)).astype(BF16)


def chip_shards(
    patches,
    clip_of_row,
    position_of_row,
    pos_embed,
    norm1_gain,
    norm1_bias,
    query_bias,
    value_bias,
    out_bias,
    norm2_gain,
    norm2_bias,
    up_bias,
    down_bias,
    qkv_weight,
    out_weight,
    up_weight,
    down_weight,
    cotangent,
):
    layers, owned, features = qkv_weight.shape[0], qkv_weight.shape[1], patches.shape[1]
    pieces = lax.axis_size("gy")
    piece_rows = patches.shape[0]
    devices = features // owned
    positions = pos_embed.shape[0]
    padded_positions = -(-positions // 256) * 256
    slots = -(-positions // pieces)
    slots = -(-slots // 16) * 16
    rows = 2 * slots
    hidden_width = up_weight.shape[2]
    up_rows = up_weight.shape[1]
    gy = lax.axis_index("gy")
    side, core = gy // 2, lax.rem(gy, 2)

    low_clip, high_clip = jnp.min(clip_of_row), jnp.max(clip_of_row)
    low_is_long = 2 * jnp.sum((clip_of_row == low_clip).astype(jnp.int32)) > clip_of_row.shape[0]
    long_clip = jnp.where(low_is_long, low_clip, high_clip)
    kept_all = ((clip_of_row == long_clip) == (side == 0)).reshape(pieces, piece_rows)
    kept_count = jnp.sum(kept_all.astype(jnp.int32), axis=1)
    kept = lax.dynamic_index_in_dim(kept_all, gy, 0, keepdims=False)
    rank_kept = jnp.cumsum(kept.astype(jnp.int32)) - 1
    rank_sent = jnp.arange(piece_rows, dtype=jnp.int32) - rank_kept - 1
    slot = jnp.arange(slots, dtype=jnp.int32)[:, None]
    pick_kept = (slot == rank_kept[None]) & kept[None]
    pick_sent = (slot == rank_sent[None]) & jnp.logical_not(kept)[None]
    choose = jnp.concatenate([pick_kept, pick_sent], axis=0)
    choose16 = choose.astype(BF16)
    sorted_positions = jnp.sum(jnp.where(choose, position_of_row[None], 0), axis=1).astype(F32)
    pos_kept, pos_sent = (
        jnp.broadcast_to(jnp.pad(part, (0, -slots % LANES))[None], (8, slots + -slots % LANES))
        for part in (sorted_positions[:slots], sorted_positions[slots:])
    )

    def slot_bias(of_core):
        mine = lax.dynamic_index_in_dim(kept_count, side * 2 + of_core, 0, keepdims=False)
        theirs = lax.dynamic_index_in_dim(kept_count, (1 - side) * 2 + of_core, 0, keepdims=False)
        steps = jnp.arange(slots, dtype=jnp.int32)
        used = jnp.concatenate([steps < mine, steps < theirs])
        return jnp.where(used, 0.0, MASKED)

    bias = jnp.concatenate([slot_bias(core), slot_bias(1 - core)]).astype(BF16)
    bias = jnp.broadcast_to(bias[:, None], (2 * rows, LANES))

    narrow = jnp.stack(
        [norm1_gain, norm1_bias, query_bias, value_bias, out_bias, norm2_gain, norm2_bias, down_bias],
        axis=1,
    )
    count = narrow.shape[1]
    small = jnp.concatenate(
        [
            jnp.pad(narrow.reshape(layers * count, owned), ((0, 0), (0, LANES - owned))),
            jnp.pad(up_bias, ((0, 8 - layers), (0, LANES - up_bias.shape[1]))),
        ],
        axis=0,
    )
    small = jnp.transpose(small.reshape(layers + 1, 8, LANES), (1, 0, 2)).reshape(8, -1)
    table_shard = jnp.concatenate(
        [
            jnp.pad(pos_embed.T, ((0, 0), (0, padded_positions - positions))),
            jnp.pad(small, ((0, 0), (0, padded_positions - small.shape[1]))),
        ],
        axis=0,
    )
    attn_shards, mlp_shards = [], []
    for layer in range(layers):
        qkv = jnp.transpose(qkv_weight[layer].reshape(owned, 3, features), (1, 0, 2))
        attn_shards.append(jnp.concatenate([qkv.reshape(3 * owned, features), out_weight[layer]], axis=0))
        mlp_shards.append(jnp.concatenate([up_weight[layer], down_weight[layer].T], axis=0))
    (state, chip_cotangent, pos_back, narrow_all, unused_up), mlp_fulls, stored = forward(
        choose16, patches, cotangent, pos_kept, pos_sent, bias, table_shard, attn_shards, mlp_shards,
        count, owned, 0,
    )
    (gradient, state_back, gradient_back), sums = backward(
        chip_cotangent, narrow_all, bias, pos_kept, pos_back, state, mlp_fulls, stored, count, owned, 1
    )

    def from_chip(values_own, values_back):
        both = jnp.concatenate([values_own, values_back], axis=0)
        parts = split_rows(both)
        return sum(dot_tn(choose16, part) for part in parts)

    activations = from_chip(state[:slots], state_back)
    input_grad = from_chip(gradient[:slots], gradient_back.astype(F32))
    table_sum = sums[-1]
    table_half = padded_positions // 2
    table_rows = jnp.concatenate(
        [table_sum[:owned, :table_half], table_sum[owned:, :table_half]], axis=1
    )
    pos_embed_grad = table_rows[:, :positions].T
    narrow_sum = table_sum[: layers * count, table_half : table_half + owned].reshape(layers, count, owned)
    up_bias_grad = table_sum[layers * count : layers * (count + 1), table_half : table_half + 4 * owned]
    up_sums, down_sums, attn_sums = ([sums[3 * (layers - 1 - layer) + i] for layer in range(layers)] for i in range(3))
    qkv_weight_grad = jnp.stack(
        [
            jnp.transpose(part[: 3 * owned].reshape(3, owned, features), (1, 0, 2)).reshape(owned, -1)
            for part in attn_sums
        ]
    )
    out_weight_grad = jnp.stack([part[3 * owned :] for part in attn_sums])
    up_weight_grad = jnp.stack(up_sums)
    down_weight_grad = jnp.stack([part.T for part in down_sums])
    return (
        activations,
        input_grad,
        pos_embed_grad,
        *(narrow_sum[:, i] for i in range(7)),
        up_bias_grad,
        narrow_sum[:, 7],
        qkv_weight_grad,
        out_weight_grad,
        up_weight_grad,
        down_weight_grad,
    )


def solution(mesh):
    return jax.shard_map(
        chip_shards if mesh.shape["gx"] == 8 and mesh.shape["gy"] == 4 else shards,
        mesh=mesh,
        in_specs=(
            P(("gx", "gy"), None),
            P("gx"),
            P(("gx", "gy")),
            P(None, ("gx", "gy")),
            P(None, ("gx", "gy")),
            P(None, ("gx", "gy")),
            P(None, ("gx", "gy")),
            P(None, ("gx", "gy")),
            P(None, ("gx", "gy")),
            P(None, ("gx", "gy")),
            P(None, ("gx", "gy")),
            P(None, ("gx", "gy")),
            P(None, ("gx", "gy")),
            P(None, ("gx", "gy"), None),
            P(None, ("gx", "gy"), None),
            P(None, "gx", "gy"),
            P(None, "gy", "gx"),
            P(("gx", "gy"), None),
        ),
        out_specs=(
            P(("gx", "gy"), None),
            P(("gx", "gy"), None),
            P(None, ("gx", "gy")),
            P(None, ("gx", "gy")),
            P(None, ("gx", "gy")),
            P(None, ("gx", "gy")),
            P(None, ("gx", "gy")),
            P(None, ("gx", "gy")),
            P(None, ("gx", "gy")),
            P(None, ("gx", "gy")),
            P(None, ("gx", "gy")),
            P(None, ("gx", "gy")),
            P(None, ("gx", "gy"), None),
            P(None, ("gx", "gy"), None),
            P(None, "gx", "gy"),
            P(None, "gy", "gx"),
        ),
        check_vma=False,
    )
```

```python
import functools
import math

import jax
import jax.numpy as jnp
from jax import lax
from jax.experimental import pallas as pl
from jax.experimental.pallas import tpu as pltpu
from jax.sharding import PartitionSpec as P

HEAD_DIM = 64


EPSILON = 1e-06
SQRT_HALF = 1.0 / math.sqrt(2.0)
NORMAL_PEAK = 1.0 / math.sqrt(2.0 * math.pi)
MASKED = -1e30


def layer_norm(values, norm_gain, norm_shift):
    row_mean = jnp.mean(values, axis=-1, keepdims=True)
    centred = values - row_mean
    row_var = jnp.mean(centred * centred, axis=-1, keepdims=True)
    return centred * lax.rsqrt(row_var + EPSILON) * norm_gain + norm_shift


def gelu_slope(pre_act):
    return (
        0.5 * (1.0 + lax.erf(pre_act * SQRT_HALF))
        + pre_act * jnp.exp(-0.5 * pre_act * pre_act) * NORMAL_PEAK
    )


def column_pair(matrix, pair_index, pair_width):
    block = lax.dynamic_slice_in_dim(matrix, pair_index * pair_width, pair_width, 1)
    return block.reshape(matrix.shape[0], 2, pair_width // 2)


def join_pairs(stacked):
    return jnp.transpose(stacked, (1, 0, 2)).reshape(
        stacked.shape[1], stacked.shape[0] * stacked.shape[2]
    )


def pair_scores(head_query, head_keys, same_clip):
    scores = jnp.einsum(
        "qhd,khd->hqk", head_query, head_keys, preferred_element_type=jnp.float32
    ) * HEAD_DIM ** (-0.5)
    return jnp.where(same_clip[None], scores, MASKED)


def pair_parts(head_query, head_keys, head_values, head_grad, same_clip, pair_total):
    scores = pair_scores(head_query, head_keys, same_clip)
    weights = jnp.exp(scores - pair_total)
    weight_grad = jnp.einsum(
        "qhd,khd->hqk", head_grad, head_values, preferred_element_type=jnp.float32
    )
    return (weights, weight_grad)


def attend(queries, key_rows, value_rows, same_clip):
    pair_width = 2 * HEAD_DIM
    pair_count = queries.shape[1] // pair_width

    def one_pair(pair_index):
        head_query = column_pair(queries, pair_index, pair_width)
        head_keys = column_pair(key_rows, pair_index, pair_width)
        head_values = column_pair(value_rows, pair_index, pair_width)
        scores = pair_scores(head_query, head_keys, same_clip)
        row_max = jnp.max(scores, axis=-1, keepdims=True)
        log_total = row_max + jnp.log(jnp.sum(jnp.exp(scores - row_max), axis=-1, keepdims=True))
        weights = jnp.exp(scores - log_total).astype(jnp.bfloat16)
        mixed = jnp.einsum("hqk,khd->qhd", weights, head_values, preferred_element_type=jnp.float32)
        return (mixed.reshape(queries.shape[0], pair_width), log_total)

    mixed, log_total = lax.map(one_pair, jnp.arange(pair_count))
    return (join_pairs(mixed), log_total)


def attend_back(queries, key_rows, value_rows, same_clip, log_total, mixed_grad):
    pair_width = 2 * HEAD_DIM
    pair_count = queries.shape[1] // pair_width
    score_scale = HEAD_DIM ** (-0.5)

    def one_pair(pair_inputs):
        pair_index, pair_total = pair_inputs
        head_query = column_pair(queries, pair_index, pair_width)
        head_keys = column_pair(key_rows, pair_index, pair_width)
        head_values = column_pair(value_rows, pair_index, pair_width)
        head_grad = column_pair(mixed_grad, pair_index, pair_width)
        weights, weight_grad = pair_parts(
            head_query, head_keys, head_values, head_grad, same_clip, pair_total
        )
        value_grad = jnp.einsum(
            "hqk,qhd->khd",
            weights.astype(jnp.bfloat16),
            head_grad,
            preferred_element_type=jnp.float32,
        )
        inner = jnp.sum(weights * weight_grad, axis=-1, keepdims=True)
        score_grad = (weights * (weight_grad - inner)).astype(jnp.bfloat16)
        query_grad = (
            jnp.einsum("hqk,khd->qhd", score_grad, head_keys, preferred_element_type=jnp.float32)
            * score_scale
        )
        key_grad = (
            jnp.einsum("hqk,qhd->khd", score_grad, head_query, preferred_element_type=jnp.float32)
            * score_scale
        )
        return (
            query_grad.reshape(queries.shape[0], pair_width),
            key_grad.reshape(key_rows.shape[0], pair_width),
            value_grad.reshape(key_rows.shape[0], pair_width),
        )

    query_grad, key_grad, value_grad = lax.map(one_pair, (jnp.arange(pair_count), log_total))
    return (join_pairs(query_grad), join_pairs(key_grad), join_pairs(value_grad))


def stacked_member(collected, member_index):
    return jnp.stack([entry[member_index] for entry in collected])


def shards(
    patches,
    clip_of_row,
    position_of_row,
    pos_embed,
    norm1_gain,
    norm1_bias,
    query_bias,
    value_bias,
    out_bias,
    norm2_gain,
    norm2_bias,
    up_bias,
    down_bias,
    qkv_weight,
    out_weight,
    up_weight,
    down_weight,
    cotangent,
):
    (
        position_table,
        gain_one,
        shift_one,
        bias_query,
        bias_value,
        bias_out,
        gain_two,
        shift_two,
        bias_up,
        bias_down,
        weight_qkv,
        weight_out,
    ) = (
        lax.all_gather(pos_embed, ("gx", "gy"), axis=1, tiled=True),
        lax.all_gather(norm1_gain, ("gx", "gy"), axis=1, tiled=True),
        lax.all_gather(norm1_bias, ("gx", "gy"), axis=1, tiled=True),
        lax.all_gather(query_bias, ("gx", "gy"), axis=1, tiled=True),
        lax.all_gather(value_bias, ("gx", "gy"), axis=1, tiled=True),
        lax.all_gather(out_bias, ("gx", "gy"), axis=1, tiled=True),
        lax.all_gather(norm2_gain, ("gx", "gy"), axis=1, tiled=True),
        lax.all_gather(norm2_bias, ("gx", "gy"), axis=1, tiled=True),
        lax.all_gather(up_bias, ("gx", "gy"), axis=1, tiled=True),
        lax.all_gather(down_bias, ("gx", "gy"), axis=1, tiled=True),
        lax.all_gather(qkv_weight, ("gx", "gy"), axis=1, tiled=True),
        lax.all_gather(out_weight, ("gx", "gy"), axis=1, tiled=True),
    )
    block_up, block_down = (
        lax.all_gather(up_weight, "gx", axis=1, tiled=True),
        lax.all_gather(down_weight, "gx", axis=2, tiled=True),
    )
    layer_count = qkv_weight.shape[0]
    features = patches.shape[1]
    row_count = patches.shape[0]
    hidden_width = block_up.shape[2]
    member = lax.axis_index("gy")
    hidden_start = member * hidden_width
    own_clip = lax.dynamic_slice_in_dim(clip_of_row, member * row_count, row_count)
    same_clip = own_clip[:, None] == clip_of_row[None, :]
    state = patches.astype(jnp.float32) + position_table[position_of_row].astype(jnp.float32)
    stored = []
    for layer_index in range(layer_count):
        norm_gain_one = gain_one[layer_index].astype(jnp.float32)
        norm_shift_one = shift_one[layer_index].astype(jnp.float32)
        act_one = layer_norm(state, norm_gain_one, norm_shift_one).astype(jnp.bfloat16)
        projected = jnp.dot(act_one, weight_qkv[layer_index], preferred_element_type=jnp.float32)
        queries = (projected[:, :features] + bias_query[layer_index].astype(jnp.float32)).astype(
            jnp.bfloat16
        )
        key_rows = projected[:, features : 2 * features].astype(jnp.bfloat16)
        value_rows = (
            projected[:, 2 * features :] + bias_value[layer_index].astype(jnp.float32)
        ).astype(jnp.bfloat16)
        all_keys, all_values = (
            lax.all_gather(key_rows, "gy", axis=0, tiled=True),
            lax.all_gather(value_rows, "gy", axis=0, tiled=True),
        )
        mixed, log_total = attend(queries, all_keys, all_values, same_clip)
        attended = mixed.astype(jnp.bfloat16)
        middle = (
            state
            + jnp.dot(attended, weight_out[layer_index], preferred_element_type=jnp.float32)
            + bias_out[layer_index].astype(jnp.float32)
        )
        norm_gain_two = gain_two[layer_index].astype(jnp.float32)
        norm_shift_two = shift_two[layer_index].astype(jnp.float32)
        act_two = layer_norm(middle, norm_gain_two, norm_shift_two).astype(jnp.bfloat16)
        up_columns = lax.dynamic_slice_in_dim(
            bias_up[layer_index], hidden_start, hidden_width
        ).astype(jnp.float32)
        mlp_rows = lax.all_gather(act_two, "gy", axis=0, tiled=True)
        pre_act = (
            jnp.dot(mlp_rows, block_up[layer_index], preferred_element_type=jnp.float32)
            + up_columns
        )
        hidden = jax.nn.gelu(pre_act, approximate=False).astype(jnp.bfloat16)
        partial_out = jnp.dot(hidden, block_down[layer_index], preferred_element_type=jnp.float32)
        mlp_out = lax.psum_scatter(
            partial_out.astype(jnp.bfloat16), "gy", scatter_dimension=0, tiled=True
        ).astype(jnp.float32)
        stored.append(
            (
                state,
                act_one,
                queries,
                key_rows,
                value_rows,
                all_keys,
                all_values,
                log_total,
                attended,
                middle,
                mlp_rows,
                pre_act,
                hidden,
            )
        )
        state = middle + mlp_out + bias_down[layer_index].astype(jnp.float32)
    gradient = cotangent.astype(jnp.float32)
    collected = [None] * layer_count
    for layer_index in reversed(range(layer_count)):
        (
            layer_input,
            act_one,
            queries,
            key_rows,
            value_rows,
            kept_keys,
            kept_values,
            log_total,
            attended,
            middle,
            mlp_rows,
            pre_act,
            hidden,
        ) = stored[layer_index]
        grad_two = gradient.astype(jnp.bfloat16)
        down_bias_part = jnp.sum(grad_two.astype(jnp.float32), axis=0)
        grad_rows = lax.all_gather(grad_two, "gy", axis=0, tiled=True)
        down_part = jnp.einsum("rf,rd->fd", hidden, grad_rows, preferred_element_type=jnp.float32)
        hidden_grad = jnp.einsum(
            "rd,fd->rf", grad_rows, block_down[layer_index], preferred_element_type=jnp.float32
        )
        pre_grad = (hidden_grad * gelu_slope(pre_act)).astype(jnp.bfloat16)
        up_part = jnp.einsum("rd,rf->df", mlp_rows, pre_grad, preferred_element_type=jnp.float32)
        up_columns_grad = jnp.sum(pre_grad.astype(jnp.float32), axis=0)
        up_bias_part = lax.dynamic_update_slice_in_dim(
            jnp.zeros((bias_up.shape[1],), jnp.float32), up_columns_grad, hidden_start, 0
        )
        rows_grad = jnp.einsum(
            "rf,df->rd", pre_grad, block_up[layer_index], preferred_element_type=jnp.float32
        )
        act_two_grad = lax.psum_scatter(
            rows_grad.astype(jnp.bfloat16), "gy", scatter_dimension=0, tiled=True
        ).astype(jnp.float32)
        norm_gain_two = gain_two[layer_index].astype(jnp.float32)
        norm_shift_two = shift_two[layer_index].astype(jnp.float32)
        unused_two, norm_two_pull = jax.vjp(layer_norm, middle, norm_gain_two, norm_shift_two)
        middle_part, gain_two_part, shift_two_part = norm_two_pull(act_two_grad)
        mid_grad = gradient + middle_part
        grad_one = mid_grad.astype(jnp.bfloat16)
        out_bias_part = jnp.sum(grad_one.astype(jnp.float32), axis=0)
        out_part = jnp.einsum("rd,re->de", attended, grad_one, preferred_element_type=jnp.float32)
        mixed_grad = jnp.einsum(
            "re,de->rd", grad_one, weight_out[layer_index], preferred_element_type=jnp.float32
        ).astype(jnp.bfloat16)
        query_grad, key_grad, value_grad = attend_back(
            queries, kept_keys, kept_values, same_clip, log_total, mixed_grad
        )
        key_grad, value_grad = (
            lax.psum_scatter(
                key_grad.astype(jnp.bfloat16), "gy", scatter_dimension=0, tiled=True
            ).astype(jnp.float32),
            lax.psum_scatter(
                value_grad.astype(jnp.bfloat16), "gy", scatter_dimension=0, tiled=True
            ).astype(jnp.float32),
        )
        qkv_grad = jnp.concatenate(
            [
                query_grad.astype(jnp.bfloat16),
                key_grad.astype(jnp.bfloat16),
                value_grad.astype(jnp.bfloat16),
            ],
            axis=1,
        )
        query_bias_part = jnp.sum(qkv_grad[:, :features].astype(jnp.float32), axis=0)
        value_bias_part = jnp.sum(qkv_grad[:, 2 * features :].astype(jnp.float32), axis=0)
        qkv_part = jnp.einsum("rd,re->de", act_one, qkv_grad, preferred_element_type=jnp.float32)
        act_one_grad = jnp.einsum(
            "re,de->rd", qkv_grad, weight_qkv[layer_index], preferred_element_type=jnp.float32
        )
        norm_gain_one = gain_one[layer_index].astype(jnp.float32)
        norm_shift_one = shift_one[layer_index].astype(jnp.float32)
        unused_one, norm_one_pull = jax.vjp(layer_norm, layer_input, norm_gain_one, norm_shift_one)
        input_part, gain_one_part, shift_one_part = norm_one_pull(act_one_grad)
        gradient = mid_grad + input_part
        collected[layer_index] = (
            gain_one_part,
            shift_one_part,
            query_bias_part,
            value_bias_part,
            out_bias_part,
            gain_two_part,
            shift_two_part,
            up_bias_part,
            down_bias_part,
            qkv_part,
            out_part,
            up_part,
            down_part,
        )
    table_part = jax.ops.segment_sum(
        gradient, position_of_row, num_segments=position_table.shape[0]
    )
    (
        pos_embed_grad,
        norm1_gain_grad,
        norm1_bias_grad,
        query_bias_grad,
        value_bias_grad,
        out_bias_grad,
        norm2_gain_grad,
        norm2_bias_grad,
        up_bias_grad,
        down_bias_grad,
        qkv_weight_grad,
        out_weight_grad,
    ) = (
        lax.psum_scatter(table_part, ("gx", "gy"), scatter_dimension=1, tiled=True),
        lax.psum_scatter(
            stacked_member(collected, 0), ("gx", "gy"), scatter_dimension=1, tiled=True
        ),
        lax.psum_scatter(
            stacked_member(collected, 1), ("gx", "gy"), scatter_dimension=1, tiled=True
        ),
        lax.psum_scatter(
            stacked_member(collected, 2), ("gx", "gy"), scatter_dimension=1, tiled=True
        ),
        lax.psum_scatter(
            stacked_member(collected, 3), ("gx", "gy"), scatter_dimension=1, tiled=True
        ),
        lax.psum_scatter(
            stacked_member(collected, 4), ("gx", "gy"), scatter_dimension=1, tiled=True
        ),
        lax.psum_scatter(
            stacked_member(collected, 5), ("gx", "gy"), scatter_dimension=1, tiled=True
        ),
        lax.psum_scatter(
            stacked_member(collected, 6), ("gx", "gy"), scatter_dimension=1, tiled=True
        ),
        lax.psum_scatter(
            stacked_member(collected, 7), ("gx", "gy"), scatter_dimension=1, tiled=True
        ),
        lax.psum_scatter(
            stacked_member(collected, 8), ("gx", "gy"), scatter_dimension=1, tiled=True
        ),
        lax.psum_scatter(
            stacked_member(collected, 9), ("gx", "gy"), scatter_dimension=1, tiled=True
        ),
        lax.psum_scatter(
            stacked_member(collected, 10), ("gx", "gy"), scatter_dimension=1, tiled=True
        ),
    )
    up_stack = stacked_member(collected, 11)
    down_stack = stacked_member(collected, 12)
    up_weight_grad, down_weight_grad = (
        lax.psum_scatter(
            up_stack.astype(jnp.bfloat16), "gx", scatter_dimension=1, tiled=True
        ).astype(jnp.float32),
        lax.psum_scatter(
            down_stack.astype(jnp.bfloat16), "gx", scatter_dimension=2, tiled=True
        ).astype(jnp.float32),
    )
    return (
        state,
        gradient,
        pos_embed_grad,
        norm1_gain_grad,
        norm1_bias_grad,
        query_bias_grad,
        value_bias_grad,
        out_bias_grad,
        norm2_gain_grad,
        norm2_bias_grad,
        up_bias_grad,
        down_bias_grad,
        qkv_weight_grad,
        out_weight_grad,
        up_weight_grad,
        down_weight_grad,
    )


LOG2_E = 1.0 / math.log(2.0)
LANES = 128
BF16 = jnp.bfloat16
F32 = jnp.float32
MESH_ID = pl.DeviceIdType.MESH
VMEM_LIMIT = 60 * 1024 * 1024


def dot_nn(left, right):
    return lax.dot_general(left, right, (((1,), (0,)), ((), ())), preferred_element_type=F32)


def dot_nt(left, right):
    return lax.dot_general(left, right, (((1,), (1,)), ((), ())), preferred_element_type=F32)


def dot_tn(left, right):
    return lax.dot_general(left, right, (((0,), (0,)), ((), ())), preferred_element_type=F32)


def my_place():
    gx = lax.axis_index("gx")
    gy = lax.axis_index("gy")
    return gx // 2, lax.rem(gx, 2), gy // 2, lax.rem(gy, 2)


def device_at(z, x, y, core):
    return (z * 2 + x, y * 2 + core)


class Copy:
    def __init__(self, describe):
        self.describe = describe

    def start(self):
        self.describe().start()

    def wait(self):
        self.describe().wait()

    def wait_recv(self):
        self.describe().wait_recv()

    def wait_send(self):
        self.describe().wait_send()


def z_partners(place):
    z, x, y, core = place
    return [3 - z, lax.rem(z + 2, 4), z + 1 - 2 * lax.rem(z, 2)]


def remote(src, dst, send_sem, recv_sem, device):
    return Copy(
        lambda: pltpu.make_async_remote_copy(
            src_ref=src,
            dst_ref=dst,
            send_sem=send_sem,
            recv_sem=recv_sem,
            device_id=device,
            device_id_type=MESH_ID,
        )
    )


def local_copy(src, dst, sem):
    return Copy(lambda: pltpu.make_async_copy(src, dst, sem))


def full_at(ref, order, z, x, y, core, *rest):
    place = (z, x, y, core) if order == "zxy" else (y, core, z, x)
    return ref.at[(*place, *rest)]


def hbm():
    return pl.BlockSpec(memory_space=pl.ANY)


def vmem():
    return pl.BlockSpec(memory_space=pltpu.VMEM)


def dma_sems(count):
    return pltpu.SemaphoreType.DMA((count,))


def added(left, right):
    return (left.astype(F32) + right.astype(F32)).astype(BF16)


def greet_signal(place):
    z, x, y, core = place
    barrier = pltpu.get_barrier_semaphore()
    others = [device_at(lax.rem(z + k, 4), x, y, core) for k in (1, 2, 3)]
    others += [device_at(z, 1 - x, y, core), device_at(z, x, 1 - y, core)]
    others += [device_at(z, x, y, 1 - core)]
    for other in others:
        pl.semaphore_signal(barrier, inc=1, device_id=other, device_id_type=MESH_ID)


def greet_wait():
    pl.semaphore_wait(pltpu.get_barrier_semaphore(), 6)


def lane_marks(head):
    lane = lax.broadcasted_iota(jnp.int32, (1, LANES), 1)
    own = (lane // HEAD_DIM == head).astype(F32)
    spare = HEAD_DIM * (1 - head)
    return lane, own, spare


def split_three(column):
    high = column.astype(BF16).astype(F32)
    rest = column - high
    middle = rest.astype(BF16).astype(F32)
    return high, middle, rest - middle


def norm_parts(values):
    row_mean = jnp.mean(values, axis=-1, keepdims=True)
    centred = values - row_mean
    row_var = jnp.mean(centred * centred, axis=-1, keepdims=True)
    rstd = lax.rsqrt(row_var + EPSILON)
    return centred * rstd, rstd


def norm_back(values, gain, grad):
    normed, rstd = norm_parts(values)
    scaled = grad * gain
    first = jnp.mean(scaled, axis=-1, keepdims=True)
    second = jnp.mean(scaled * normed, axis=-1, keepdims=True)
    back = (scaled - first - normed * second) * rstd
    return back, jnp.sum(grad * normed, axis=0, keepdims=True), jnp.sum(grad, axis=0, keepdims=True)


class Gather:
    def __init__(self, place, shard, full, order, start, rows, send, recv, local, z_first=True):
        z, x, y, core = place
        split = rows // 32 * 16 if rows % 32 == 0 else rows - 16
        every = slice(None)
        both, low, high = pl.ds(start, rows), pl.ds(start, split), pl.ds(start + split, rows - split)

        def at(*where):
            return full_at(full, order, *where)

        def copy(slot, src, dst, device):
            return remote(src, dst, send.at[slot], recv.at[slot], device)

        def same(slot, ref, device):
            return copy(slot, ref, ref, device)

        to_x, to_y = device_at(z, 1 - x, y, core), device_at(z, x, 1 - y, core)
        own = at(z, x, y, core, both)
        self.keep = local_copy(shard.at[both], own, local)
        source = shard.at[both] if z_first else at(z, every, every, core, both)
        target = own if z_first else source
        self.along_z = [
            copy(k, source, target, device_at(to_z, x, y, core))
            for k, to_z in enumerate(z_partners(place))
        ]
        depth = every if z_first else z
        self.first = [
            same(3, at(depth, x, y, core, low), to_x),
            same(4, at(depth, x, y, core, high), to_y),
        ]
        self.second = [
            same(5, at(depth, every, y, core, low), to_y),
            same(6, at(depth, x, every, core, high), to_x),
        ]
        self.third = [same(7, at(every, every, every, core, both), device_at(z, x, y, 1 - core))]
        parts = [self.along_z, self.first, self.second] if z_first else [self.first, self.second, self.along_z]
        self.stages = [*parts, self.third]

    def start(self):
        self.keep.start()
        if self.stages[0] is self.first:
            self.keep.wait()
        for copy in self.stages[0]:
            copy.start()

    def advance(self, stage):
        if self.stages[stage - 1] is self.along_z and stage == 1:
            self.keep.wait()
        for copy in self.stages[stage - 1]:
            copy.wait_recv()
        for copy in self.stages[stage]:
            copy.start()

    def finish(self):
        for copy in self.third:
            copy.wait_recv()

    def drain(self):
        for stage in self.stages:
            for copy in stage:
                copy.wait_send()


def spread_matrix(width, columns):
    row = lax.broadcasted_iota(jnp.int32, (LANES, columns), 0)
    lane = lax.broadcasted_iota(jnp.int32, (LANES, columns), 1)
    return (row == lax.rem(lane, width)).astype(F32).astype(BF16)


def pack_table(shard, table_columns, narrow, up_bias):
    layers, owned = narrow[0].shape
    width = shard.shape[1]
    pieces = []
    for layer in range(layers):
        rows = jnp.concatenate([ref[layer : layer + 1].astype(F32) for ref in narrow], axis=0)
        pieces.append(jnp.concatenate([rows, jnp.zeros((8, LANES - owned), F32)], axis=1))
    rows = jnp.concatenate([up_bias[...].astype(F32), jnp.zeros((8 - layers, up_bias.shape[1]), F32)], axis=0)
    pieces.append(jnp.concatenate([rows, jnp.zeros((8, LANES - up_bias.shape[1]), F32)], axis=1))
    pieces.append(jnp.zeros((8, width - LANES * (layers + 1)), F32))
    below = jnp.concatenate(pieces, axis=1)
    shard[...] = jnp.concatenate([table_columns[...].astype(F32), below], axis=0).astype(BF16)


def sort_rows(place, clips, positions, choose, bias, pos_kept, pos_sent):
    z, x, y, core = place
    pieces, piece_rows = clips.shape
    slots = choose.shape[0] // 2
    clip = clips[...].astype(F32)
    low = jnp.min(jnp.min(clip, axis=1, keepdims=True), axis=0, keepdims=True)
    high = jnp.max(jnp.max(clip, axis=1, keepdims=True), axis=0, keepdims=True)
    is_low = (clip == low).astype(F32)
    low_rows = jnp.sum(jnp.sum(is_low, axis=1, keepdims=True), axis=0, keepdims=True)
    long_clip = jnp.where(2.0 * low_rows > float(pieces * piece_rows), low, high)
    is_long = (clip == long_clip).astype(F32)
    kept = jnp.where(y == 0, is_long, 1.0 - is_long)
    kept_rows = jnp.sum(kept, axis=1, keepdims=True)
    piece = lax.broadcasted_iota(jnp.int32, (pieces, 1), 0)

    def of_piece(values, index):
        return jnp.sum(jnp.where(piece == index, values, 0.0), axis=0, keepdims=True)

    slot = lax.broadcasted_iota(jnp.int32, (slots, LANES), 0).astype(F32)
    for i, index in enumerate(
        (y * 2 + core, (1 - y) * 2 + core, y * 2 + 1 - core, (1 - y) * 2 + 1 - core)
    ):
        used = slot < of_piece(kept_rows, index)
        bias[i * slots : (i + 1) * slots] = jnp.where(used, 0.0, MASKED).astype(BF16)
    own = of_piece(kept, y * 2 + core)
    before = lax.broadcasted_iota(jnp.int32, (piece_rows, piece_rows), 0)
    after = lax.broadcasted_iota(jnp.int32, (piece_rows, piece_rows), 1)
    rank = dot_nn(
        jnp.broadcast_to(own, (8, piece_rows)).astype(BF16), (before <= after).astype(F32).astype(BF16)
    )[0:1]
    index = lax.broadcasted_iota(jnp.int32, (1, piece_rows), 1).astype(F32)
    target = jnp.where(own > 0.5, rank - 1.0, index - rank + float(slots))
    spot = lax.broadcasted_iota(jnp.int32, (2 * slots, piece_rows), 0).astype(F32)
    choose[...] = jnp.zeros_like(choose)
    choose[:, 0:piece_rows] = (spot == target).astype(F32).astype(BF16)
    position = positions[...].astype(F32)
    coarse = jnp.floor(position * (1.0 / 32.0))
    rows = lax.broadcasted_iota(jnp.int32, (8, piece_rows), 0)
    digits = jnp.where(rows == 0, coarse, position - 32.0 * coarse).astype(BF16)
    for at, out in ((slice(0, slots), pos_kept), (slice(slots, 2 * slots), pos_sent)):
        found = dot_nt(digits, choose[at, 0:piece_rows])
        out[:, 0:slots] = jnp.broadcast_to(32.0 * found[0:1] + found[1:2], (8, slots))


def forward_kernel(sizes, *refs):
    layers, count, owned, up_rows = sizes
    (clips, positions, patches, cotangent, table_columns), refs = refs[:5], refs[5:]
    narrow_in, refs = refs[:count], refs[count:]
    (up_bias_in, qkv_in, out_in, up_in, down_in), refs = refs[:5], refs[5:]
    (final, chip_cot, pos_kept, pos_back, narrow, up_bias, choose, bias), refs = refs[:8], refs[8:]
    mlp_fulls, refs = refs[:layers], refs[layers:]
    kept, refs = refs[: 12 * layers], refs[12 * layers :]
    (
        table_full, attn_full, table, weights, mlp_block, sorted_rows, arrived_rows, middle, act, query,
        key, value, key_sib, value_sib, exact, mixed, lse, hidden, slope, keys, values,
        pos_sent, table_shard, attn_shards, mlp_shards,
        send, recv, local, swap_send, swap_recv, save_sem, load_sem,
    ) = refs
    state = final
    place = my_place()
    z, x, y, core = place
    rows, features = state.shape
    slots = rows // 2
    halves = [slice(0, slots), slice(slots, rows)]
    blocks = mlp_fulls[0].shape[0] * mlp_fulls[0].shape[1]
    to_y, to_core = device_at(z, x, 1 - y, core), device_at(z, x, y, 1 - core)
    score_scale = HEAD_DIM ** (-0.5) * LOG2_E

    def gather(slot, shard, full, order, start, size, z_first=True):
        return Gather(
            place, shard, full, order, start, size, send.at[slot], recv.at[slot], local.at[slot], z_first
        )

    gathers = [gather(0, table_shard, table_full, "zxy", 0, table_shard.shape[0])]
    for layer in range(layers):
        slot = 1 + 3 * layer
        gathers.append(gather(slot, attn_shards.at[layer], attn_full.at[layer], "zxy", 0, 4 * owned))
        for part in range(2):
            last_half = up_rows // 2 if layer == layers - 1 and part == 1 else 0
            gathers.append(
                gather(
                    slot + 1 + part, mlp_shards.at[layer], mlp_fulls[layer], "yzx", part * up_rows,
                    up_rows - last_half,
                )
            )
            if last_half:
                gathers.append(
                    gather(
                        slot + 2 + part, mlp_shards.at[layer], mlp_fulls[layer], "yzx",
                        (part + 1) * up_rows - last_half, last_half, False,
                    )
                )
    def swap(slot, src, dst, device):
        return remote(src, dst, swap_send.at[slot], swap_recv.at[slot], device)

    start_table, start_attn = gathers[0], gathers[1]
    side_gather = gathers[-1]
    greet_signal(place)
    pack_table(table_shard, table_columns, narrow_in, up_bias_in)
    greet_wait()
    start_table.start()
    for layer in range(layers):
        at = up_in.shape[1]
        mlp_shards[layer, 0:at] = up_in[layer]
        mlp_shards[layer, at:] = jnp.transpose(down_in[layer].astype(F32)).astype(BF16)
        parts = [qkv_in[layer, :, i * features : (i + 1) * features] for i in range(3)]
        parts = [part.astype(F32) for part in (*parts, out_in[layer])]
        attn_shards[layer] = jnp.concatenate(parts, axis=0).astype(BF16)
    sort_rows(place, clips, positions, choose, bias, pos_kept, pos_sent)
    piece_rows = patches.shape[0]
    sorted_rows[...] = dot_nn(choose[:, 0:piece_rows], patches[...]).astype(BF16)
    send_pos = swap(0, pos_sent, pos_back, to_y)
    send_pos.start()
    send_rows = swap(1, sorted_rows.at[halves[1]], arrived_rows, to_y)
    send_rows.start()
    side_gather.start()
    chip_cot[halves[0]] = dot_nn(choose[halves[0], 0:piece_rows], cotangent[...]).astype(BF16)
    start_table.advance(1)
    start_attn.start()
    side_gather.advance(1)
    start_table.advance(2)
    start_table.advance(3)
    start_attn.advance(1)
    gathers[2].start()
    send_pos.wait()
    send_rows.wait()
    start_table.finish()

    devices = 32
    for a in range(4):
        block = table_full[a].reshape(8, owned + 8, table.shape[1]).astype(F32)
        table[a * 8 * owned : (a + 1) * 8 * owned] = (
            block[:, :owned].reshape(8 * owned, table.shape[1]).astype(BF16)
        )
    lane = lax.broadcasted_iota(jnp.int32, (devices, 1, features), 2)
    device = lax.broadcasted_iota(jnp.int32, (devices, 1, features), 0)
    for b in range(3):
        width = owned if b < 2 else 4 * owned
        packed = table_full[:, :, :, :, owned:, b * LANES : (b + 1) * LANES]
        packed = packed.reshape(devices * 8, LANES)
        wide = dot_nn(packed, spread_matrix(width, features)).reshape(devices, 8, features)
        if b < 2:
            wide = jnp.where(lane // owned == device, wide, 0.0)
            narrow[8 * b : 8 * b + 8] = jnp.sum(wide, axis=0)
        else:
            wide = jnp.where(lane // width == lax.rem(device, 8), wide, 0.0)
            up_bias[...] = jnp.sum(wide.reshape(4, 8, 8, features), axis=1)

    start_attn.advance(2)
    position = lax.broadcasted_iota(jnp.int32, (slots, table.shape[1]), 1).astype(F32)
    for at, pos, row_ref in ((halves[0], pos_kept, sorted_rows), (halves[1], pos_back, arrived_rows)):
        column = jnp.transpose(jnp.broadcast_to(pos[0:1, 0:slots], (LANES, slots)))[:, 0:1]
        lookup = (position == column).astype(F32).astype(BF16)
        state[at] = row_ref[0:slots].astype(F32) + dot_nt(lookup, table[...])

    def save(layer, index, ref):
        return local_copy(ref, kept[12 * layer + index], save_sem.at[index])

    def save_block(layer, index, block):
        ref = (hidden, slope)[index - 10].at[lax.rem(block, 2)]
        return local_copy(ref, kept[12 * layer + index].at[block], save_sem.at[index + 2 * lax.rem(block, 2)])

    def load_block(layer, block):
        slot = lax.rem(block, 2)
        return local_copy(
            mlp_fulls[layer].at[block // 2, lax.rem(block, 2)], mlp_block.at[slot], load_sem.at[slot]
        )

    def attend_pair(pair, layer):
        at_lanes = pl.ds(pl.multiple_of(pair * LANES, LANES), LANES)
        values[halves[0]] = value[halves[0], at_lanes]
        values[halves[1]] = value[halves[1], at_lanes]
        values[rows : rows + slots] = value_sib[layer, halves[0], at_lanes]
        values[rows + slots :] = value_sib[layer, halves[1], at_lanes]
        lanes = lax.broadcasted_iota(jnp.int32, (1, LANES), 1)
        results = [[], []]
        totals = [[], []]
        for head in range(2):
            lane, own, spare = lane_marks(head)
            own16 = own.astype(BF16)
            at_spare = (lane == spare).astype(BF16)
            keys[0:rows] = key[:, at_lanes] * own16 + bias[0:rows] * at_spare
            keys[rows:] = key_sib[layer, :, at_lanes] * own16 + bias[rows:] * at_spare
            for at in halves:
                scores = dot_nt(query[at, at_lanes] * own16 + at_spare, keys[...])
                top = jnp.max(scores, axis=-1, keepdims=True)
                weight = jnp.exp2(scores - top)
                total = jnp.sum(weight, axis=-1, keepdims=True)
                results[head].append(dot_nn(weight.astype(BF16), values[...]) * (1.0 / total))
                totals[head].append(top + jnp.log2(total))
        for index, at in enumerate(halves):
            both = jnp.where(lanes < HEAD_DIM, results[0][index], results[1][index])
            mixed[at, at_lanes] = both.astype(BF16)
            exact[at, at_lanes] = both
            held = lse[at]
            held = jnp.where(lanes == 2 * pair, totals[0][index], held)
            lse[at] = jnp.where(lanes == 2 * pair + 1, totals[1][index], held)

    def saved_refs(layer):
        return (query, key, value, key_sib.at[layer], value_sib.at[layer], exact)

    lse[...] = jnp.zeros_like(lse)
    for layer in range(layers):
        after = layer > 0
        base = count * layer

        def line(index):
            return narrow[base + index : base + index + 1]

        save(layer, 0, state).start()
        for at in halves:
            normed, unused = norm_parts(state[at])
            act[at] = (normed * line(0) + line(1)).astype(BF16)
        attn, up, down = gathers[1 + 3 * layer : 4 + 3 * layer]
        if not after:
            up.advance(1)
            down.start()
            up.advance(2)
            attn.advance(3)
            down.advance(1)
            gathers[4].start()
        attn.finish()
        if after:
            save(layer - 1, 1, weights).wait()
        for a in range(4):
            block = attn_full[layer, a].reshape(8, 4 * owned, features).astype(F32)
            for index in range(4):
                part = block[:, index * owned : (index + 1) * owned].reshape(8 * owned, features)
                weights[index, a * 8 * owned : (a + 1) * 8 * owned] = part.astype(BF16)
        save(layer, 1, weights).start()
        if after:
            for index in range(2, 8):
                save(layer - 1, index, saved_refs(layer - 1)[index - 2]).wait()
            save(layer - 1, 8, lse).wait()
        for at in halves:
            key[at] = dot_nn(act[at], weights[1]).astype(BF16)
        swap(2 + 2 * layer, key, key_sib.at[layer], to_core).start()
        for at in halves:
            value[at] = (dot_nn(act[at], weights[2]) + line(3)).astype(BF16)
        swap(3 + 2 * layer, value, value_sib.at[layer], to_core).start()
        for at in halves:
            query[at] = ((dot_nn(act[at], weights[0]) + line(2)) * score_scale).astype(BF16)
        swap(2 + 2 * layer, key, key_sib.at[layer], to_core).wait()
        swap(3 + 2 * layer, value, value_sib.at[layer], to_core).wait()

        def one_pair(pair, carry, layer=layer, up=up, down=down):
            attend_pair(pair, layer)
            if layer == 0:

                @pl.when(pair == 0)
                def _():
                    down.advance(2)
                    up.advance(3)
                    gathers[4].advance(1)
                    gathers[5].start()

                @pl.when(pair == 4)
                def _():
                    gathers[5].advance(1)
                    gathers[6].start()
                    side_gather.advance(2)

            else:

                @pl.when(pair == 0)
                def _():
                    down.advance(2)
                    up.advance(3)

                @pl.when(pair == 2)
                def _():
                    side_gather.advance(3)
                    down.advance(3)

            return carry

        lax.fori_loop(0, features // LANES, one_pair, 0)
        for index in range(2, 8):
            save(layer, index, saved_refs(layer)[index - 2]).start()
        save(layer, 8, lse).start()
        if after:
            save(layer - 1, 9, middle).wait()
        for at in halves:
            total = state[at] + dot_nn(mixed[at], weights[3]) + line(4)
            middle[at] = total
            normed, unused = norm_parts(total)
            act[at] = (normed * line(5) + line(6)).astype(BF16)
        save(layer, 9, middle).start()
        save(layer, 0, state).wait()
        for at in halves:
            state[at] = middle[at] + line(7)
        if layer == 0:
            gathers[4].advance(2)
            down.advance(3)
        up.finish()
        down.finish()
        if layer == layers - 1:
            side_gather.finish()
        load_block(layer, 0).start()
        if layer == layers - 1:
            sorted_back = swap(2 + 2 * layers, sorted_rows.at[halves[1]], chip_cot.at[halves[1]], to_y)
            sorted_rows[halves[1]] = dot_nn(choose[halves[1], 0:piece_rows], cotangent[...]).astype(BF16)
            sorted_back.start()

        def one_block(block, carry, layer=layer):
            slot = lax.rem(block, 2)
            pl.when(block + 1 < blocks)(lambda: load_block(layer, block + 1).start())
            load_block(layer, block).wait()

            @pl.when(block >= 2)
            def _():
                save_block(layer, 10, block - 2).wait()
                save_block(layer, 11, block - 2).wait()

            weight_up = mlp_block[slot, :, :, 0:up_rows, :].reshape(features, features)
            weight_down = mlp_block[slot, :, :, up_rows:, :].reshape(features, features)
            shift = up_bias[block, layer : layer + 1]
            for at in halves:
                pre_act = dot_nn(act[at], weight_up) + shift
                below = 0.5 * (1.0 + lax.erf(pre_act * SQRT_HALF))
                hidden_part = (pre_act * below).astype(BF16)
                hidden[slot, at] = hidden_part
                bend = below + pre_act * jnp.exp(-0.5 * pre_act * pre_act) * NORMAL_PEAK
                slope[slot, at] = bend.astype(BF16)
                state[at] += dot_nt(hidden_part, weight_down)
            save_block(layer, 10, block).start()
            save_block(layer, 11, block).start()
            return carry

        lax.fori_loop(0, blocks, one_block, 0)
        for block in (blocks - 2, blocks - 1):
            save_block(layer, 10, block).wait()
            save_block(layer, 11, block).wait()
        if layer < layers - 1:
            gathers[5].advance(2)
            gathers[6].advance(1)
            gathers[4].advance(3)
    last = layers - 1
    swap(2 + 2 * layers, sorted_rows.at[halves[1]], chip_cot.at[halves[1]], to_y).wait()
    save(last, 1, weights).wait()
    for index in range(2, 8):
        save(last, index, saved_refs(last)[index - 2]).wait()
    save(last, 8, lse).wait()
    save(last, 9, middle).wait()
    for one in gathers:
        one.drain()


def forward(clips, positions, patches, cotangent, table_columns, narrow, up_bias, weights, slots, collective_id):
    layers, owned = narrow[0].shape
    count = len(narrow)
    rows, features = 2 * slots, patches.shape[1]
    piece_rows = patches.shape[0]
    up_rows = weights[2].shape[1]
    deep = 2 * up_rows
    blocks = 4
    line = (8, slots + -slots % LANES)
    table_shape = (owned + 8, table_columns.shape[1])
    wide = (rows, features)

    def like(shape, dtype):
        return jax.ShapeDtypeStruct(shape, dtype)

    saved = [
        like(wide, F32), like((4, features, features), BF16), *[like(wide, BF16)] * 5, like(wide, F32),
        like((rows, LANES), F32), like(wide, F32), *[like((blocks,) + wide, BF16)] * 2,
    ]
    out_shape = [
        like(wide, F32), like(wide, BF16), like(line, F32), like(line, F32),
        like((layers * count, features), F32), like((blocks, 8, features), F32),
        like((rows, piece_rows + -piece_rows % LANES), BF16), like((2 * rows, LANES), BF16),
        *[like((2, 2, 4, 2, deep, features), BF16)] * layers,
        *(saved * layers),
    ]
    groups = 2 + 3 * layers
    half16 = pltpu.VMEM((rows // 2, features), BF16)
    wide16, wide32 = pltpu.VMEM(wide, BF16), pltpu.VMEM(wide, F32)
    each16 = pltpu.VMEM((layers,) + wide, BF16)
    scratch = [
        pltpu.VMEM((4, 2, 2, 2) + table_shape, BF16),
        pltpu.VMEM((layers, 4, 2, 2, 2, 4 * owned, features), BF16),
        pltpu.VMEM((features, table_shape[1]), BF16),
        pltpu.VMEM((4, features, features), BF16),
        pltpu.VMEM((2, 4, 2, deep, features), BF16),
        wide16, half16, wide32, wide16, wide16, wide16, wide16, each16, each16, wide32, wide16,
        pltpu.VMEM((rows, LANES), F32),
        pltpu.VMEM((2,) + wide, BF16),
        pltpu.VMEM((2,) + wide, BF16),
        pltpu.VMEM((2 * rows, LANES), BF16),
        pltpu.VMEM((2 * rows, LANES), BF16),
        pltpu.VMEM(line, F32),
        pltpu.VMEM(table_shape, BF16),
        pltpu.VMEM((layers, 4 * owned, features), BF16),
        pltpu.VMEM((layers, deep, features), BF16),
        pltpu.SemaphoreType.DMA((groups, 8)),
        pltpu.SemaphoreType.DMA((groups, 8)),
        dma_sems(groups),
        dma_sems(3 + 2 * layers),
        dma_sems(3 + 2 * layers),
        dma_sems(14),
        dma_sems(2),
    ]
    args = (clips, positions, patches, cotangent, table_columns, *narrow, up_bias, *weights)
    results = pl.pallas_call(
        functools.partial(forward_kernel, (layers, count, owned, up_rows)),
        out_shape=out_shape,
        in_specs=[vmem()] * len(args),
        out_specs=[vmem()] * 8 + [hbm()] * (len(out_shape) - 8),
        scratch_shapes=scratch,
        compiler_params=pltpu.CompilerParams(
            collective_id=collective_id, has_side_effects=True, vmem_limit_bytes=VMEM_LIMIT
        ),
        name="forward",
    )(*args)
    mlp_fulls = results[8 : 8 + layers]
    kept = results[8 + layers :]
    return results[:8], mlp_fulls, [kept[12 * i : 12 * i + 12] for i in range(layers)]


class Sum:
    def __init__(self, place, part, write, rows, in_low, in_high, second, last, send, recv):
        z, x, y, core = place
        self.place, self.part, self.write = place, part, write
        self.in_low, self.in_high, self.second_in, self.last_in = in_low, in_high, second, last
        split = rows // 32 * 16
        self.low, self.high, self.rows = pl.ds(0, split), pl.ds(split, rows - split), pl.ds(0, rows)
        self.low_at, self.high_at = pl.ds(0, split), pl.ds(0, rows - split)
        self.finished = False
        every = slice(None)

        def copy(slot, src, dst, device):
            return remote(src, dst, send.at[slot], recv.at[slot], device)

        to_x, to_y = device_at(z, 1 - x, y, core), device_at(z, x, 1 - y, core)
        self.first = [
            copy(0, part.at[1 - y, :, :, self.low], in_low.at[:, :, self.low_at], to_y),
            copy(1, part.at[:, :, 1 - x, self.high], in_high.at[:, :, self.high_at], to_x),
        ]
        self.second = [
            copy(2, part.at[y, :, 1 - x, self.low], second.at[0, :, self.low_at], to_x),
            copy(3, part.at[1 - y, :, x, self.high], second.at[1, :, self.high_at], to_y),
        ]
        self.third = []
        for k, to_z in enumerate(z_partners(place)):
            self.third.append(
                copy(4 + k, part.at[y, to_z, x, self.rows], last.at[k, self.rows], device_at(to_z, x, y, core))
            )

    def start(self):
        for copy in self.first:
            copy.start()

    def cross(self):
        z, x, y, core = self.place
        part, low, high = self.part, self.low, self.high
        for copy in self.first:
            copy.wait()

        def add_one(i, carry):
            a, b = i // 2, lax.rem(i, 2)
            part[y, a, b, low] = added(part[y, a, b, low], self.in_low[a, b, self.low_at])
            part[b, a, x, high] = added(part[b, a, x, high], self.in_high[b, a, self.high_at])
            return carry

        lax.fori_loop(0, 8, add_one, 0)
        for copy in self.second:
            copy.start()

    def along_z(self, before):
        z, x, y, core = self.place
        part, low, high = self.part, self.low, self.high
        for copy in self.second:
            copy.wait()

        def add_one(a, carry):
            part[y, a, x, low] = added(part[y, a, x, low], self.second_in[0, a, self.low_at])
            part[y, a, x, high] = added(part[y, a, x, high], self.second_in[1, a, self.high_at])
            return carry

        lax.fori_loop(0, 4, add_one, 0)
        if before is not None:
            before.finish()
        for copy in self.third:
            copy.start()

    def finish(self):
        if self.finished:
            return
        self.finished = True
        z, x, y, core = self.place
        for copy in self.third:
            copy.wait()
        total = self.part[y, z, x, self.rows].astype(F32)
        for k in range(3):
            total = total + self.last_in[k, self.rows].astype(F32)
        self.write(total)


def attend_pair_back(pair, wide, exact, lse, bias):
    rows = lse.shape[0]
    block = rows // 2
    at_lanes = pl.ds(pl.multiple_of(pair * LANES, LANES), LANES)
    lanes = lax.broadcasted_iota(jnp.int32, (1, LANES), 1)
    query = wide[0, :, at_lanes]
    grad = wide[5, :, at_lanes]
    product = grad.astype(F32) * exact[:, at_lanes]
    heads = []
    for head in range(2):
        lane, own, spare = lane_marks(head)
        own16 = own.astype(BF16)
        total = jnp.sum(jnp.where(lanes == 2 * pair + head, lse[...], 0.0), axis=-1, keepdims=True)
        inner = jnp.sum(product * own, axis=-1, keepdims=True)
        lse_parts, inner_parts = split_three(-total), split_three(-inner)
        query_own = query * own16
        grad_own = grad * own16
        query_aug = jnp.where(lane == spare, 1.0, 0.0)
        grad_aug = jnp.zeros((1, LANES), F32)
        for k in range(3):
            query_aug = jnp.where(lane == spare + 1 + k, lse_parts[k], query_aug)
            grad_aug = jnp.where(lane == spare + 1 + k, inner_parts[k], grad_aug)
        query_aug = query_own + query_aug.astype(BF16)
        grad_aug = grad_own + grad_aug.astype(BF16)
        at_spare = (lane == spare).astype(BF16)
        ones = ((lane > spare) & (lane < spare + 4)).astype(BF16)
        heads.append((own16, at_spare, ones, query_own, grad_own, query_aug, grad_aug))
    query_grad = jnp.zeros((LANES, rows), F32)
    for side in range(2):
        at_key, at_value = (1, 2) if side == 0 else (3, 4)
        for start in range(0, rows, block):
            at = slice(start, start + block)
            key, value = wide[at_key, at, at_lanes], wide[at_value, at, at_lanes]
            shift = bias[side * rows + start : side * rows + start + block]
            key_grad = jnp.zeros((block, LANES), F32)
            value_grad = jnp.zeros((block, LANES), F32)
            for own16, at_spare, ones, query_own, grad_own, query_aug, grad_aug in heads:
                key_own = key * own16
                weights = jnp.exp2(dot_nt(key_own + shift * at_spare + ones, query_aug))
                weight_grad = dot_nt(value * own16 + ones, grad_aug)
                score_grad = (weights * weight_grad).astype(BF16)
                value_grad = value_grad + dot_nn(weights.astype(BF16), grad_own)
                key_grad = key_grad + dot_nn(score_grad, query_own)
                query_grad = query_grad + dot_tn(key_own, score_grad)
            wide[at_key, at, at_lanes] = (key_grad * (1.0 / LOG2_E)).astype(BF16)
            wide[at_value, at, at_lanes] = value_grad.astype(BF16)
    wide[0, :, at_lanes] = (jnp.transpose(query_grad) * HEAD_DIM ** (-0.5)).astype(BF16)


def backward_kernel(sizes, *refs):
    layers, count, owned, up_rows, piece_rows = sizes
    (narrow, bias, pos_kept, pos_back, choose_from, chip_cot, final), refs = refs[:7], refs[7:]
    mlp_fulls, refs = refs[:layers], refs[layers:]
    kept, refs = refs[: 12 * layers], refs[12 * layers :]
    (activations, input_grad), refs = refs[:2], refs[2:]
    (up_out, down_out, qkv_out, out_out, table_out), refs = refs[:5], refs[5:]
    (
        grad, grad_back, wide, middle, before, total, lse, weights, mlp_block, act_t, grad_t, sent, arrived, arrived_attn,
        part_mlp, part_attn, in_low, in_high, second_in, last_large, last_small, lines, up_lines,
        sum_send, sum_recv, core_send, core_recv, far_send, far_recv, swap_send, swap_recv, load_sem, block_sem,
    ) = refs
    place = my_place()
    z, x, y, core = place
    rows, features = grad.shape
    slots = rows // 2
    halves = [slice(0, slots), slice(slots, rows)]
    to_y, to_core = device_at(z, x, 1 - y, core), device_at(z, x, y, 1 - core)
    blocks = 4
    top = layers - 1
    exact = total

    lane_half = features // 2
    half_rows = 2 * owned
    last_in = (last_large, last_small)

    def write_up(layer, value):
        up_out[layer] = value

    def write_down(layer, value):
        down_out[layer] = jnp.transpose(value)

    def write_attn(layer, part, value):
        for index in range(3):
            row, column = (index // 2) * owned, (index % 2) * lane_half
            start = index * features + part * lane_half
            qkv_out[layer, :, start : start + lane_half] = value[
                row : row + owned, column : column + lane_half
            ]
        start = part * lane_half
        out_out[layer, :, start : start + lane_half] = value[owned:, lane_half:]

    def write_table(value):
        table_out[...] = value

    groups = []

    def add_group(part, size, write):
        index = len(groups)
        groups.append(
            Sum(
                place, part, write, size, in_low.at[index % 2], in_high.at[index % 2],
                second_in.at[index % 2], last_in[index % 4 // 2].at[index % 2], sum_send.at[index], sum_recv.at[index],
            )
        )

    for layer in reversed(range(layers)):
        add_group(part_mlp.at[0], up_rows, functools.partial(write_up, layer))
        add_group(part_mlp.at[1], up_rows, functools.partial(write_down, layer))
        for part in range(2):
            at = pl.ds(part * half_rows, half_rows)
            add_group(part_attn.at[:, :, :, at], half_rows, functools.partial(write_attn, layer, part))
    add_group(part_mlp.at[0], half_rows, write_table)

    def along_z(index):
        groups[index].along_z(groups[index - 2] if index > 1 else None)

    def load(layer, index, ref, slot):
        return local_copy(kept[12 * layer + index], ref, load_sem.at[slot])

    def place_of(step):
        return lax.rem(step, 2), jnp.where(step < 2, 1 - core, core)

    def load_block(layer, step):
        row, column = place_of(step)
        slot = lax.rem(step, 2)
        block = row * 2 + column
        return [
            local_copy(mlp_fulls[layer].at[row, column], mlp_block.at[slot], block_sem.at[slot]),
            local_copy(kept[12 * layer + 10].at[block], wide.at[slot], block_sem.at[2 + slot]),
            local_copy(kept[12 * layer + 11].at[block], wide.at[2 + slot], block_sem.at[4 + slot]),
        ]

    def to_sibling_block(slot, src, dst):
        return remote(src, dst, core_send.at[slot], core_recv.at[slot], to_core)

    load_final = local_copy(final.at[pl.ds(0, slots)], middle.at[pl.ds(0, slots)], load_sem.at[0])
    choose = wide.at[6, :, pl.ds(0, choose_from.shape[1])]
    load_choose = local_copy(choose_from, choose, load_sem.at[1])
    final_back = activations.at[pl.ds(0, slots)]
    swap_final = remote(
        final.at[pl.ds(slots, slots)], final_back, swap_send.at[0], swap_recv.at[0], to_y
    )
    swap_grad = remote(wide.at[3, pl.ds(0, slots)], grad_back, swap_send.at[1], swap_recv.at[1], to_y)

    greet_signal(place)
    load_cot = local_copy(chip_cot, wide.at[5], load_sem.at[1])
    load_cot.start()
    load(top, 9, middle, 0).start()
    for copy in load_block(top, 0):
        copy.start()
    lines[...] = jnp.zeros_like(lines)
    up_lines[...] = jnp.zeros_like(up_lines)
    load_cot.wait()
    grad[...] = wide[5].astype(F32)

    for layer in reversed(range(layers)):
        base = count * layer
        first = 4 * (top - layer)
        load(layer, 0, before, 1).start()
        load(layer, 1, weights, 2).start()

        def line(index, base=base):
            return narrow[base + index : base + index + 1]

        def note(index, value, base=base):
            lines[base + index : base + index + 1] = value

        load(layer, 9, middle, 0).wait()
        normed, unused = norm_parts(middle[...])
        act_t[...] = jnp.transpose(normed * line(5) + line(6)).astype(BF16)
        wide[5] = grad[...].astype(BF16)
        grad_t[...] = jnp.transpose(grad[...]).astype(BF16)
        total[...] = jnp.zeros_like(total)
        if layer == top:
            greet_wait()
            swap_final.start()

        def one_block(step, carry, layer=layer, first=first):
            slot = lax.rem(step, 2)

            @pl.when(step + 1 < blocks)
            def _():
                for copy in load_block(layer, step + 1):
                    copy.start()

            for copy in load_block(layer, step):
                copy.wait()
            weight_up = mlp_block[slot, :, :, 0:up_rows, :].reshape(features, features)
            weight_down = mlp_block[slot, :, :, up_rows:, :].reshape(features, features)
            row, column = place_of(step)
            sums_up = jnp.zeros((1, features), F32)
            for at in halves:
                hidden_grad = dot_nn(wide[5, at], weight_down)
                pre_grad = (hidden_grad * wide[2 + slot, at].astype(F32)).astype(BF16)
                wide[4, at] = pre_grad
                sums_up = sums_up + jnp.sum(pre_grad.astype(F32), axis=0, keepdims=True)
                total[at] += dot_nt(pre_grad, weight_up)
            up_lines[row * 2 + column, layer : layer + 1] = sums_up

            def parts(store):
                deep = 2 * up_rows
                for a in range(4):
                    at = slice(a * deep, (a + 1) * deep)
                    store(0, a, dot_nn(act_t[at], wide[4]).reshape(2, up_rows, features))
                    store(1, a, dot_nn(grad_t[at], wide[slot]).reshape(2, up_rows, features))

            @pl.when(step < 2)
            def _():
                def store(i, a, value):
                    sent[i, a] = value.astype(BF16)

                @pl.when(step == 1)
                def _():
                    to_sibling_block(0, sent, arrived.at[0]).wait_send()

                parts(store)
                to_sibling_block(step, sent, arrived.at[step]).start()

            @pl.when(step >= 2)
            def _():
                @pl.when(step == 2)
                def _():
                    to_sibling_block(1, sent, arrived.at[1]).wait_send()

                to_sibling_block(step - 2, sent, arrived.at[step - 2]).wait_recv()

                def store(i, a, value):
                    other = arrived[step - 2, i, a].astype(F32)
                    part_mlp[i, step - 2, a] = (value + other).astype(BF16)

                parts(store)

            if layer < top:
                pl.when(step == 0)(groups[first - 1].cross)

                @pl.when(step == 1)
                def _():
                    along_z(first - 2)
                    groups[first - 3].finish()

                pl.when(step == 3)(lambda: along_z(first - 1))
            return carry

        lax.fori_loop(0, blocks, one_block, 0)
        for i in range(2):
            groups[first + i].start()
        gain_sum = jnp.zeros((1, features), F32)
        shift_sum = jnp.zeros((1, features), F32)
        down_sum = jnp.zeros((1, features), F32)
        out_sum = jnp.zeros((1, features), F32)
        for index in range(5):
            load(layer, 2 + index, wide.at[index], 3 + index).start()
        load(layer, 8, lse, 9).start()
        for at in halves:
            down_sum = down_sum + jnp.sum(wide[5, at].astype(F32), axis=0, keepdims=True)
            back, gain_part, shift_part = norm_back(middle[at], line(5), total[at])
            mid_grad = grad[at] + back
            grad[at] = mid_grad
            mid_grad = mid_grad.astype(BF16)
            wide[5, at] = mid_grad
            out_sum = out_sum + jnp.sum(mid_grad.astype(F32), axis=0, keepdims=True)
            gain_sum, shift_sum = gain_sum + gain_part, shift_sum + shift_part
        load(layer, 7, exact, 8).start()
        if layer > 0:
            load(layer - 1, 9, middle, 0).start()
        else:
            load_final.start()
        note(5, gain_sum)
        note(6, shift_sum)
        note(7, down_sum)
        note(4, out_sum)

        load(layer, 1, weights, 2).wait()
        for at in halves:
            wide[5, at] = dot_nt(wide[5, at], weights[3]).astype(BF16)
        for index in range(5):
            load(layer, 2 + index, wide.at[index], 3 + index).wait()
        load(layer, 7, exact, 8).wait()
        load(layer, 8, lse, 9).wait()

        def far_copies(pair):
            at_lanes = pl.ds(pl.multiple_of(pair * LANES, LANES), LANES)
            return [
                remote(
                    wide.at[3 + i, :, at_lanes], wide.at[6 + i, :, at_lanes],
                    far_send.at[i, pair], far_recv.at[i, pair], to_core,
                )
                for i in range(2)
            ]

        grad_t[...] = jnp.transpose(exact[...]).astype(BF16)
        load(layer, 0, before, 1).wait()
        normed, unused = norm_parts(before[...])
        act_t[...] = jnp.transpose(normed * line(0) + line(1)).astype(BF16)
        pairs = features // LANES

        def attn_copy(part):
            at = pl.ds(part * half_rows, half_rows)
            return to_sibling_block(2 + part, sent.at[:, :, :, at], arrived_attn.at[:, :, :, at])

        def attn_part(part, base=base):
            lanes = slice(part * lane_half, (part + 1) * lane_half)
            for pair in range(part * pairs // 2, (part + 1) * pairs // 2):
                for copy in far_copies(pair):
                    copy.wait()
            value_sum = jnp.zeros((1, lane_half), F32)
            for at in halves:
                wide[1, at, lanes] = added(wide[1, at, lanes], wide[6, at, lanes])
                value_grad = added(wide[2, at, lanes], wide[7, at, lanes])
                wide[2, at, lanes] = value_grad
                value_sum = value_sum + jnp.sum(value_grad.astype(F32), axis=0, keepdims=True)
            lines[base + 3 : base + 4, lanes] = value_sum
            for a in range(4):
                at = slice(a * 8 * owned, (a + 1) * 8 * owned)
                query_key = [dot_nn(act_t[at], wide[i, :, lanes]) for i in range(2)]
                value_out = [
                    dot_nn(act_t[at], wide[2, :, lanes]),
                    dot_nn(grad_t[at], grad[:, lanes].astype(BF16)),
                ]
                value = jnp.concatenate(
                    [
                        jnp.concatenate(both, axis=1).reshape(2, 2, 2, owned, features)
                        for both in (query_key, value_out)
                    ],
                    axis=3,
                ).astype(BF16)
                at = slice(part * half_rows, (part + 1) * half_rows)
                for i in range(2):
                    for j in range(2):
                        part_attn[j, a, i, at] = jnp.where(core == 0, value[i, j, 0], value[i, j, 1])
                        sent[j, a, i, at] = jnp.where(core == 0, value[i, j, 1], value[i, j, 0])
            attn_copy(part).start()

        def attn_core(part, first=first):
            at = pl.ds(part * half_rows, half_rows)
            attn_copy(part).wait()

            def add_core(i, carry):
                a, b, c = i // 8, lax.rem(i // 2, 4), lax.rem(i, 2)
                part_attn[a, b, c, at] = added(part_attn[a, b, c, at], arrived_attn[a, b, c, at])
                return carry

            lax.fori_loop(0, 16, add_core, 0)
            groups[first + 2 + part].start()

        def one_pair(pair, carry, first=first):
            attend_pair_back(pair, wide, exact, lse, bias)
            for copy in far_copies(pair):
                copy.start()
            pl.when(pair == 1)(groups[first].cross)
            pl.when(pair == 2)(groups[first + 1].cross)

            @pl.when(pair == 4)
            def _():
                along_z(first)
                attn_part(0)

            pl.when(pair == 5)(lambda: attn_core(0))
            return carry

        lax.fori_loop(0, pairs, one_pair, 0)
        note(2, jnp.sum(wide[0].astype(F32), axis=0, keepdims=True))
        along_z(first + 1)
        attn_part(1)
        for at in halves:
            act_grad = dot_nt(wide[0, at], weights[0])
            act_grad = act_grad + dot_nt(wide[1, at], weights[1])
            total[at] = act_grad + dot_nt(wide[2, at], weights[2])
        groups[first + 2].cross()
        attn_core(1)
        if layer > 0:
            for copy in load_block(layer - 1, 0):
                copy.start()
        gain_sum = jnp.zeros((1, features), F32)
        shift_sum = jnp.zeros((1, features), F32)
        for at in halves:
            back, gain_part, shift_part = norm_back(before[at], line(0), total[at])
            grad[at] = grad[at] + back
            gain_sum, shift_sum = gain_sum + gain_part, shift_sum + shift_part
        note(0, gain_sum)
        note(1, shift_sum)

    load_choose.start()
    wide[3, 0:slots] = grad[halves[1]].astype(BF16)
    swap_grad.start()
    last = 4 * layers
    groups[last - 1].cross()
    along_z(last - 2)
    grad_t[...] = jnp.transpose(grad[...]).astype(BF16)
    side = features - LANES
    for i in range(2):
        position = lax.broadcasted_iota(jnp.int32, (slots, side), 1).astype(F32) + float(i * side)
        for at, pos in ((halves[0], pos_kept), (halves[1], pos_back)):
            column = jnp.transpose(jnp.broadcast_to(pos[0:1, 0:slots], (LANES, slots)))[:, 0:1]
            weights[i, at, 0:side] = (position == column).astype(F32).astype(BF16)
    lane = lax.broadcasted_iota(jnp.int32, (8, 1, features), 2)
    device = lax.broadcasted_iota(jnp.int32, (8, 1, features), 0)
    for a in range(4):
        at = slice(a * 8 * owned, (a + 1) * 8 * owned)
        left, right = (
            dot_nn(grad_t[at], weights[i, 0:rows, 0:side]).reshape(8, owned, side) for i in range(2)
        )
        own = jnp.where(lane // owned == device + 8 * a, lines[...][None], 0.0)
        narrow_rows = dot_nt(
            own.reshape(8 * layers * count, features).astype(BF16), spread_matrix(owned, features)
        ).reshape(8, layers * count, LANES)
        own = jnp.where(lane // (4 * owned) == device, up_lines[a][None], 0.0)
        up_rows_here = dot_nt(
            own.reshape(64, features).astype(BF16), spread_matrix(4 * owned, features)
        ).reshape(8, 8, LANES)
        spare = jnp.zeros((8, 2 * owned - layers * count - 8, LANES), F32)
        value = jnp.concatenate(
            [
                jnp.concatenate([left, right], axis=1),
                jnp.concatenate([narrow_rows, up_rows_here, spare], axis=1),
            ],
            axis=2,
        )
        value = value.astype(BF16).reshape(2, 2, 2, 2 * owned, features)
        for i in range(2):
            for j in range(2):
                mine = jnp.where(core == 0, value[i, j, 0], value[i, j, 1])
                others = jnp.where(core == 0, value[i, j, 1], value[i, j, 0])
                part_mlp[0, j, a, i, 0 : 2 * owned] = mine
                sent[j, a, i, 0 : 2 * owned] = others
    short = pl.ds(0, 2 * owned)
    send_table = to_sibling_block(4, sent.at[:, :, :, short], arrived.at[0, :, :, :, short])
    send_table.start()
    along_z(last - 1)
    send_table.wait()

    def add_table(i, carry):
        a, b, c = i // 8, lax.rem(i // 2, 4), lax.rem(i, 2)
        part_mlp[0, a, b, c, short] = added(part_mlp[0, a, b, c, short], arrived[0, a, b, c, short])
        return carry

    lax.fori_loop(0, 16, add_table, 0)
    groups[last].start()
    load_final.wait()
    load_choose.wait()
    swap_final.wait()
    return_rows(choose, activations, middle, final_back)
    groups[last].cross()
    swap_grad.wait()
    return_rows(choose, input_grad, grad, grad_back)
    along_z(last)
    groups[last - 1].finish()
    groups[last].finish()


def return_rows(choose, out, kept, received):
    slots = received.shape[0]
    total = jnp.zeros(out.shape, F32)
    for at, values in ((slice(0, slots), kept[0:slots]), (slice(slots, 2 * slots), received[...])):
        rest = values.astype(F32)
        for unused in range(3 if received.dtype == F32 or at.start == 0 else 1):
            part = rest.astype(BF16)
            total = total + dot_tn(choose[at, 0 : out.shape[0]], part)
            rest = rest - part.astype(F32)
    out[...] = total


def backward(
    chip_cot, narrow, bias, pos_kept, pos_back, choose, final, mlp_fulls, kept, count, owned, piece_rows,
    collective_id,
):
    layers = len(mlp_fulls)
    rows, features = final.shape
    deep = mlp_fulls[0].shape[4]
    up_rows = deep // 2
    wide = (rows, features)

    def like(shape, dtype):
        return jax.ShapeDtypeStruct(shape, dtype)

    out_shape = [like((piece_rows, features), F32)] * 2
    out_shape += [
        like((layers, up_rows, features), F32),
        like((layers, features, up_rows), F32),
        like((layers, owned, 3 * features), F32),
        like((layers, owned, features), F32),
        like((2 * owned, features), F32),
    ]
    most = max(up_rows, 4 * owned)
    half = most // 2
    places = (2, 4, 2, most, features)
    wide32 = pltpu.VMEM(wide, F32)
    turned = pltpu.VMEM((features, rows), BF16)
    groups = 4 * layers + 1
    scratch = [
        wide32,
        pltpu.VMEM((rows // 2, features), BF16),
        pltpu.VMEM((8,) + wide, BF16),
        wide32, wide32, wide32,
        pltpu.VMEM((rows, LANES), F32),
        pltpu.VMEM((4, features, features), BF16),
        pltpu.VMEM((2, 4, 2, deep, features), BF16),
        turned, turned,
        pltpu.VMEM(places, BF16),
        pltpu.VMEM((2,) + places, BF16),
        pltpu.VMEM(places, BF16),
        pltpu.VMEM((2,) + places, BF16),
        pltpu.VMEM(places, BF16),
        pltpu.VMEM((2, 4, 2, half, features), BF16),
        pltpu.VMEM((2, 2, 4, half, features), BF16),
        pltpu.VMEM((2, 2, 4, half, features), BF16),
        pltpu.VMEM((2, 3, most, features), BF16),
        pltpu.VMEM((2, 3, 2 * owned, features), BF16),
        pltpu.VMEM((layers * count, features), F32),
        pltpu.VMEM((4, 8, features), F32),
        pltpu.SemaphoreType.DMA((groups, 7)),
        pltpu.SemaphoreType.DMA((groups, 7)),
        dma_sems(5),
        dma_sems(5),
        pltpu.SemaphoreType.DMA((2, features // LANES)),
        pltpu.SemaphoreType.DMA((2, features // LANES)),
        dma_sems(2),
        dma_sems(2),
        dma_sems(10),
        dma_sems(6),
    ]
    flat = [ref for layer in kept for ref in layer]
    args = (narrow, bias, pos_kept, pos_back, choose, chip_cot, final, *mlp_fulls, *flat)
    results = pl.pallas_call(
        functools.partial(backward_kernel, (layers, count, owned, up_rows, piece_rows)),
        out_shape=out_shape,
        in_specs=[vmem()] * 4 + [hbm()] * (len(args) - 4),
        out_specs=[vmem()] * len(out_shape),
        scratch_shapes=scratch,
        compiler_params=pltpu.CompilerParams(
            collective_id=collective_id, has_side_effects=True, vmem_limit_bytes=VMEM_LIMIT
        ),
        name="backward",
    )(*args)
    return results


def chip_shards(
    patches,
    clip_of_row,
    position_of_row,
    pos_embed,
    norm1_gain,
    norm1_bias,
    query_bias,
    value_bias,
    out_bias,
    norm2_gain,
    norm2_bias,
    up_bias,
    down_bias,
    qkv_weight,
    out_weight,
    up_weight,
    down_weight,
    cotangent,
):
    layers, owned, features = qkv_weight.shape
    features //= 3
    pieces = lax.axis_size("gy")
    piece_rows = patches.shape[0]
    positions = pos_embed.shape[0]
    padded_positions = -(-positions // 256) * 256
    slots = -(-positions // pieces)
    slots = -(-slots // 16) * 16
    narrow = (
        norm1_gain, norm1_bias, query_bias, value_bias, out_bias, norm2_gain, norm2_bias, down_bias
    )
    count = len(narrow)
    table_columns = jnp.pad(pos_embed.T, ((0, 0), (0, padded_positions - positions)))
    (state, chip_cotangent, pos_kept, pos_back, narrow_all, unused_up, choose, bias), mlp_fulls, stored = forward(
        clip_of_row.reshape(pieces, piece_rows), position_of_row.reshape(1, piece_rows), patches, cotangent,
        table_columns, narrow, up_bias, (qkv_weight, out_weight, up_weight, down_weight), slots, 0,
    )
    (
        activations, input_grad, up_weight_grad, down_weight_grad, qkv_weight_grad, out_weight_grad, table_sum
    ) = backward(
        chip_cotangent, narrow_all, bias, pos_kept, pos_back, choose, state, mlp_fulls, stored, count, owned,
        piece_rows, 1,
    )
    table_half = padded_positions // 2
    table_rows = jnp.concatenate(
        [table_sum[:owned, :table_half], table_sum[owned:, :table_half]], axis=1
    )
    pos_embed_grad = table_rows[:, :positions].T
    narrow_sum = table_sum[: layers * count, table_half : table_half + owned].reshape(layers, count, owned)
    up_bias_grad = table_sum[layers * count : layers * (count + 1), table_half : table_half + 4 * owned]
    return (
        activations,
        input_grad,
        pos_embed_grad,
        *(narrow_sum[:, i] for i in range(7)),
        up_bias_grad,
        narrow_sum[:, 7],
        qkv_weight_grad,
        out_weight_grad,
        up_weight_grad,
        down_weight_grad,
    )


def solution(mesh):
    return jax.shard_map(
        chip_shards if mesh.shape["gx"] == 8 and mesh.shape["gy"] == 4 else shards,
        mesh=mesh,
        in_specs=(
            P(("gx", "gy"), None),
            P("gx"),
            P(("gx", "gy")),
            P(None, ("gx", "gy")),
            P(None, ("gx", "gy")),
            P(None, ("gx", "gy")),
            P(None, ("gx", "gy")),
            P(None, ("gx", "gy")),
            P(None, ("gx", "gy")),
            P(None, ("gx", "gy")),
            P(None, ("gx", "gy")),
            P(None, ("gx", "gy")),
            P(None, ("gx", "gy")),
            P(None, ("gx", "gy"), None),
            P(None, ("gx", "gy"), None),
            P(None, "gx", "gy"),
            P(None, "gy", "gx"),
            P(("gx", "gy"), None),
        ),
        out_specs=(
            P(("gx", "gy"), None),
            P(("gx", "gy"), None),
            P(None, ("gx", "gy")),
            P(None, ("gx", "gy")),
            P(None, ("gx", "gy")),
            P(None, ("gx", "gy")),
            P(None, ("gx", "gy")),
            P(None, ("gx", "gy")),
            P(None, ("gx", "gy")),
            P(None, ("gx", "gy")),
            P(None, ("gx", "gy")),
            P(None, ("gx", "gy")),
            P(None, ("gx", "gy"), None),
            P(None, ("gx", "gy"), None),
            P(None, "gx", "gy"),
            P(None, "gy", "gx"),
        ),
        check_vma=False,
    )
```
